32 devices in a mesh: gx: 8 (over y, x, core), gy: 4 (over z).
Axes of the slice: x: 2, y: 2, z: 4, core: 2. Of those that a mesh axis runs over, the one named last changes fastest.
Arguments:
- tiles: bfloat16 [3, 8, 384, 4352], P(None, None, 'gy', 'gx'), may hold values from 0.099609375 to 4
- offsets: int32 [4, 8, 2], P('gy', 'gx'), may hold values from 0 to 32, as said below
- psf: float32 [3, 3, 31], replicated, may hold values from 0.05 to 1
Outputs:
- restored: float32 [3, 8, 256, 4096], P(None, None, 'gy', 'gx')
- level_one: float32 [3, 4, 128, 2048], P(None, None, 'gy', 'gx')
- level_two: float32 [3, 2, 64, 1024], P(None, None, 'gy', 'gx')
The draws below stay inside these ranges and needn't reach their ends.
Inputs may be any that keep to these rules, and one draw needn't show every extreme that they name: offsets[j, i, 0] is 0 for j = 0 and 32 for j = 3; offsets[j, i, 1] is 0 for i = 0 and 32 for i = 7.
All inputs are finite; a program needn't handle non-finite values.
Results may differ from the reference program's by a relative error of at most 0.0015.
Values may be sent and summed in bfloat16 or wider, within the bound.
No kernel may reach another device: no remote copies, remote signals or barrier semaphores. Data moves between devices by JAX's collectives and lax.ppermute only.
A program may use at most 128 MiB of HBM per device.

```python
import math
import jax
import jax.numpy as jnp
from jax import lax

CHANNELS = 3
SLAB = 8
CY = 64
CX = 512
MARGIN = 32
TAPS = 31
ITERS = 2
HALF = 15
TY = 96
TX = 544
GRID_Y = 4
GRID_X = 8
NY = 256
NX = 4096


def draw_offsets(key, part):
    shape = (GRID_Y, GRID_X, 2)
    shifts = jax.random.randint(key, shape, 0, MARGIN + 1)
    rows = lax.broadcasted_iota(jnp.int32, shape, 0)
    cols = lax.broadcasted_iota(jnp.int32, shape, 1)
    which = lax.broadcasted_iota(jnp.int32, shape, 2)
    shifts = jnp.where((which == 0) & (rows == GRID_Y - 1), MARGIN, shifts)
    shifts = jnp.where((which == 1) & (cols == GRID_X - 1), MARGIN, shifts)
    shifts = jnp.where((which == 0) & (rows == 0), 0, shifts)
    shifts = jnp.where((which == 1) & (cols == 0), 0, shifts)
    return shifts.astype(jnp.int32)


def levels(stream_key, dims, pieces, least, top_value):
    gain, own = 1.0, jax.random.fold_in(stream_key, 6)
    for position, blocks in pieces:
        steps = jnp.exp(jax.random.uniform(jax.random.fold_in(own, position), (blocks,), jnp.float32, least / len(pieces), top_value / len(pieces)))
        gain = gain * jnp.repeat(steps, dims[position] // blocks).reshape([-1 if axis == position else 1 for axis in range(len(dims))])
    return gain


def setup_inputs(seed: int = 0) -> dict:
    key_of = jax.random.split(jax.random.key(seed), 4)
    return {
        "tiles": jnp.clip(jnp.exp(math.log(4.0) - 3.6927934 * jax.random.uniform(key_of[0], (CHANNELS, SLAB, GRID_Y * TY, GRID_X * TX), jnp.float32) ** levels(key_of[0], (CHANNELS, SLAB, GRID_Y * TY, GRID_X * TX), ((2, 4), (3, 8)), -0.2, 0.2)), 0.099609375, 4.0).astype(jnp.bfloat16),
        "offsets": draw_offsets(jax.random.fold_in(key_of[3], 71), 0),
        "psf": jnp.clip(jnp.exp(jax.random.uniform(key_of[2], (CHANNELS, 3, TAPS), jnp.float32, math.log(0.05), math.log(1.0))), 0.05, 1.0),
    }


HIGH = lax.Precision.HIGHEST
GAUSS = (0.0625, 0.25, 0.375, 0.25, 0.0625)


def correlate(field, taps, axis, stride, pad_lo, pad_hi):
    moved = jnp.moveaxis(field, axis, -1)
    lead = moved.shape[:-1]
    flat = moved.reshape((-1, 1, moved.shape[-1]))
    result = lax.conv_general_dilated(flat, taps.reshape((1, 1, -1)), (stride,), [(pad_lo, pad_hi)], dimension_numbers=("NCH", "OIH", "NCH"), precision=HIGH)
    return jnp.moveaxis(result.reshape(lead + (result.shape[-1],)), -1, axis)


def blur(field, taps):
    field = correlate(field, taps[0], 0, 1, HALF, HALF)
    field = correlate(field, taps[1], 1, 1, HALF, HALF)
    return correlate(field, taps[2], 2, 1, HALF, HALF)


def shrink(field):
    gauss = jnp.array(GAUSS, jnp.float32)
    for axis in range(3):
        field = correlate(field, gauss, axis, 2, 2, 2)
    return field


def reference(tiles, offsets, psf):
    canvas = jnp.zeros((CHANNELS, SLAB, NY + 2 * MARGIN, NX + 2 * MARGIN), jnp.float32)
    cover = jnp.zeros((NY + 2 * MARGIN, NX + 2 * MARGIN), jnp.float32)

    def place(index, carry):
        canvas, cover = carry
        index = jnp.asarray(index).astype(jnp.int32)
        row = index // GRID_X
        col = index % GRID_X
        top = (row * CY + offsets[row, col, 0]).astype(jnp.int32)
        left = (col * CX + offsets[row, col, 1]).astype(jnp.int32)
        zero = jnp.zeros((), jnp.int32)
        block = lax.dynamic_slice(tiles, (zero, zero, (row * TY).astype(jnp.int32), (col * TX).astype(jnp.int32)), (CHANNELS, SLAB, TY, TX)).astype(jnp.float32)
        before = lax.dynamic_slice(canvas, (zero, zero, top, left), (CHANNELS, SLAB, TY, TX))
        canvas = lax.dynamic_update_slice(canvas, before + block, (zero, zero, top, left))
        seen = lax.dynamic_slice(cover, (top, left), (TY, TX))
        cover = lax.dynamic_update_slice(cover, seen + 1.0, (top, left))
        return canvas, cover

    canvas, cover = lax.fori_loop(0, GRID_Y * GRID_X, place, (canvas, cover))
    joined = canvas[:, :, :NY, :NX] / cover[:NY, :NX]
    kern = psf / jnp.sum(psf, axis=-1, keepdims=True)

    def channel(pair):
        field, taps = pair
        estimate = field
        for step in range(ITERS):
            ratio = field / blur(estimate, taps)
            estimate = estimate * blur(ratio, taps[:, ::-1])
        fine = shrink(estimate)
        coarse = shrink(fine)
        return estimate, fine, coarse

    restored, level_one, level_two = lax.map(channel, (joined, kern))
    return restored, level_one, level_two
```

```python
import functools

import jax
import jax.numpy as jnp
import ml_dtypes
import numpy as np
from jax import lax
from jax.experimental import pallas as pl
from jax.experimental.pallas import tpu as pltpu
from jax.sharding import PartitionSpec as P

MARGIN = 32
REACH = 15
TAPS = 31
DEPTH = 8
LANE = 128
GAUSS = (1, 4, 6, 4, 1)
TINY = 1e-30
BF16 = jnp.bfloat16
F32 = jnp.float32
MIB = 1 << 20

BEFORE = 66
FRAME = 200
BIG = 34
SMALL = 26


def params(mib):
    return pltpu.CompilerParams(vmem_limit_bytes=mib * MIB)


def cost(flops, nbytes):
    return pl.CostEstimate(flops=int(flops), bytes_accessed=int(nbytes), transcendentals=0)


def dot(a, b):
    return jnp.dot(a, b, preferred_element_type=F32)


def split(value):
    high = value.astype(BF16)
    return high, (value - high.astype(F32)).astype(BF16)


def place_kernel(off_ref, tile_ref, own_ref, right_ref, low_ref, corner_ref, canvas):
    depth, tile_y, tile_x = tile_ref.shape[1:]
    parts = canvas.shape[0]
    wide = parts * LANE
    rows = own_ref.shape[1]
    cols = own_ref.shape[2]
    top = off_ref[0]
    left = off_ref[1]
    canvas[...] = jnp.zeros_like(canvas)
    shift = (
        lax.broadcasted_iota(jnp.int32, (tile_x, wide), 1)
        == lax.broadcasted_iota(jnp.int32, (tile_x, wide), 0) + left
    )
    shift = jnp.where(shift, 1.0, 0.0).astype(BF16)
    for z in range(depth):
        moved = dot(tile_ref[0, z], shift)
        for b in range(parts):
            to = pl.ds(top * depth + z, tile_y, stride=depth)
            canvas[b, to, :] = moved[:, b * LANE : (b + 1) * LANE]
    for b in range(parts - 1):
        to = slice(b * LANE, (b + 1) * LANE)
        own_ref[0, :, to] = canvas[b, :rows, :].astype(BF16)
        low_ref[0, :, to] = canvas[b, rows:, :].astype(BF16)
    right_ref[0] = canvas[parts - 1, :rows, :].astype(BF16)
    half = rows // 2
    upper = canvas[parts - 1, rows : rows + half, :]
    lower = canvas[parts - 1, rows + half :, :]
    corner_ref[0] = (upper + pltpu.roll(lower, LANE // 2, 1)).astype(BF16)


def place(tiles, offsets):
    n, depth, tile_y, tile_x = tiles.shape
    rows = (tile_y - MARGIN) * depth
    cols = tile_x - MARGIN
    block = lambda r, c: pl.BlockSpec((1, r, c), lambda i, off: (i, 0, 0))
    shape = lambda r, c: jax.ShapeDtypeStruct((n, r, c), BF16)
    sizes = ((rows, cols), (rows, LANE), (rows, cols), (rows // 2, LANE))
    return pl.pallas_call(
        place_kernel,
        grid_spec=pltpu.PrefetchScalarGridSpec(
            num_scalar_prefetch=1,
            grid=(n,),
            in_specs=[pl.BlockSpec((1, depth, tile_y, tile_x), lambda i, off: (i, 0, 0, 0))],
            out_specs=[block(*s) for s in sizes],
            scratch_shapes=[pltpu.VMEM((cols // LANE + 1, 2 * rows, LANE), F32)],
        ),
        out_shape=[shape(*s) for s in sizes],
        compiler_params=params(32),
        cost_estimate=cost(n * 2e9, n * 2.5e6),
        name="place",
    )(offsets, tiles)


def join_kernel(own_ref, low_ref, right_ref, corner_ref, exact_ref, short_ref):
    rows = own_ref.shape[1]
    half = rows // 2

    def seen(x):
        return jnp.where(x != 0, 1.0, 0.0)

    own = own_ref[0].astype(F32)
    low = low_ref[0].astype(F32)
    total = own + low
    count = seen(own) + seen(low)
    right = right_ref[0].astype(F32)
    corner = corner_ref[0].astype(F32)
    lane = lax.broadcasted_iota(jnp.int32, (half, LANE), 1)
    inside = lane < LANE // 2
    upper = jnp.where(inside, corner, 0.0)
    lower = jnp.where(inside, pltpu.roll(corner, LANE // 2, 1), 0.0)
    corner = jnp.concatenate([upper, lower], axis=0)
    edge_total = total[:, :LANE] + right + corner
    edge_count = count[:, :LANE] + seen(right) + seen(corner)
    edge = edge_total / edge_count
    rest = total[:, LANE:] / count[:, LANE:]
    exact_ref[0, :, :LANE] = edge
    exact_ref[0, :, LANE:] = rest
    short_ref[0, :, :LANE] = edge.astype(BF16)
    short_ref[0, :, LANE:] = rest.astype(BF16)


def join(own, low, right, corner):
    n, rows, cols = own.shape
    block = lambda a: pl.BlockSpec((1,) + a.shape[1:], lambda i: (i, 0, 0))
    return pl.pallas_call(
        join_kernel,
        grid=(n,),
        in_specs=[block(a) for a in (own, low, right, corner)],
        out_specs=[block(own), block(own)],
        out_shape=[jax.ShapeDtypeStruct(own.shape, F32), jax.ShapeDtypeStruct(own.shape, BF16)],
        compiler_params=params(32),
        cost_estimate=cost(n * 5e6, n * 3e6),
        name="join",
    )(own, low, right, corner)


def bands_kernel(kern_ref, across_ref, within_ref):
    which = pl.program_id(0)
    wide = 3 * 2 * LANE
    shape = (16, wide)
    row = lax.broadcasted_iota(jnp.int32, shape, 0)
    lane = lax.broadcasted_iota(jnp.int32, shape, 1)
    tap = row - (lane - 4 * LANE) - (LANE - REACH)
    base = jnp.zeros(shape, F32)
    for k in range(TAPS):
        base = jnp.where(tap == k, kern_ref[which, 2 * TAPS + k], base)

    @pl.loop(0, across_ref.shape[1] // 16)
    def _(q):
        turned = pltpu.roll(base, wide - 4 * LANE + 16 * q, 1)
        across_ref[0, pl.ds(pl.multiple_of(16 * q, 16), 16), :] = turned[:, : 2 * LANE].astype(BF16)

    shape = (16, within_ref.shape[2])
    row = lax.broadcasted_iota(jnp.int32, shape, 0)
    lane = lax.broadcasted_iota(jnp.int32, shape, 1)
    tap_y = lane // DEPTH - row // DEPTH
    tap_z = lane % DEPTH - row % DEPTH + REACH
    in_y = jnp.zeros(shape, F32)
    in_z = jnp.zeros(shape, F32)
    for k in range(TAPS):
        in_y = jnp.where(tap_y == k, kern_ref[which, TAPS + k], in_y)
    for k in range(REACH + 1 - DEPTH, REACH + DEPTH):
        in_z = jnp.where(tap_z == k, kern_ref[which, k], in_z)
    both = in_y * in_z

    @pl.loop(0, within_ref.shape[1] // 16)
    def _(q):
        turned = pltpu.roll(both, 16 * q, 1)
        within_ref[0, pl.ds(pl.multiple_of(16 * q, 16), 16), :] = turned.astype(BF16)


def bands(kern):
    count = kern.shape[0]
    shapes = ((4 * LANE, 2 * LANE), (BIG * DEPTH, (BIG + 2 * REACH) * DEPTH))
    return pl.pallas_call(
        bands_kernel,
        grid=(count,),
        in_specs=[pl.BlockSpec(memory_space=pltpu.SMEM)],
        out_specs=[pl.BlockSpec((1,) + s, lambda i: (i, 0, 0)) for s in shapes],
        out_shape=[jax.ShapeDtypeStruct((count,) + s, BF16) for s in shapes],
        compiler_params=params(32),
        cost_estimate=cost(count * 1e6, count * 4e6),
        name="bands",
    )(kern)


@functools.lru_cache(None)
def pyramid_matrices(rows, cols, depth):
    half_x, half_y, half_z = cols // 2, rows // 2, depth // 2
    taps = np.array(GAUSS, np.float32) / 16
    extra_x = (-2, -1, half_x)
    one_x = np.zeros((cols + 2 * LANE, half_x + LANE), np.float32)
    for lane in range(half_x + len(extra_x)):
        x = lane if lane < half_x else extra_x[lane - half_x]
        for k in range(5):
            one_x[LANE + 2 * x + k - 2, lane] = taps[k]
    extra_y = (-2, -1, half_y)
    order = [(z, y) for z in range(half_z) for y in range(half_y)]
    order += [(z, y) for y in extra_y for z in range(half_z)]
    height = -(-len(order) // 16) * 16
    reach_in = (rows + 10) * depth
    one_zy = np.zeros((height, reach_in), np.float32)
    for i, (z, y) in enumerate(order):
        for a in range(5):
            for b in range(5):
                zi = 2 * z + b - 2
                if 0 <= zi < depth:
                    one_zy[i, (2 * y + a - 2 + 6) * depth + zi] = taps[a] * taps[b]
    two_x = np.zeros((half_x + LANE, half_x // 2), np.float32)
    for x in range(half_x // 2):
        for k in range(5):
            source = 2 * x + k - 2
            lane = source if 0 <= source < half_x else half_x + extra_x.index(source)
            two_x[lane, x] = taps[k]
    place_of = {zy: i for i, zy in enumerate(order)}
    two_zy = np.zeros((half_z * half_y // 4, height), np.float32)
    for z in range(half_z // 2):
        for y in range(half_y // 2):
            for a in range(5):
                for b in range(5):
                    at = (2 * z + b - 2, 2 * y + a - 2)
                    if 0 <= at[0] < half_z:
                        two_zy[z * (half_y // 2) + y, place_of[at]] = taps[a] * taps[b]
    return tuple(m.astype(ml_dtypes.bfloat16) for m in (one_x, one_zy, two_x, two_zy))


def deconvolve_kernel(
    sides_ref,
    exact_ref,
    above_ref,
    below_ref,
    far_ref,
    left_ref,
    right_ref,
    across_ref,
    within_ref,
    one_x_ref,
    one_zy_ref,
    two_x_ref,
    two_zy_ref,
    restored_ref,
    level_one_ref,
    level_two_ref,
    joined,
    joined_short,
    ratio,
    estimate,
    estimate_short,
    result,
    high,
    low,
):
    rows8, cols = exact_ref.shape[1:]
    wide = cols + 2 * LANE
    far8 = far_ref.shape[1]
    own = slice(far8 + rows8, far8 + 2 * rows8)
    frame8 = far8 + 3 * rows8
    middle = slice(LANE, LANE + cols)

    joined_short[:far8, middle] = far_ref[0]
    joined_short[far8 : far8 + rows8, middle] = above_ref[0]
    joined_short[own, middle] = exact_ref[0].astype(BF16)
    joined_short[far8 + 2 * rows8 : frame8, middle] = below_ref[0]
    joined_short[:frame8, :LANE] = left_ref[0]
    joined_short[:frame8, LANE + cols :] = right_ref[0]
    joined_short[frame8:, :] = jnp.zeros_like(joined_short[frame8:, :])
    joined[...] = joined_short[...].astype(F32)
    joined[own, middle] = exact_ref[0]

    def run_x(source, which, chunks, size, exact):
        @pl.loop(0, chunks)
        def _(i):
            at = pl.ds(pl.multiple_of(i * size, 16), size)
            for n in range(wide // (2 * LANE)):
                begin = 2 * LANE * n - LANE
                lo, hi = max(begin, 0), min(begin + 4 * LANE, wide)
                out = dot(source[at, lo:hi], across_ref[0, which, lo - begin : hi - begin, :])
                to = slice(2 * LANE * n, 2 * LANE * (n + 1))
                if exact:
                    high[at, to], low[at, to] = split(out)
                else:
                    high[at, to] = out.astype(BF16)

    def run_zy(which, chunks, size, exact, finish):
        deep = (size + 2 * REACH) * DEPTH
        matrix = within_ref[0, which, : size * DEPTH, :deep]

        @pl.loop(0, chunks)
        def _(i):
            start = i * (size * DEPTH)
            at = pl.ds(pl.multiple_of(start, 16), deep)
            for n in range(wide // (2 * LANE)):
                to = slice(2 * LANE * n, 2 * LANE * (n + 1))
                out = dot(matrix, high[at, to])
                if exact:
                    out = out + dot(matrix, low[at, to])
                finish(start, size * DEPTH, to, out)

    def rows_at(start, shift, size):
        return pl.ds(pl.multiple_of(start + shift * DEPTH, 8), size)

    def ratio_from(shift):
        def finish(start, size, to, out):
            top = joined[rows_at(start, shift, size), to]
            at = pl.ds(pl.multiple_of(start, 16), size)
            ratio[at, to] = (top / jnp.maximum(out, TINY)).astype(BF16)

        return finish

    def first_estimate(start, size, to, out):
        at = pl.ds(pl.multiple_of(start, 16), size)
        value = joined[rows_at(start, 2 * REACH, size), to] * out
        estimate[at, to] = value
        estimate_short[at, to] = value.astype(BF16)

    def last_estimate(start, size, to, out):
        at = pl.ds(pl.multiple_of(start, 16), size)
        value = estimate[rows_at(start, 2 * REACH, size), to] * out
        for b in range(2):
            result[to.start // LANE + b, at, :] = value[:, b * LANE : (b + 1) * LANE]

    run_x(joined_short, 0, 5, 40 * DEPTH, False)
    run_zy(0, 5, BIG, False, ratio_from(REACH))
    run_x(ratio, 1, 5, BIG * DEPTH, True)
    run_zy(1, 4, BIG, True, first_estimate)
    run_x(estimate_short, 0, 4, BIG * DEPTH, False)
    run_zy(0, 4, SMALL, False, ratio_from(3 * REACH))
    ratio[4 * SMALL * DEPTH : (4 * SMALL + 4) * DEPTH, :] = jnp.zeros((4 * DEPTH, wide), BF16)
    run_x(ratio, 1, 3, 36 * DEPTH, True)
    run_zy(1, 3, SMALL, True, last_estimate)

    planes = restored_ref.shape[1]
    height = restored_ref.shape[2]
    for z in range(planes):
        at = pl.ds(6 * planes + z, height, stride=planes)
        for b in range(cols // LANE):
            restored_ref[0, z, :, b * LANE : (b + 1) * LANE] = result[1 + b, at, :]

    def twice(left, right):
        big, small = split(right)
        return dot(left, big) + dot(left, small)

    def twice_left(left, right):
        big, small = split(left)
        return dot(big, right) + dot(small, right)

    reach_in = one_zy_ref.shape[1]
    fine = jnp.concatenate([result[b, :reach_in, :] for b in range(wide // LANE)], axis=1)
    one = twice(one_zy_ref[...], twice_left(fine, one_x_ref[...]))
    half_z, half_y, half_x = level_one_ref.shape[1:]
    inner = half_z * half_y
    level_one_ref[0] = one[:inner, :half_x].reshape(half_z, half_y, half_x)
    row = lax.broadcasted_iota(jnp.int32, one.shape, 0) - inner
    lane = lax.broadcasted_iota(jnp.int32, one.shape, 1) - half_x
    up, down, left, right = (sides_ref[k] for k in range(4))
    keep_row = jnp.where(row < 0, 1, jnp.where(row < 2 * half_z, up, down))
    keep_lane = jnp.where(lane < 0, 1, jnp.where(lane < 2, left, right))
    one = jnp.where(keep_row * keep_lane > 0, one, 0.0)
    two = twice(two_zy_ref[...], twice_left(one, two_x_ref[...]))
    level_two_ref[0] = two.reshape(level_two_ref.shape[1:])


def deconvolve(sides, exact, above, below, far, left, right, across, within, matrices):
    n, rows8, cols = exact.shape
    rows = rows8 // DEPTH
    wide = cols + 2 * LANE
    per = lambda a: pl.BlockSpec((1,) + a.shape[1:], lambda i: (i,) + (0,) * (a.ndim - 1))
    same = lambda a: pl.BlockSpec(a.shape, lambda i: (0,) * a.ndim)
    operands = (exact, above, below, far, left, right, across, within)
    outs = (
        (n, DEPTH, rows, cols),
        (n, DEPTH // 2, rows // 2, cols // 2),
        (n, DEPTH // 4, rows // 4, cols // 4),
    )
    shapes = [jax.ShapeDtypeStruct(s, F32) for s in outs]
    first = 5 * BIG * DEPTH
    second = 4 * BIG * DEPTH
    third = 3 * SMALL * DEPTH
    return pl.pallas_call(
        deconvolve_kernel,
        grid=(n,),
        in_specs=[pl.BlockSpec(memory_space=pltpu.SMEM)]
        + [per(a) for a in operands]
        + [same(m) for m in matrices],
        out_specs=[per(s) for s in shapes],
        out_shape=shapes,
        scratch_shapes=[
            pltpu.VMEM((FRAME * DEPTH, wide), F32),
            pltpu.VMEM((FRAME * DEPTH, wide), BF16),
            pltpu.VMEM((first, wide), BF16),
            pltpu.VMEM((second, wide), F32),
            pltpu.VMEM((second, wide), BF16),
            pltpu.VMEM((wide // LANE, third, LANE), F32),
            pltpu.VMEM((FRAME * DEPTH, wide), BF16),
            pltpu.VMEM((first, wide), BF16),
        ],
        compiler_params=params(52),
        cost_estimate=cost(n * 9e9, n * 8e6),
        name="deconvolve",
    )(sides, *operands, *matrices)


def per_device(tiles, offsets, psf):
    chans, depth, tile_y, tile_x = tiles.shape
    cols = tile_x - MARGIN
    rows = tile_y - MARGIN
    size_x, size_y = lax.axis_size("gx"), lax.axis_size("gy")
    at_x, at_y = lax.axis_index("gx"), lax.axis_index("gy")

    def shift(block, axis, distance):
        devices = range(lax.axis_size(axis))
        route = [(i, i + distance) for i in devices if i + distance in devices]
        return lax.ppermute(block, axis, route)

    def shift_diagonal(block):
        route = [
            (x * size_y + y, (x + 1) * size_y + y + 1)
            for x in range(size_x - 1)
            for y in range(size_y - 1)
        ]
        return lax.ppermute(block, ("gx", "gy"), route)

    kern = psf / jnp.sum(psf, axis=-1, keepdims=True)
    both = jnp.stack([kern, kern[:, :, ::-1]], axis=1)
    across, within = bands(both.reshape(chans * 2, 3 * TAPS))
    across = across.reshape((chans, 2) + across.shape[1:])
    within = within.reshape((chans, 2) + within.shape[1:])
    matrices = [jnp.asarray(m) for m in pyramid_matrices(rows, cols, depth)]
    sides = jnp.stack([at_y > 0, at_y < size_y - 1, at_x > 0, at_x < size_x - 1])
    sides = sides.astype(jnp.int32)

    own, right, low, corner = place(tiles, offsets.reshape(2))
    low = shift(low, "gy", 1)
    right = shift(right, "gx", 1)
    corner = shift_diagonal(corner)
    exact, short = join(own, low, right, corner)
    above = shift(short, "gy", 1)
    below = shift(short, "gy", -1)
    far = shift(short[:, -2 * depth :, :], "gy", 2)
    column = (far, above, short, below)
    last = jnp.concatenate([a[:, :, -LANE:] for a in column], axis=1)
    first = jnp.concatenate([a[:, :, :LANE] for a in column], axis=1)
    left = shift(last, "gx", 1)
    right = shift(first, "gx", -1)
    return tuple(
        deconvolve(sides, exact, above, below, far, left, right, across, within, matrices)
    )


def solution(mesh):
    in_specs = (P(None, None, "gy", "gx"), P("gy", "gx", None), P())
    out_specs = (P(None, None, "gy", "gx"), P(None, None, "gy", "gx"), P(None, None, "gy", "gx"))
    return jax.shard_map(
        per_device, mesh=mesh, in_specs=in_specs, out_specs=out_specs, check_vma=False
    )
```

```python
import functools

import jax
import jax.numpy as jnp
import ml_dtypes
import numpy as np
from jax import lax
from jax.experimental import pallas as pl
from jax.experimental.pallas import tpu as pltpu
from jax.sharding import PartitionSpec as P

MARGIN = 32
REACH = 15
TAPS = 31
DEPTH = 8
LANE = 128
GAUSS = (1, 4, 6, 4, 1)
TINY = 1e-30
BF16 = jnp.bfloat16
F32 = jnp.float32
MIB = 1 << 20

BEFORE = 66
FRAME = 200
BIG = 34
SMALL = 26


def params(mib):
    return pltpu.CompilerParams(vmem_limit_bytes=mib * MIB)


def cost(flops, nbytes):
    return pl.CostEstimate(flops=int(flops), bytes_accessed=int(nbytes), transcendentals=0)


def dot(a, b):
    return jnp.dot(a, b, preferred_element_type=F32)


def split(value):
    high = value.astype(BF16)
    return high, (value - high.astype(F32)).astype(BF16)


def place_kernel(off_ref, tile_ref, own_ref, right_ref, low_ref, canvas):
    depth, tile_y, tile_x = tile_ref.shape[1:]
    parts = canvas.shape[0]
    wide = parts * LANE
    rows = own_ref.shape[1]
    cols = own_ref.shape[2]
    top = off_ref[0]
    left = off_ref[1]
    canvas[...] = jnp.zeros_like(canvas)
    shift = (
        lax.broadcasted_iota(jnp.int32, (tile_x, wide), 1)
        == lax.broadcasted_iota(jnp.int32, (tile_x, wide), 0) + left
    )
    shift = jnp.where(shift, 1.0, 0.0).astype(BF16)
    for z in range(depth):
        moved = dot(tile_ref[0, z], shift)
        for b in range(parts):
            to = pl.ds(top * depth + z, tile_y, stride=depth)
            canvas[b, to, :] = moved[:, b * LANE : (b + 1) * LANE]
    for b in range(parts - 1):
        to = slice(b * LANE, (b + 1) * LANE)
        own_ref[0, :, to] = canvas[b, :rows, :].astype(BF16)
        low_ref[0, :rows, to] = canvas[b, rows:, :].astype(BF16)
    right_ref[0] = canvas[parts - 1, :rows, :].astype(BF16)
    half = rows // 2
    upper = canvas[parts - 1, rows : rows + half, :]
    lower = canvas[parts - 1, rows + half :, :]
    corner = (upper + pltpu.roll(lower, LANE // 2, 1)).astype(BF16)
    eighth = half // (parts - 1)
    for b in range(parts - 1):
        low_ref[0, rows:, b * LANE : (b + 1) * LANE] = corner[b * eighth : (b + 1) * eighth]


def place(tiles, offsets, begin, n):
    _, depth, tile_y, tile_x = tiles.shape
    rows = (tile_y - MARGIN) * depth
    cols = tile_x - MARGIN
    block = lambda r, c: pl.BlockSpec((1, r, c), lambda i, off: (i, 0, 0))
    shape = lambda r, c: jax.ShapeDtypeStruct((n, r, c), BF16)
    extra = rows // 2 * LANE // cols
    sizes = ((rows, cols), (rows, LANE), (rows + extra, cols))
    tile = pl.BlockSpec((1, depth, tile_y, tile_x), lambda i, off: (begin + i, 0, 0, 0))
    return pl.pallas_call(
        place_kernel,
        grid_spec=pltpu.PrefetchScalarGridSpec(
            num_scalar_prefetch=1,
            grid=(n,),
            in_specs=[tile],
            out_specs=[block(*s) for s in sizes],
            scratch_shapes=[pltpu.VMEM((cols // LANE + 1, 2 * rows, LANE), F32)],
        ),
        out_shape=[shape(*s) for s in sizes],
        compiler_params=params(16),
        cost_estimate=cost(n * 2e9, n * 2.5e6),
        name="place",
    )(offsets, tiles)


def join_kernel(own_ref, low_ref, side_ref, exact_ref, short_ref, tail_ref):
    rows = own_ref.shape[1]
    half = rows // 2

    def seen(x):
        return jnp.where(x != 0, 1.0, 0.0)

    own = own_ref[0].astype(F32)
    low = low_ref[0].astype(F32)
    total = own + low
    count = seen(own) + seen(low)
    right = side_ref[0, :rows].astype(F32)
    corner = side_ref[0, rows:].astype(F32)
    lane = lax.broadcasted_iota(jnp.int32, (half, LANE), 1)
    inside = lane < LANE // 2
    upper = jnp.where(inside, corner, 0.0)
    lower = jnp.where(inside, pltpu.roll(corner, LANE // 2, 1), 0.0)
    corner = jnp.concatenate([upper, lower], axis=0)
    edge_total = total[:, :LANE] + right + corner
    edge_count = count[:, :LANE] + seen(right) + seen(corner)
    edge = edge_total / edge_count
    rest = total[:, LANE:] / count[:, LANE:]
    exact_ref[0, :, :LANE] = edge
    exact_ref[0, :, LANE:] = rest
    short_ref[0, :, :LANE] = edge.astype(BF16)
    short_ref[0, :, LANE:] = rest.astype(BF16)
    tail = tail_ref.shape[1]
    tail_ref[0, :, :LANE] = edge[rows - tail :].astype(BF16)
    tail_ref[0, :, LANE:] = rest[rows - tail :].astype(BF16)


def join(own, low, side, at):
    _, rows, cols = own.shape
    block = lambda r, c, k: pl.BlockSpec((1, r, c), lambda i: (k, 0, 0))
    tail = 2 * DEPTH
    sizes = ((rows, cols, F32), (rows, cols, BF16), (tail, cols, BF16))
    return pl.pallas_call(
        join_kernel,
        grid=(1,),
        in_specs=[block(rows, cols, at), block(rows, cols, at), block(*side.shape[1:], at)],
        out_specs=[block(r, c, 0) for r, c, _ in sizes],
        out_shape=[jax.ShapeDtypeStruct((1, r, c), t) for r, c, t in sizes],
        compiler_params=params(16),
        cost_estimate=cost(5e6, 3e6),
        name="join",
    )(own, low, side)


def bands_kernel(kern_ref, across_ref, within_ref):
    which = pl.program_id(0)
    wide = 3 * 2 * LANE
    shape = (16, wide)
    row = lax.broadcasted_iota(jnp.int32, shape, 0)
    lane = lax.broadcasted_iota(jnp.int32, shape, 1)
    tap = row - (lane - 4 * LANE) - (LANE - REACH)
    base = jnp.zeros(shape, F32)
    for k in range(TAPS):
        base = jnp.where(tap == k, kern_ref[which, 2 * TAPS + k], base)

    for q in range(across_ref.shape[1] // 16):
        turned = pltpu.roll(base, (wide - 4 * LANE + 16 * q) % wide, 1)
        across_ref[0, 16 * q : 16 * (q + 1), :] = turned[:, : 2 * LANE].astype(BF16)

    shape = (16, within_ref.shape[2])
    row = lax.broadcasted_iota(jnp.int32, shape, 0)
    lane = lax.broadcasted_iota(jnp.int32, shape, 1)
    tap_y = lane // DEPTH - row // DEPTH
    tap_z = lane % DEPTH - row % DEPTH + REACH
    in_y = jnp.zeros(shape, F32)
    in_z = jnp.zeros(shape, F32)
    for k in range(TAPS):
        in_y = jnp.where(tap_y == k, kern_ref[which, TAPS + k], in_y)
    for k in range(REACH + 1 - DEPTH, REACH + DEPTH):
        in_z = jnp.where(tap_z == k, kern_ref[which, k], in_z)
    both = in_y * in_z

    for q in range(within_ref.shape[1] // 16):
        turned = pltpu.roll(both, 16 * q, 1)
        within_ref[0, 16 * q : 16 * (q + 1), :] = turned.astype(BF16)


def bands(kern):
    count = kern.shape[0]
    shapes = ((4 * LANE, 2 * LANE), (BIG * DEPTH, (BIG + 2 * REACH) * DEPTH))
    return pl.pallas_call(
        bands_kernel,
        grid=(count,),
        in_specs=[pl.BlockSpec(memory_space=pltpu.SMEM)],
        out_specs=[pl.BlockSpec((1,) + s, lambda i: (i, 0, 0)) for s in shapes],
        out_shape=[jax.ShapeDtypeStruct((count,) + s, BF16) for s in shapes],
        compiler_params=params(32),
        cost_estimate=cost(count * 1e6, count * 4e6),
        name="bands",
    )(kern)


@functools.lru_cache(None)
def pyramid_matrices(rows, cols, depth):
    half_x, half_y, half_z = cols // 2, rows // 2, depth // 2
    taps = np.array(GAUSS, np.float32) / 16
    extra_x = (-2, -1, half_x)
    one_x = np.zeros((cols + 2 * LANE, half_x + LANE), np.float32)
    for lane in range(half_x + len(extra_x)):
        x = lane if lane < half_x else extra_x[lane - half_x]
        for k in range(5):
            one_x[LANE + 2 * x + k - 2, lane] = taps[k]
    extra_y = (-2, -1, half_y)
    order = [(z, y) for z in range(half_z) for y in range(half_y)]
    order += [(z, y) for y in extra_y for z in range(half_z)]
    height = -(-len(order) // 16) * 16
    reach_in = (rows + 10) * depth
    one_zy = np.zeros((height, reach_in), np.float32)
    for i, (z, y) in enumerate(order):
        for a in range(5):
            for b in range(5):
                zi = 2 * z + b - 2
                if 0 <= zi < depth:
                    one_zy[i, (2 * y + a - 2 + 6) * depth + zi] = taps[a] * taps[b]
    two_x = np.zeros((half_x + LANE, half_x // 2), np.float32)
    for x in range(half_x // 2):
        for k in range(5):
            source = 2 * x + k - 2
            lane = source if 0 <= source < half_x else half_x + extra_x.index(source)
            two_x[lane, x] = taps[k]
    place_of = {zy: i for i, zy in enumerate(order)}
    two_zy = np.zeros((half_z * half_y // 4, height), np.float32)
    for z in range(half_z // 2):
        for y in range(half_y // 2):
            for a in range(5):
                for b in range(5):
                    at = (2 * z + b - 2, 2 * y + a - 2)
                    if 0 <= at[0] < half_z:
                        two_zy[z * (half_y // 2) + y, place_of[at]] = taps[a] * taps[b]
    return tuple(m.astype(ml_dtypes.bfloat16) for m in (one_x, one_zy, two_x, two_zy))


def deconvolve_kernel(
    sides_ref,
    exact_ref,
    above_ref,
    below_ref,
    far_ref,
    left_ref,
    right_ref,
    across_ref,
    within_ref,
    one_x_ref,
    one_zy_ref,
    two_x_ref,
    two_zy_ref,
    *others,
):
    if len(others) > 11:
        others = others[3:]
    deconvolve_body(
        sides_ref,
        exact_ref,
        above_ref,
        below_ref,
        far_ref,
        left_ref,
        right_ref,
        across_ref,
        within_ref,
        one_x_ref,
        one_zy_ref,
        two_x_ref,
        two_zy_ref,
        *others,
    )


def deconvolve_body(
    sides_ref,
    exact_ref,
    above_ref,
    below_ref,
    far_ref,
    left_ref,
    right_ref,
    across_ref,
    within_ref,
    one_x_ref,
    one_zy_ref,
    two_x_ref,
    two_zy_ref,
    restored_ref,
    level_one_ref,
    level_two_ref,
    joined,
    joined_short,
    ratio,
    estimate,
    estimate_short,
    result,
    high,
    low,
):
    rows8, cols = exact_ref.shape[1:]
    wide = cols + 2 * LANE
    far8 = far_ref.shape[1]
    own = slice(far8 + rows8, far8 + 2 * rows8)
    frame8 = far8 + 3 * rows8
    middle = slice(LANE, LANE + cols)

    joined_short[:far8, middle] = far_ref[0]
    joined_short[far8 : far8 + rows8, middle] = above_ref[0]
    joined_short[own, middle] = exact_ref[0].astype(BF16)
    joined_short[far8 + 2 * rows8 : frame8, middle] = below_ref[0]
    joined_short[:frame8, :LANE] = left_ref[0]
    joined_short[:frame8, LANE + cols :] = right_ref[0]
    joined_short[frame8:, :] = jnp.zeros_like(joined_short[frame8:, :])
    joined[...] = joined_short[...].astype(F32)
    joined[own, middle] = exact_ref[0]

    def run_x(source, which, begin_at, end_at, size, exact):
        @pl.loop(begin_at, end_at)
        def _(i):
            at = pl.ds(pl.multiple_of(i * size, 16), size)
            for n in range(wide // (2 * LANE)):
                begin = 2 * LANE * n - LANE
                lo, hi = max(begin, 0), min(begin + 4 * LANE, wide)
                out = dot(source[at, lo:hi], across_ref[0, which, lo - begin : hi - begin, :])
                to = slice(2 * LANE * n, 2 * LANE * (n + 1))
                if exact:
                    high[at, to], low[at, to] = split(out)
                else:
                    high[at, to] = out.astype(BF16)

    def run_zy(which, begin_at, end_at, size, exact, finish):
        deep = (size + 2 * REACH) * DEPTH
        matrix = within_ref[0, which, : size * DEPTH, :deep]

        @pl.loop(begin_at, end_at)
        def _(i):
            start = i * (size * DEPTH)
            at = pl.ds(pl.multiple_of(start, 16), deep)
            for n in range(wide // (2 * LANE)):
                to = slice(2 * LANE * n, 2 * LANE * (n + 1))
                out = dot(matrix, high[at, to])
                if exact:
                    out = out + dot(matrix, low[at, to])
                finish(start, size * DEPTH, to, out)

    def rows_at(start, shift, size):
        return pl.ds(pl.multiple_of(start + shift * DEPTH, 8), size)

    def ratio_from(shift):
        def finish(start, size, to, out):
            top = joined[rows_at(start, shift, size), to]
            at = pl.ds(pl.multiple_of(start, 16), size)
            ratio[at, to] = (top / jnp.maximum(out, TINY)).astype(BF16)

        return finish

    def first_estimate(start, size, to, out):
        at = pl.ds(pl.multiple_of(start, 16), size)
        value = joined[rows_at(start, 2 * REACH, size), to] * out
        estimate[at, to] = value
        estimate_short[at, to] = value.astype(BF16)

    def last_estimate(start, size, to, out):
        at = pl.ds(pl.multiple_of(start, 16), size)
        value = estimate[rows_at(start, 2 * REACH, size), to] * out
        for b in range(2):
            result[to.start // LANE + b, at, :] = value[:, b * LANE : (b + 1) * LANE]

    run_x(joined_short, 0, 0, 5, 40 * DEPTH, False)
    run_zy(0, 0, 5, BIG, False, ratio_from(REACH))
    run_x(ratio, 1, 0, 1, BIG * DEPTH, False)
    run_x(ratio, 1, 1, 4, BIG * DEPTH, True)
    run_x(ratio, 1, 4, 5, BIG * DEPTH, False)
    run_zy(1, 0, 1, BIG, False, first_estimate)
    run_zy(1, 1, 3, BIG, True, first_estimate)
    run_zy(1, 3, 4, BIG, False, first_estimate)
    run_x(estimate_short, 0, 0, 4, BIG * DEPTH, False)
    run_zy(0, 0, 4, SMALL, False, ratio_from(3 * REACH))
    ratio[4 * SMALL * DEPTH : (4 * SMALL + 4) * DEPTH, :] = jnp.zeros((4 * DEPTH, wide), BF16)
    run_x(ratio, 1, 0, 3, 36 * DEPTH, True)
    run_zy(1, 0, 3, SMALL, True, last_estimate)

    planes = restored_ref.shape[1]
    height = restored_ref.shape[2]
    for z in range(planes):
        at = pl.ds(6 * planes + z, height, stride=planes)
        for b in range(cols // LANE):
            restored_ref[0, z, :, b * LANE : (b + 1) * LANE] = result[1 + b, at, :]

    def twice(left, right):
        big, small = split(right)
        return dot(left, big) + dot(left, small)

    def twice_left(left, right):
        big, small = split(left)
        return dot(big, right) + dot(small, right)

    reach_in = one_zy_ref.shape[1]
    fine = jnp.concatenate([result[b, :reach_in, :] for b in range(wide // LANE)], axis=1)
    one = twice(one_zy_ref[...], dot(fine.astype(BF16), one_x_ref[...]))
    half_z, half_y, half_x = level_one_ref.shape[1:]
    inner = half_z * half_y
    level_one_ref[0] = one[:inner, :half_x].reshape(half_z, half_y, half_x)
    row = lax.broadcasted_iota(jnp.int32, one.shape, 0) - inner
    lane = lax.broadcasted_iota(jnp.int32, one.shape, 1) - half_x
    up, down, left, right = (sides_ref[k] for k in range(4))
    keep_row = jnp.where(row < 0, 1, jnp.where(row < 2 * half_z, up, down))
    keep_lane = jnp.where(lane < 0, 1, jnp.where(lane < 2, left, right))
    one = jnp.where(keep_row * keep_lane > 0, one, 0.0)
    two = twice(two_zy_ref[...], twice_left(one, two_x_ref[...]))
    level_two_ref[0] = two.reshape(level_two_ref.shape[1:])


def deconvolve(at, chans, sides, group, across, within, matrices, earlier):
    rows8, cols = group[0].shape[1:]
    rows = rows8 // DEPTH
    wide = cols + 2 * LANE
    first = lambda a: pl.BlockSpec((1,) + a.shape[1:], lambda i: (0,) * a.ndim)
    mine = lambda s: pl.BlockSpec((1,) + s[1:], lambda i: (at,) + (0,) * (len(s) - 1))
    same = lambda a: pl.BlockSpec(a.shape, lambda i: (0,) * a.ndim)
    outs = (
        (chans, DEPTH, rows, cols),
        (chans, DEPTH // 2, rows // 2, cols // 2),
        (chans, DEPTH // 4, rows // 4, cols // 4),
    )
    shapes = [jax.ShapeDtypeStruct(s, F32) for s in outs]
    ratio_rows = 5 * BIG * DEPTH
    estimate_rows = 4 * BIG * DEPTH
    result_rows = 3 * SMALL * DEPTH
    operands = [sides, *group, across, within, *matrices]
    return pl.pallas_call(
        deconvolve_kernel,
        grid=(1,),
        in_specs=[pl.BlockSpec(memory_space=pltpu.SMEM)]
        + [first(a) for a in group]
        + [mine(across.shape), mine(within.shape)]
        + [same(m) for m in matrices]
        + [pl.BlockSpec(memory_space=pl.ANY) for _ in earlier],
        out_specs=[mine(s) for s in outs],
        out_shape=shapes,
        input_output_aliases={len(operands) + k: k for k in range(len(earlier))},
        scratch_shapes=[
            pltpu.VMEM((FRAME * DEPTH, wide), F32),
            pltpu.VMEM((FRAME * DEPTH, wide), BF16),
            pltpu.VMEM((ratio_rows, wide), BF16),
            pltpu.VMEM((estimate_rows, wide), F32),
            pltpu.VMEM((estimate_rows, wide), BF16),
            pltpu.VMEM((wide // LANE, result_rows, LANE), F32),
            pltpu.VMEM((FRAME * DEPTH, wide), BF16),
            pltpu.VMEM((ratio_rows, wide), BF16),
        ],
        compiler_params=params(40),
        cost_estimate=cost(9e9, 8e6),
        name="deconvolve",
    )(*operands, *earlier)


def per_device(tiles, offsets, psf):
    chans, depth, tile_y, tile_x = tiles.shape
    cols = tile_x - MARGIN
    rows = tile_y - MARGIN
    size_x, size_y = lax.axis_size("gx"), lax.axis_size("gy")
    at_x, at_y = lax.axis_index("gx"), lax.axis_index("gy")

    def shift(block, axis, distance):
        devices = range(lax.axis_size(axis))
        route = [(i, i + distance) for i in devices if i + distance in devices]
        return lax.ppermute(block, axis, route)

    sides = jnp.stack([at_y > 0, at_y < size_y - 1, at_x > 0, at_x < size_x - 1])
    sides = sides.astype(jnp.int32)
    matrices = [jnp.asarray(m) for m in pyramid_matrices(rows, cols, depth)]

    parts = ((0, 1), (1, chans - 1))
    placed = [place(tiles, offsets.reshape(2), begin, n) for begin, n in parts]
    lows = [shift(low, "gy", 1) for _, _, low in placed]

    psf, _ = lax.optimization_barrier((psf, placed[0][1]))
    kern = psf / jnp.sum(psf, axis=-1, keepdims=True)
    both = jnp.stack([kern, kern[:, :, ::-1]], axis=1)
    across, within = bands(both.reshape(chans * 2, 3 * TAPS))
    across = across.reshape((chans, 2) + across.shape[1:])
    within = within.reshape((chans, 2) + within.shape[1:])
    lows[0], across, within = lax.optimization_barrier((lows[0], across, within))

    joined = []
    for (begin, n), (own, right, _), low in zip(parts, placed, lows):
        strips = [low[:, rows * depth :, k : k + LANE] for k in range(0, cols, LANE)]
        side = shift(jnp.concatenate([right] + strips, axis=1), "gx", 1)
        joined += [join(own, low, side, k) for k in range(n)]

    arrived = []
    for _, short, tail in joined:
        above = shift(short, "gy", 1)
        below = shift(short, "gy", -1)
        far = shift(tail, "gy", 2)
        arrived.append((above, below, far))

    outs = ()
    for at in range(chans):
        exact, short, _ = joined[at]
        above, below, far = arrived[at]
        if at == chans - 1:
            above, below, _ = lax.optimization_barrier((above, below, outs[2]))
        column = (far, above, short, below)
        last = jnp.concatenate([a[:, :, -LANE:] for a in column], axis=1)
        first = jnp.concatenate([a[:, :, :LANE] for a in column], axis=1)
        left = shift(last, "gx", 1)
        right = shift(first, "gx", -1)
        group = (exact, above, below, far, left, right)
        outs = deconvolve(at, chans, sides, group, across, within, matrices, outs)
    return tuple(outs)


def solution(mesh):
    in_specs = (P(None, None, "gy", "gx"), P("gy", "gx", None), P())
    out_specs = (P(None, None, "gy", "gx"), P(None, None, "gy", "gx"), P(None, None, "gy", "gx"))
    return jax.shard_map(
        per_device, mesh=mesh, in_specs=in_specs, out_specs=out_specs, check_vma=False
    )
```

```python
import functools

import jax
import jax.numpy as jnp
import ml_dtypes
import numpy as np
from jax import lax
from jax.experimental import pallas as pl
from jax.experimental.pallas import tpu as pltpu
from jax.sharding import PartitionSpec as P

MARGIN = 32
REACH = 15
TAPS = 31
DEPTH = 8
LANE = 128
GAUSS = (1, 4, 6, 4, 1)
TINY = 1e-30
BF16 = jnp.bfloat16
F32 = jnp.float32
MIB = 1 << 20

BEFORE = 66
FRAME = 200
BIG = 34
SMALL = 26


def params(mib):
    return pltpu.CompilerParams(vmem_limit_bytes=mib * MIB)


def cost(flops, nbytes):
    return pl.CostEstimate(flops=int(flops), bytes_accessed=int(nbytes), transcendentals=0)


def dot(a, b):
    return jnp.dot(a, b, preferred_element_type=F32)


def split(value):
    high = value.astype(BF16)
    return high, (value - high.astype(F32)).astype(BF16)


def place_kernel(off_ref, tile_ref, own_ref, right_ref, low_ref, canvas):
    depth, tile_y, tile_x = tile_ref.shape[1:]
    parts = canvas.shape[0]
    wide = parts * LANE
    rows = own_ref.shape[1]
    cols = own_ref.shape[2]
    top = off_ref[0]
    left = off_ref[1]
    canvas[...] = jnp.zeros_like(canvas)
    shift = (
        lax.broadcasted_iota(jnp.int32, (tile_x, wide), 1)
        == lax.broadcasted_iota(jnp.int32, (tile_x, wide), 0) + left
    )
    shift = jnp.where(shift, 1.0, 0.0).astype(BF16)
    for z in range(depth):
        moved = dot(tile_ref[0, z], shift)
        for b in range(parts):
            to = pl.ds(top * depth + z, tile_y, stride=depth)
            canvas[b, to, :] = moved[:, b * LANE : (b + 1) * LANE]
    for b in range(parts - 1):
        to = slice(b * LANE, (b + 1) * LANE)
        own_ref[0, :, to] = canvas[b, :rows, :].astype(BF16)
        low_ref[0, :rows, to] = canvas[b, rows:, :].astype(BF16)
    right_ref[0] = canvas[parts - 1, :rows, :].astype(BF16)
    half = rows // 2
    upper = canvas[parts - 1, rows : rows + half, :]
    lower = canvas[parts - 1, rows + half :, :]
    corner = (upper + pltpu.roll(lower, LANE // 2, 1)).astype(BF16)
    eighth = half // (parts - 1)
    for b in range(parts - 1):
        low_ref[0, rows:, b * LANE : (b + 1) * LANE] = corner[b * eighth : (b + 1) * eighth]


def place(tiles, offsets, begin, n):
    _, depth, tile_y, tile_x = tiles.shape
    rows = (tile_y - MARGIN) * depth
    cols = tile_x - MARGIN
    block = lambda r, c: pl.BlockSpec((1, r, c), lambda i, off: (i, 0, 0))
    shape = lambda r, c: jax.ShapeDtypeStruct((n, r, c), BF16)
    extra = rows // 2 * LANE // cols
    sizes = ((rows, cols), (rows, LANE), (rows + extra, cols))
    tile = pl.BlockSpec((1, depth, tile_y, tile_x), lambda i, off: (begin + i, 0, 0, 0))
    return pl.pallas_call(
        place_kernel,
        grid_spec=pltpu.PrefetchScalarGridSpec(
            num_scalar_prefetch=1,
            grid=(n,),
            in_specs=[tile],
            out_specs=[block(*s) for s in sizes],
            scratch_shapes=[pltpu.VMEM((cols // LANE + 1, 2 * rows, LANE), F32)],
        ),
        out_shape=[shape(*s) for s in sizes],
        compiler_params=params(16),
        cost_estimate=cost(n * 2e9, n * 2.5e6),
        name="place",
    )(offsets, tiles)


def join_kernel(own_ref, low_ref, side_ref, exact_ref, short_ref, tail_ref):
    rows = own_ref.shape[1]
    half = rows // 2

    def seen(x):
        return jnp.where(x != 0, 1.0, 0.0)

    own = own_ref[0].astype(F32)
    low = low_ref[0].astype(F32)
    total = own + low
    count = seen(own) + seen(low)
    right = side_ref[0, :rows].astype(F32)
    corner = side_ref[0, rows:].astype(F32)
    lane = lax.broadcasted_iota(jnp.int32, (half, LANE), 1)
    inside = lane < LANE // 2
    upper = jnp.where(inside, corner, 0.0)
    lower = jnp.where(inside, pltpu.roll(corner, LANE // 2, 1), 0.0)
    corner = jnp.concatenate([upper, lower], axis=0)
    edge_total = total[:, :LANE] + right + corner
    edge_count = count[:, :LANE] + seen(right) + seen(corner)
    edge = edge_total / edge_count
    rest = total[:, LANE:] / count[:, LANE:]
    exact_ref[0, :, :LANE] = edge
    exact_ref[0, :, LANE:] = rest
    short_ref[0, :, :LANE] = edge.astype(BF16)
    short_ref[0, :, LANE:] = rest.astype(BF16)
    tail = tail_ref.shape[1]
    tail_ref[0, :, :LANE] = edge[rows - tail :].astype(BF16)
    tail_ref[0, :, LANE:] = rest[rows - tail :].astype(BF16)


def join(own, low, side, at):
    _, rows, cols = own.shape
    block = lambda r, c, k: pl.BlockSpec((1, r, c), lambda i: (k, 0, 0))
    tail = 2 * DEPTH
    sizes = ((rows, cols, F32), (rows, cols, BF16), (tail, cols, BF16))
    return pl.pallas_call(
        join_kernel,
        grid=(1,),
        in_specs=[block(rows, cols, at), block(rows, cols, at), block(*side.shape[1:], at)],
        out_specs=[block(r, c, 0) for r, c, _ in sizes],
        out_shape=[jax.ShapeDtypeStruct((1, r, c), t) for r, c, t in sizes],
        compiler_params=params(16),
        cost_estimate=cost(5e6, 3e6),
        name="join",
    )(own, low, side)


def bands_kernel(kern_ref, across_ref, within_ref):
    which = pl.program_id(0)
    wide = 3 * 2 * LANE
    shape = (16, wide)
    row = lax.broadcasted_iota(jnp.int32, shape, 0)
    lane = lax.broadcasted_iota(jnp.int32, shape, 1)
    tap = row - (lane - 4 * LANE) - (LANE - REACH)
    base = jnp.zeros(shape, F32)
    for k in range(TAPS):
        base = jnp.where(tap == k, kern_ref[which, 2 * TAPS + k], base)

    for q in range(across_ref.shape[1] // 16):
        turned = pltpu.roll(base, (wide - 4 * LANE + 16 * q) % wide, 1)
        across_ref[0, 16 * q : 16 * (q + 1), :] = turned[:, : 2 * LANE].astype(BF16)

    shape = (16, within_ref.shape[2])
    row = lax.broadcasted_iota(jnp.int32, shape, 0)
    lane = lax.broadcasted_iota(jnp.int32, shape, 1)
    tap_y = lane // DEPTH - row // DEPTH
    tap_z = lane % DEPTH - row % DEPTH + REACH
    in_y = jnp.zeros(shape, F32)
    in_z = jnp.zeros(shape, F32)
    for k in range(TAPS):
        in_y = jnp.where(tap_y == k, kern_ref[which, TAPS + k], in_y)
    for k in range(REACH + 1 - DEPTH, REACH + DEPTH):
        in_z = jnp.where(tap_z == k, kern_ref[which, k], in_z)
    both = in_y * in_z

    for q in range(within_ref.shape[1] // 16):
        turned = pltpu.roll(both, 16 * q, 1)
        within_ref[0, 16 * q : 16 * (q + 1), :] = turned.astype(BF16)


def bands(kern):
    count = kern.shape[0]
    shapes = ((4 * LANE, 2 * LANE), (BIG * DEPTH, (BIG + 2 * REACH) * DEPTH))
    return pl.pallas_call(
        bands_kernel,
        grid=(count,),
        in_specs=[pl.BlockSpec(memory_space=pltpu.SMEM)],
        out_specs=[pl.BlockSpec((1,) + s, lambda i: (i, 0, 0)) for s in shapes],
        out_shape=[jax.ShapeDtypeStruct((count,) + s, BF16) for s in shapes],
        compiler_params=params(32),
        cost_estimate=cost(count * 1e6, count * 4e6),
        name="bands",
    )(kern)


@functools.lru_cache(None)
def pyramid_matrices(rows, cols, depth):
    half_x, half_y, half_z = cols // 2, rows // 2, depth // 2
    taps = np.array(GAUSS, np.float32) / 16
    extra_x = (-2, -1, half_x)
    one_x = np.zeros((cols + 2 * LANE, half_x + LANE), np.float32)
    for lane in range(half_x + len(extra_x)):
        x = lane if lane < half_x else extra_x[lane - half_x]
        for k in range(5):
            one_x[LANE + 2 * x + k - 2, lane] = taps[k]
    extra_y = (-2, -1, half_y)
    order = [(z, y) for z in range(half_z) for y in range(half_y)]
    order += [(z, y) for y in extra_y for z in range(half_z)]
    height = -(-len(order) // 16) * 16
    reach_in = (rows + 10) * depth
    one_zy = np.zeros((height, reach_in), np.float32)
    for i, (z, y) in enumerate(order):
        for a in range(5):
            for b in range(5):
                zi = 2 * z + b - 2
                if 0 <= zi < depth:
                    one_zy[i, (2 * y + a - 2 + 6) * depth + zi] = taps[a] * taps[b]
    two_x = np.zeros((half_x + LANE, half_x // 2), np.float32)
    for x in range(half_x // 2):
        for k in range(5):
            source = 2 * x + k - 2
            lane = source if 0 <= source < half_x else half_x + extra_x.index(source)
            two_x[lane, x] = taps[k]
    place_of = {zy: i for i, zy in enumerate(order)}
    two_zy = np.zeros((half_z * half_y // 4, height), np.float32)
    for z in range(half_z // 2):
        for y in range(half_y // 2):
            for a in range(5):
                for b in range(5):
                    at = (2 * z + b - 2, 2 * y + a - 2)
                    if 0 <= at[0] < half_z:
                        two_zy[z * (half_y // 2) + y, place_of[at]] = taps[a] * taps[b]
    return tuple(m.astype(ml_dtypes.bfloat16) for m in (one_x, one_zy, two_x, two_zy))


def deconvolve_kernel(
    sides_ref,
    exact_ref,
    above_ref,
    below_ref,
    far_ref,
    left_ref,
    right_ref,
    across_ref,
    within_ref,
    one_x_ref,
    one_zy_ref,
    two_x_ref,
    two_zy_ref,
    *others,
):
    if len(others) > 11:
        others = others[3:]
    deconvolve_body(
        sides_ref,
        exact_ref,
        above_ref,
        below_ref,
        far_ref,
        left_ref,
        right_ref,
        across_ref,
        within_ref,
        one_x_ref,
        one_zy_ref,
        two_x_ref,
        two_zy_ref,
        *others,
    )


def deconvolve_body(
    sides_ref,
    exact_ref,
    above_ref,
    below_ref,
    far_ref,
    left_ref,
    right_ref,
    across_ref,
    within_ref,
    one_x_ref,
    one_zy_ref,
    two_x_ref,
    two_zy_ref,
    restored_ref,
    level_one_ref,
    level_two_ref,
    joined,
    joined_short,
    ratio,
    estimate,
    estimate_short,
    result,
    high,
    low,
):
    rows8, cols = exact_ref.shape[1:]
    wide = cols + 2 * LANE
    far8 = far_ref.shape[1]
    own = slice(far8 + rows8, far8 + 2 * rows8)
    frame8 = far8 + 3 * rows8
    middle = slice(LANE, LANE + cols)

    joined_short[:far8, middle] = far_ref[0]
    joined_short[far8 : far8 + rows8, middle] = above_ref[0]
    joined_short[own, middle] = exact_ref[0].astype(BF16)
    joined_short[far8 + 2 * rows8 : frame8, middle] = below_ref[0]
    joined_short[:frame8, :LANE] = left_ref[0]
    joined_short[:frame8, LANE + cols :] = right_ref[0]
    joined_short[frame8:, :] = jnp.zeros_like(joined_short[frame8:, :])
    joined[...] = joined_short[...].astype(F32)
    joined[own, middle] = exact_ref[0]

    blocks = range(wide // (2 * LANE))

    def correlate(source, which, size, start, exact, finish):
        deep = (size + 2 * REACH) * DEPTH
        size8 = size * DEPTH
        matrix = within_ref[0, which, :size8, :deep]
        here = slice(start, start + size8)
        for n in blocks:
            to = slice(2 * LANE * n, 2 * LANE * (n + 1))
            out = dot(matrix, source[start : start + deep, to])
            if exact:
                high[here, to], low[here, to] = split(out)
            else:
                high[here, to] = out.astype(BF16)
        for n in blocks:
            begin = 2 * LANE * n - LANE
            lo, hi = max(begin, 0), min(begin + 4 * LANE, wide)
            band = across_ref[0, which, lo - begin : hi - begin, :]
            out = dot(high[here, lo:hi], band)
            if exact:
                out = out + dot(low[here, lo:hi], band)
            finish(start, size8, slice(2 * LANE * n, 2 * LANE * (n + 1)), out)

    def ratio_from(shift):
        def finish(start, size8, to, out):
            top = joined[start + shift * DEPTH : start + shift * DEPTH + size8, to]
            bottom = jnp.maximum(out, TINY)
            inverse = pl.reciprocal(bottom, approx=True)
            inverse = inverse * (2.0 - bottom * inverse)
            ratio[start : start + size8, to] = (top * inverse).astype(BF16)

        return finish

    def first_estimate(start, size8, to, out):
        at = slice(start, start + size8)
        begin = start + 2 * REACH * DEPTH
        value = joined[begin : begin + size8, to] * out
        estimate[at, to] = value
        estimate_short[at, to] = value.astype(BF16)

    def last_estimate(start, size8, to, out):
        begin = start + 2 * REACH * DEPTH
        value = estimate[begin : begin + size8, to] * out
        for b in range(2):
            result[to.start // LANE + b, start : start + size8, :] = value[:, b * LANE : (b + 1) * LANE]

    for i in range(5):
        correlate(joined_short, 0, BIG, i * BIG * DEPTH, False, ratio_from(REACH))
    for i in range(4):
        correlate(ratio, 1, BIG, i * BIG * DEPTH, i in (1, 2), first_estimate)
    for i in range(4):
        correlate(estimate_short, 0, SMALL, i * SMALL * DEPTH, False, ratio_from(3 * REACH))
    ratio[4 * SMALL * DEPTH : (4 * SMALL + 4) * DEPTH, :] = jnp.zeros((4 * DEPTH, wide), BF16)
    for i in range(3):
        correlate(ratio, 1, SMALL, i * SMALL * DEPTH, True, last_estimate)

    planes = restored_ref.shape[1]
    height = restored_ref.shape[2]
    for z in range(planes):
        at = pl.ds(6 * planes + z, height, stride=planes)
        for b in range(cols // LANE):
            restored_ref[0, z, :, b * LANE : (b + 1) * LANE] = result[1 + b, at, :]

    def twice(left, right):
        big, small = split(right)
        return dot(left, big) + dot(left, small)

    def twice_left(left, right):
        big, small = split(left)
        return dot(big, right) + dot(small, right)

    reach_in = one_zy_ref.shape[1]
    fine = jnp.concatenate([result[b, :reach_in, :] for b in range(wide // LANE)], axis=1)
    one = twice(one_zy_ref[...], dot(fine.astype(BF16), one_x_ref[...]))
    half_z, half_y, half_x = level_one_ref.shape[1:]
    inner = half_z * half_y
    level_one_ref[0] = one[:inner, :half_x].reshape(half_z, half_y, half_x)
    row = lax.broadcasted_iota(jnp.int32, one.shape, 0) - inner
    lane = lax.broadcasted_iota(jnp.int32, one.shape, 1) - half_x
    up, down, left, right = (sides_ref[k] for k in range(4))
    keep_row = jnp.where(row < 0, 1, jnp.where(row < 2 * half_z, up, down))
    keep_lane = jnp.where(lane < 0, 1, jnp.where(lane < 2, left, right))
    one = jnp.where(keep_row * keep_lane > 0, one, 0.0)
    two = twice(two_zy_ref[...], twice_left(one, two_x_ref[...]))
    level_two_ref[0] = two.reshape(level_two_ref.shape[1:])


def deconvolve(at, chans, sides, group, across, within, matrices, earlier):
    rows8, cols = group[0].shape[1:]
    rows = rows8 // DEPTH
    wide = cols + 2 * LANE
    first = lambda a: pl.BlockSpec((1,) + a.shape[1:], lambda i: (0,) * a.ndim)
    mine = lambda s: pl.BlockSpec((1,) + s[1:], lambda i: (at,) + (0,) * (len(s) - 1))
    same = lambda a: pl.BlockSpec(a.shape, lambda i: (0,) * a.ndim)
    outs = (
        (chans, DEPTH, rows, cols),
        (chans, DEPTH // 2, rows // 2, cols // 2),
        (chans, DEPTH // 4, rows // 4, cols // 4),
    )
    shapes = [jax.ShapeDtypeStruct(s, F32) for s in outs]
    ratio_rows = 5 * BIG * DEPTH
    estimate_rows = 4 * BIG * DEPTH
    result_rows = 3 * SMALL * DEPTH
    operands = [sides, *group, across, within, *matrices]
    return pl.pallas_call(
        deconvolve_kernel,
        grid=(1,),
        in_specs=[pl.BlockSpec(memory_space=pltpu.SMEM)]
        + [first(a) for a in group]
        + [mine(across.shape), mine(within.shape)]
        + [same(m) for m in matrices]
        + [pl.BlockSpec(memory_space=pl.ANY) for _ in earlier],
        out_specs=[mine(s) for s in outs],
        out_shape=shapes,
        input_output_aliases={len(operands) + k: k for k in range(len(earlier))},
        scratch_shapes=[
            pltpu.VMEM((FRAME * DEPTH, wide), F32),
            pltpu.VMEM((FRAME * DEPTH, wide), BF16),
            pltpu.VMEM((ratio_rows, wide), BF16),
            pltpu.VMEM((estimate_rows, wide), F32),
            pltpu.VMEM((estimate_rows, wide), BF16),
            pltpu.VMEM((wide // LANE, result_rows, LANE), F32),
            pltpu.VMEM((ratio_rows, wide), BF16),
            pltpu.VMEM((ratio_rows, wide), BF16),
        ],
        compiler_params=params(40),
        cost_estimate=cost(9e9, 8e6),
        name="deconvolve",
    )(*operands, *earlier)


def per_device(tiles, offsets, psf):
    chans, depth, tile_y, tile_x = tiles.shape
    cols = tile_x - MARGIN
    rows = tile_y - MARGIN
    size_x, size_y = lax.axis_size("gx"), lax.axis_size("gy")
    at_x, at_y = lax.axis_index("gx"), lax.axis_index("gy")

    def shift(block, axis, distance):
        devices = range(lax.axis_size(axis))
        route = [(i, i + distance) for i in devices if i + distance in devices]
        return lax.ppermute(block, axis, route)

    sides = jnp.stack([at_y > 0, at_y < size_y - 1, at_x > 0, at_x < size_x - 1])
    sides = sides.astype(jnp.int32)
    matrices = [jnp.asarray(m) for m in pyramid_matrices(rows, cols, depth)]

    parts = ((0, 1), (1, chans - 1))
    placed = [place(tiles, offsets.reshape(2), begin, n) for begin, n in parts]
    lows = [shift(low, "gy", 1) for _, _, low in placed]

    psf, _ = lax.optimization_barrier((psf, placed[0][1]))
    kern = psf / jnp.sum(psf, axis=-1, keepdims=True)
    both = jnp.stack([kern, kern[:, :, ::-1]], axis=1)
    across, within = bands(both.reshape(chans * 2, 3 * TAPS))
    across = across.reshape((chans, 2) + across.shape[1:])
    within = within.reshape((chans, 2) + within.shape[1:])
    lows[0], across, within = lax.optimization_barrier((lows[0], across, within))

    joined = []
    for (begin, n), (own, right, _), low in zip(parts, placed, lows):
        strips = [low[:, rows * depth :, k : k + LANE] for k in range(0, cols, LANE)]
        side = shift(jnp.concatenate([right] + strips, axis=1), "gx", 1)
        joined += [join(own, low, side, k) for k in range(n)]

    fars = shift(jnp.concatenate([tail for _, _, tail in joined], axis=0), "gy", 2)
    arrived = []
    for at, (_, short, _) in enumerate(joined):
        above = shift(short, "gy", 1)
        below = shift(short, "gy", -1)
        arrived.append((above, below, fars[at : at + 1]))

    outs = ()
    for at in range(chans):
        exact, short, _ = joined[at]
        above, below, far = arrived[at]
        if at:
            above, below, _ = lax.optimization_barrier((above, below, outs[2]))
        column = (far, above, short, below)
        last = jnp.concatenate([a[:, :, -LANE:] for a in column], axis=1)
        first = jnp.concatenate([a[:, :, :LANE] for a in column], axis=1)
        left = shift(last, "gx", 1)
        right = shift(first, "gx", -1)
        group = (exact, above, below, far, left, right)
        outs = deconvolve(at, chans, sides, group, across, within, matrices, outs)
    return tuple(outs)


def solution(mesh):
    in_specs = (P(None, None, "gy", "gx"), P("gy", "gx", None), P())
    out_specs = (P(None, None, "gy", "gx"), P(None, None, "gy", "gx"), P(None, None, "gy", "gx"))
    return jax.shard_map(
        per_device, mesh=mesh, in_specs=in_specs, out_specs=out_specs, check_vma=False
    )
```

```python
import functools

import jax
import jax.numpy as jnp
import ml_dtypes
import numpy as np
from jax import lax
from jax.experimental import pallas as pl
from jax.experimental.pallas import tpu as pltpu
from jax.sharding import PartitionSpec as P

MARGIN = 32
REACH = 15
TAPS = 31
DEPTH = 8
LANE = 128
GAUSS = (1, 4, 6, 4, 1)
TINY = 1e-30
BF16 = jnp.bfloat16
F32 = jnp.float32
MIB = 1 << 20

BEFORE = 66
FRAME = 200
BIG = 34
SMALL = 26


def params(mib):
    return pltpu.CompilerParams(vmem_limit_bytes=mib * MIB)


def cost(flops, nbytes):
    return pl.CostEstimate(flops=int(flops), bytes_accessed=int(nbytes), transcendentals=0)


def dot(a, b):
    return jnp.dot(a, b, preferred_element_type=F32)


def split(value):
    high = value.astype(BF16)
    return high, (value - high.astype(F32)).astype(BF16)


def place_kernel(off_ref, tile_ref, own_ref, right_ref, low_ref, corner_ref, canvas):
    depth, tile_y, tile_x = tile_ref.shape[1:]
    parts = canvas.shape[0]
    wide = parts * LANE
    rows = own_ref.shape[1]
    cols = own_ref.shape[2]
    top = off_ref[0]
    left = off_ref[1]
    canvas[...] = jnp.zeros_like(canvas)
    shift = (
        lax.broadcasted_iota(jnp.int32, (tile_x, wide), 1)
        == lax.broadcasted_iota(jnp.int32, (tile_x, wide), 0) + left
    )
    shift = jnp.where(shift, 1.0, 0.0).astype(BF16)
    for z in range(depth):
        moved = dot(tile_ref[0, z], shift)
        for b in range(parts):
            to = pl.ds(top * depth + z, tile_y, stride=depth)
            canvas[b, to, :] = moved[:, b * LANE : (b + 1) * LANE]
    for b in range(parts - 1):
        to = slice(b * LANE, (b + 1) * LANE)
        own_ref[0, :, to] = canvas[b, :rows, :].astype(BF16)
        low_ref[0, :, to] = canvas[b, rows:, :].astype(BF16)
    right_ref[0] = canvas[parts - 1, :rows, :].astype(BF16)
    half = rows // 2
    upper = canvas[parts - 1, rows : rows + half, :]
    lower = canvas[parts - 1, rows + half :, :]
    corner_ref[0] = (upper + pltpu.roll(lower, LANE // 2, 1)).astype(BF16)


def place(tiles, offsets, begin, n):
    _, depth, tile_y, tile_x = tiles.shape
    rows = (tile_y - MARGIN) * depth
    cols = tile_x - MARGIN
    block = lambda r, c: pl.BlockSpec((1, r, c), lambda i, off: (i, 0, 0))
    shape = lambda r, c: jax.ShapeDtypeStruct((n, r, c), BF16)
    sizes = ((rows, cols), (rows, LANE), (rows, cols), (rows // 2, LANE))
    tile = pl.BlockSpec((1, depth, tile_y, tile_x), lambda i, off: (begin + i, 0, 0, 0))
    return pl.pallas_call(
        place_kernel,
        grid_spec=pltpu.PrefetchScalarGridSpec(
            num_scalar_prefetch=1,
            grid=(n,),
            in_specs=[tile],
            out_specs=[block(*s) for s in sizes],
            scratch_shapes=[pltpu.VMEM((cols // LANE + 1, 2 * rows, LANE), F32)],
        ),
        out_shape=[shape(*s) for s in sizes],
        compiler_params=params(16),
        cost_estimate=cost(n * 2e9, n * 2.5e6),
        name="place",
    )(offsets, tiles)


def join_kernel(own_ref, low_ref, right_ref, corner_ref, exact_ref, first_ref, last_ref):
    rows, cols = own_ref.shape[1:]
    half = rows // 2

    def seen(x):
        return jnp.where(x != 0, 1.0, 0.0)

    own = own_ref[0].astype(F32)
    low = low_ref[0].astype(F32)
    total = own + low
    count = seen(own) + seen(low)
    right = right_ref[0].astype(F32)
    corner = corner_ref[0].astype(F32)
    lane = lax.broadcasted_iota(jnp.int32, (half, LANE), 1)
    inside = lane < LANE // 2
    upper = jnp.where(inside, corner, 0.0)
    lower = jnp.where(inside, pltpu.roll(corner, LANE // 2, 1), 0.0)
    corner = jnp.concatenate([upper, lower], axis=0)
    edge_total = total[:, :LANE] + right + corner
    edge_count = count[:, :LANE] + seen(right) + seen(corner)
    edge = edge_total / edge_count
    rest = total[:, LANE:] / count[:, LANE:]
    exact_ref[0, :, :LANE] = edge
    exact_ref[0, :, LANE:] = rest
    first_ref[0] = edge.astype(BF16)
    last_ref[0] = rest[:, -LANE:].astype(BF16)


def join(own, low, right, corner):
    n, rows, cols = own.shape
    block = lambda r, c: pl.BlockSpec((1, r, c), lambda i: (i, 0, 0))
    sizes = ((rows, cols, F32), (rows, LANE, BF16), (rows, LANE, BF16))
    return pl.pallas_call(
        join_kernel,
        grid=(n,),
        in_specs=[block(*a.shape[1:]) for a in (own, low, right, corner)],
        out_specs=[block(r, c) for r, c, _ in sizes],
        out_shape=[jax.ShapeDtypeStruct((n, r, c), t) for r, c, t in sizes],
        compiler_params=params(16),
        cost_estimate=cost(5e6, 3e6),
        name="join",
    )(own, low, right, corner)


SIDE = 63


def pack_kernel(exact_ref, left_ref, right_ref, out_ref, tail_ref):
    rows, cols = exact_ref.shape[1:]
    lane = lax.broadcasted_iota(jnp.int32, (rows, LANE), 1)
    out_ref[0, :rows, :cols] = exact_ref[0].astype(BF16)
    left = left_ref[0].astype(F32)
    right = right_ref[0].astype(F32)
    out_ref[0, :rows, cols:] = jnp.where(lane < SIDE, right, left).astype(BF16)
    extra = out_ref.shape[1] - rows
    pick = lax.broadcasted_iota(jnp.int32, (extra, LANE), 1) == SIDE - 1
    pick &= lax.broadcasted_iota(jnp.int32, (extra, LANE), 0) == 0
    pick = jnp.where(pick, 1.0, 0.0).astype(BF16)
    column = lax.dot_general(
        pick, left_ref[0], (((1,), (1,)), ((), ())), preferred_element_type=F32
    )
    out_ref[0, rows:, :cols] = column.astype(BF16)
    out_ref[0, rows:, cols:] = jnp.zeros((extra, LANE), BF16)
    tail_ref[0] = out_ref[0, rows - 2 * DEPTH :, :]


def pack(exact, left, right, at):
    _, rows, cols = exact.shape
    block = lambda r, c, k: pl.BlockSpec((1, r, c), lambda i: (k, 0, 0))
    extra = 2 * DEPTH
    sizes = ((rows + extra, cols + LANE), (2 * extra, cols + LANE))
    return pl.pallas_call(
        pack_kernel,
        grid=(1,),
        in_specs=[block(*a.shape[1:], at) for a in (exact, left, right)],
        out_specs=[block(*s, 0) for s in sizes],
        out_shape=[jax.ShapeDtypeStruct((1,) + s, BF16) for s in sizes],
        compiler_params=params(16),
        cost_estimate=cost(1e6, 1e6),
        name="pack",
    )(exact, left, right)


def bands_kernel(kern_ref, across_ref, within_ref):
    which = pl.program_id(0)
    wide = 3 * 2 * LANE
    shape = (16, wide)
    row = lax.broadcasted_iota(jnp.int32, shape, 0)
    lane = lax.broadcasted_iota(jnp.int32, shape, 1)
    tap = row - (lane - 4 * LANE) - (LANE - REACH)
    base = jnp.zeros(shape, F32)
    for k in range(TAPS):
        base = jnp.where(tap == k, kern_ref[which, 2 * TAPS + k], base)

    for q in range(across_ref.shape[1] // 16):
        turned = pltpu.roll(base, (wide - 4 * LANE + 16 * q) % wide, 1)
        across_ref[0, 16 * q : 16 * (q + 1), :] = turned[:, : 2 * LANE].astype(BF16)

    shape = (16, within_ref.shape[2])
    row = lax.broadcasted_iota(jnp.int32, shape, 0)
    lane = lax.broadcasted_iota(jnp.int32, shape, 1)
    tap_y = lane // DEPTH - row // DEPTH
    tap_z = lane % DEPTH - row % DEPTH + REACH
    in_y = jnp.zeros(shape, F32)
    in_z = jnp.zeros(shape, F32)
    for k in range(TAPS):
        in_y = jnp.where(tap_y == k, kern_ref[which, TAPS + k], in_y)
    for k in range(REACH + 1 - DEPTH, REACH + DEPTH):
        in_z = jnp.where(tap_z == k, kern_ref[which, k], in_z)
    both = in_y * in_z

    for q in range(within_ref.shape[1] // 16):
        turned = pltpu.roll(both, 16 * q, 1)
        within_ref[0, 16 * q : 16 * (q + 1), :] = turned.astype(BF16)


def bands(kern):
    count = kern.shape[0]
    shapes = ((4 * LANE, 2 * LANE), (BIG * DEPTH, (BIG + 2 * REACH) * DEPTH))
    return pl.pallas_call(
        bands_kernel,
        grid=(count,),
        in_specs=[pl.BlockSpec(memory_space=pltpu.SMEM)],
        out_specs=[pl.BlockSpec((1,) + s, lambda i: (i, 0, 0)) for s in shapes],
        out_shape=[jax.ShapeDtypeStruct((count,) + s, BF16) for s in shapes],
        compiler_params=params(32),
        cost_estimate=cost(count * 1e6, count * 4e6),
        name="bands",
    )(kern)


@functools.lru_cache(None)
def pyramid_matrices(rows, cols, depth):
    half_x, half_y, half_z = cols // 2, rows // 2, depth // 2
    taps = np.array(GAUSS, np.float32) / 16
    extra_x = (-2, -1, half_x)
    one_x = np.zeros((cols + 2 * LANE, half_x + LANE), np.float32)
    for lane in range(half_x + len(extra_x)):
        x = lane if lane < half_x else extra_x[lane - half_x]
        for k in range(5):
            one_x[LANE + 2 * x + k - 2, lane] = taps[k]
    extra_y = (-2, -1, half_y)
    order = [(z, y) for z in range(half_z) for y in range(half_y)]
    order += [(z, y) for y in extra_y for z in range(half_z)]
    height = -(-len(order) // 16) * 16
    reach_in = (rows + 10) * depth
    one_zy = np.zeros((height, reach_in), np.float32)
    for i, (z, y) in enumerate(order):
        for a in range(5):
            for b in range(5):
                zi = 2 * z + b - 2
                if 0 <= zi < depth:
                    one_zy[i, (2 * y + a - 2 + 6) * depth + zi] = taps[a] * taps[b]
    two_x = np.zeros((half_x + LANE, half_x // 2), np.float32)
    for x in range(half_x // 2):
        for k in range(5):
            source = 2 * x + k - 2
            lane = source if 0 <= source < half_x else half_x + extra_x.index(source)
            two_x[lane, x] = taps[k]
    place_of = {zy: i for i, zy in enumerate(order)}
    two_zy = np.zeros((half_z * half_y // 4, height), np.float32)
    for z in range(half_z // 2):
        for y in range(half_y // 2):
            for a in range(5):
                for b in range(5):
                    at = (2 * z + b - 2, 2 * y + a - 2)
                    if 0 <= at[0] < half_z:
                        two_zy[z * (half_y // 2) + y, place_of[at]] = taps[a] * taps[b]
    return tuple(m.astype(ml_dtypes.bfloat16) for m in (one_x, one_zy, two_x, two_zy))


def deconvolve_kernel(
    sides_ref,
    exact_ref,
    above_ref,
    below_ref,
    far_ref,
    left_ref,
    right_ref,
    across_ref,
    within_ref,
    one_x_ref,
    one_zy_ref,
    two_x_ref,
    two_zy_ref,
    *others,
):
    if len(others) > 11:
        others = others[3:]
    deconvolve_body(
        sides_ref,
        exact_ref,
        above_ref,
        below_ref,
        far_ref,
        left_ref,
        right_ref,
        across_ref,
        within_ref,
        one_x_ref,
        one_zy_ref,
        two_x_ref,
        two_zy_ref,
        *others,
    )


def deconvolve_body(
    sides_ref,
    exact_ref,
    above_ref,
    below_ref,
    far_ref,
    left_ref,
    right_ref,
    across_ref,
    within_ref,
    one_x_ref,
    one_zy_ref,
    two_x_ref,
    two_zy_ref,
    restored_ref,
    level_one_ref,
    level_two_ref,
    joined,
    joined_short,
    ratio,
    estimate,
    estimate_short,
    result,
    high,
    low,
):
    rows8, cols = exact_ref.shape[1:]
    wide = cols + 2 * LANE
    far8 = far_ref.shape[1] // 2
    own = slice(far8 + rows8, far8 + 2 * rows8)
    frame8 = far8 + 3 * rows8
    middle = slice(LANE, LANE + cols)
    after = slice(LANE + cols, wide)

    extra = far8
    lane = lax.broadcasted_iota(jnp.int32, (extra, LANE), 1)
    pick = jnp.where(lane == SIDE - 1, 1.0, 0.0).astype(BF16)

    def unpack(source, count, begin):
        to = slice(begin, begin + count)
        joined_short[to, middle] = source[0, :count, :cols]
        sides = source[0, :count, cols:]
        joined_short[to, after] = sides
        column = lax.dot_general(
            source[0, count:, :cols], pick, (((0,), (0,)), ((), ())), preferred_element_type=F32
        )[rows8 - count :]
        lane = lax.broadcasted_iota(jnp.int32, (count, LANE), 1)
        joined_short[to, :LANE] = jnp.where(lane == SIDE - 1, column, sides.astype(F32)).astype(BF16)

    unpack(far_ref, far8, 0)
    unpack(above_ref, rows8, far8)
    unpack(below_ref, rows8, far8 + 2 * rows8)
    joined_short[own, middle] = exact_ref[0].astype(BF16)
    joined_short[own, :LANE] = left_ref[0]
    joined_short[own, after] = right_ref[0]
    joined_short[frame8:, :] = jnp.zeros_like(joined_short[frame8:, :])
    joined[...] = joined_short[...].astype(F32)
    joined[own, middle] = exact_ref[0]

    blocks = range(wide // (2 * LANE))

    def correlate(source, which, size, start, exact, finish):
        deep = (size + 2 * REACH) * DEPTH
        size8 = size * DEPTH
        matrix = within_ref[0, which, :size8, :deep]
        here = slice(start, start + size8)
        for n in blocks:
            to = slice(2 * LANE * n, 2 * LANE * (n + 1))
            out = dot(matrix, source[start : start + deep, to])
            if exact:
                high[here, to], low[here, to] = split(out)
            else:
                high[here, to] = out.astype(BF16)
        for n in blocks:
            begin = 2 * LANE * n - LANE
            lo, hi = max(begin, 0), min(begin + 4 * LANE, wide)
            band = across_ref[0, which, lo - begin : hi - begin, :]
            out = dot(high[here, lo:hi], band)
            if exact:
                out = out + dot(low[here, lo:hi], band)
            finish(start, size8, slice(2 * LANE * n, 2 * LANE * (n + 1)), out)

    def ratio_from(shift):
        def finish(start, size8, to, out):
            top = joined[start + shift * DEPTH : start + shift * DEPTH + size8, to]
            bottom = jnp.maximum(out, TINY)
            inverse = pl.reciprocal(bottom, approx=True)
            inverse = inverse * (2.0 - bottom * inverse)
            ratio[start : start + size8, to] = (top * inverse).astype(BF16)

        return finish

    def first_estimate(start, size8, to, out):
        at = slice(start, start + size8)
        begin = start + 2 * REACH * DEPTH
        value = joined[begin : begin + size8, to] * out
        estimate[at, to] = value
        estimate_short[at, to] = value.astype(BF16)

    def last_estimate(start, size8, to, out):
        begin = start + 2 * REACH * DEPTH
        value = estimate[begin : begin + size8, to] * out
        for b in range(2):
            result[to.start // LANE + b, start : start + size8, :] = value[:, b * LANE : (b + 1) * LANE]

    for i in range(5):
        correlate(joined_short, 0, BIG, i * BIG * DEPTH, False, ratio_from(REACH))
    for i in range(4):
        correlate(ratio, 1, BIG, i * BIG * DEPTH, i in (1, 2), first_estimate)
    for i in range(4):
        correlate(estimate_short, 0, SMALL, i * SMALL * DEPTH, False, ratio_from(3 * REACH))
    ratio[4 * SMALL * DEPTH : (4 * SMALL + 4) * DEPTH, :] = jnp.zeros((4 * DEPTH, wide), BF16)
    for i in range(3):
        correlate(ratio, 1, SMALL, i * SMALL * DEPTH, True, last_estimate)

    planes = restored_ref.shape[1]
    height = restored_ref.shape[2]
    for z in range(planes):
        at = pl.ds(6 * planes + z, height, stride=planes)
        for b in range(cols // LANE):
            restored_ref[0, z, :, b * LANE : (b + 1) * LANE] = result[1 + b, at, :]

    def twice(left, right):
        big, small = split(right)
        return dot(left, big) + dot(left, small)

    def twice_left(left, right):
        big, small = split(left)
        return dot(big, right) + dot(small, right)

    reach_in = one_zy_ref.shape[1]
    fine = jnp.concatenate([result[b, :reach_in, :] for b in range(wide // LANE)], axis=1)
    one = twice(one_zy_ref[...], dot(fine.astype(BF16), one_x_ref[...]))
    half_z, half_y, half_x = level_one_ref.shape[1:]
    inner = half_z * half_y
    level_one_ref[0] = one[:inner, :half_x].reshape(half_z, half_y, half_x)
    row = lax.broadcasted_iota(jnp.int32, one.shape, 0) - inner
    lane = lax.broadcasted_iota(jnp.int32, one.shape, 1) - half_x
    up, down, left, right = (sides_ref[k] for k in range(4))
    keep_row = jnp.where(row < 0, 1, jnp.where(row < 2 * half_z, up, down))
    keep_lane = jnp.where(lane < 0, 1, jnp.where(lane < 2, left, right))
    one = jnp.where(keep_row * keep_lane > 0, one, 0.0)
    two = twice(two_zy_ref[...], twice_left(one, two_x_ref[...]))
    level_two_ref[0] = two.reshape(level_two_ref.shape[1:])


def deconvolve(at, chans, sides, group, places, across, within, matrices, earlier):
    rows8, cols = group[0].shape[1:]
    rows = rows8 // DEPTH
    wide = cols + 2 * LANE
    one = lambda a, k: pl.BlockSpec((1,) + a.shape[1:], lambda i: (k, 0, 0))
    mine = lambda s: pl.BlockSpec((1,) + s[1:], lambda i: (at,) + (0,) * (len(s) - 1))
    same = lambda a: pl.BlockSpec(a.shape, lambda i: (0,) * a.ndim)
    outs = (
        (chans, DEPTH, rows, cols),
        (chans, DEPTH // 2, rows // 2, cols // 2),
        (chans, DEPTH // 4, rows // 4, cols // 4),
    )
    shapes = [jax.ShapeDtypeStruct(s, F32) for s in outs]
    ratio_rows = 5 * BIG * DEPTH
    estimate_rows = 4 * BIG * DEPTH
    result_rows = 3 * SMALL * DEPTH
    operands = [sides, *group, across, within, *matrices]
    return pl.pallas_call(
        deconvolve_kernel,
        grid=(1,),
        in_specs=[pl.BlockSpec(memory_space=pltpu.SMEM)]
        + [one(a, k) for a, k in zip(group, places)]
        + [mine(across.shape), mine(within.shape)]
        + [same(m) for m in matrices]
        + [pl.BlockSpec(memory_space=pl.ANY) for _ in earlier],
        out_specs=[mine(s) for s in outs],
        out_shape=shapes,
        input_output_aliases={len(operands) + k: k for k in range(len(earlier))},
        scratch_shapes=[
            pltpu.VMEM((FRAME * DEPTH, wide), F32),
            pltpu.VMEM((FRAME * DEPTH, wide), BF16),
            pltpu.VMEM((ratio_rows, wide), BF16),
            pltpu.VMEM((estimate_rows, wide), F32),
            pltpu.VMEM((estimate_rows, wide), BF16),
            pltpu.VMEM((wide // LANE, result_rows, LANE), F32),
            pltpu.VMEM((ratio_rows, wide), BF16),
            pltpu.VMEM((ratio_rows, wide), BF16),
        ],
        compiler_params=params(40),
        cost_estimate=cost(1e6, 1e5),
        name="deconvolve",
    )(*operands, *earlier)


def per_device(tiles, offsets, psf):
    chans, depth, tile_y, tile_x = tiles.shape
    cols = tile_x - MARGIN
    rows = tile_y - MARGIN
    size_x, size_y = lax.axis_size("gx"), lax.axis_size("gy")
    at_x, at_y = lax.axis_index("gx"), lax.axis_index("gy")

    def shift(block, axis, distance):
        devices = range(lax.axis_size(axis))
        route = [(i, i + distance) for i in devices if i + distance in devices]
        return lax.ppermute(block, axis, route)

    def shift_diagonal(block):
        route = [
            (x * size_y + y, (x + 1) * size_y + y + 1)
            for x in range(size_x - 1)
            for y in range(size_y - 1)
        ]
        return lax.ppermute(block, ("gx", "gy"), route)

    sides = jnp.stack([at_y > 0, at_y < size_y - 1, at_x > 0, at_x < size_x - 1])
    sides = sides.astype(jnp.int32)
    matrices = [jnp.asarray(m) for m in pyramid_matrices(rows, cols, depth)]

    parts = ((0, 1), (1, chans - 1))
    sent = []
    for begin, n in parts:
        own, right, low, corner = place(tiles, offsets.reshape(2), begin, n)
        sent.append(
            [own, shift(low, "gy", 1), shift(right, "gx", 1), shift_diagonal(corner)]
        )

    psf, _ = lax.optimization_barrier((psf, sent[0][0]))
    kern = psf / jnp.sum(psf, axis=-1, keepdims=True)
    both = jnp.stack([kern, kern[:, :, ::-1]], axis=1)
    across, within = bands(both.reshape(chans * 2, 3 * TAPS))
    across = across.reshape((chans, 2) + across.shape[1:])
    within = within.reshape((chans, 2) + within.shape[1:])
    sent[0][1], across, within = lax.optimization_barrier((sent[0][1], across, within))

    groups = []
    for (begin, n), pieces in zip(parts, sent):
        exact, first, last = join(*pieces)
        left = shift(last, "gx", 1)
        right = shift(first, "gx", -1)
        for at in range(n):
            message, tail = pack(exact, left, right, at)
            above = shift(message, "gy", 1)
            below = shift(message, "gy", -1)
            groups.append((exact, above, below, tail, left, right, at))
    far = shift(jnp.concatenate([g[3] for g in groups], axis=0), "gy", 2)

    outs = ()
    for at, (exact, above, below, _, left, right, k) in enumerate(groups):
        group = (exact, above, below, far, left, right)
        places = (k, 0, 0, at, k, k)
        outs = deconvolve(at, chans, sides, group, places, across, within, matrices, outs)
    return tuple(outs)


def solution(mesh):
    in_specs = (P(None, None, "gy", "gx"), P("gy", "gx", None), P())
    out_specs = (P(None, None, "gy", "gx"), P(None, None, "gy", "gx"), P(None, None, "gy", "gx"))
    return jax.shard_map(
        per_device, mesh=mesh, in_specs=in_specs, out_specs=out_specs, check_vma=False
    )
```

```python
import functools

import jax
import jax.numpy as jnp
import ml_dtypes
import numpy as np
from jax import lax
from jax.experimental import pallas as pl
from jax.experimental.pallas import tpu as pltpu
from jax.sharding import PartitionSpec as P

MARGIN = 32
REACH = 15
TAPS = 31
DEPTH = 8
LANE = 128
GAUSS = (1, 4, 6, 4, 1)
TINY = 1e-30
BF16 = jnp.bfloat16
F32 = jnp.float32
MIB = 1 << 20

BEFORE = 66
FRAME = 200
BIG = 34
SMALL = 26


def params(mib):
    return pltpu.CompilerParams(vmem_limit_bytes=mib * MIB)


def cost(flops, nbytes):
    return pl.CostEstimate(flops=int(flops), bytes_accessed=int(nbytes), transcendentals=0)


ANY = pl.BlockSpec(memory_space=pl.ANY)


def skipping(kernel, at, count):
    def run(*refs):
        kernel(*refs[:at], *refs[at + count :])

    return run


def dot(a, b):
    return jnp.dot(a, b, preferred_element_type=F32)


def split(value):
    high = value.astype(BF16)
    return high, (value - high.astype(F32)).astype(BF16)


def place_kernel(off_ref, tile_ref, own_ref, right_ref, low_ref, canvas):
    depth, tile_y, tile_x = tile_ref.shape[1:]
    parts = canvas.shape[0]
    wide = parts * LANE
    rows = own_ref.shape[1]
    cols = own_ref.shape[2]
    top = off_ref[0]
    left = off_ref[1]
    canvas[...] = jnp.zeros_like(canvas)
    shift = (
        lax.broadcasted_iota(jnp.int32, (tile_x, wide), 1)
        == lax.broadcasted_iota(jnp.int32, (tile_x, wide), 0) + left
    )
    shift = jnp.where(shift, 1.0, 0.0).astype(BF16)
    for z in range(depth):
        moved = dot(tile_ref[0, z], shift)
        for b in range(parts):
            to = pl.ds(top * depth + z, tile_y, stride=depth)
            canvas[b, to, :] = moved[:, b * LANE : (b + 1) * LANE]
    for b in range(parts - 1):
        to = slice(b * LANE, (b + 1) * LANE)
        own_ref[0, :, to] = canvas[b, :rows, :].astype(BF16)
        low_ref[0, :rows, to] = canvas[b, rows:, :].astype(BF16)
    right_ref[0] = canvas[parts - 1, :rows, :].astype(BF16)
    half = rows // 2
    upper = canvas[parts - 1, rows : rows + half, :]
    lower = canvas[parts - 1, rows + half :, :]
    corner = (upper + pltpu.roll(lower, LANE // 2, 1)).astype(BF16)
    part = half // (parts - 1)
    for b in range(parts - 1):
        low_ref[0, rows:, b * LANE : (b + 1) * LANE] = corner[b * part : (b + 1) * part]


def place(tiles, offsets, begin, n, after):
    _, depth, tile_y, tile_x = tiles.shape
    rows = (tile_y - MARGIN) * depth
    cols = tile_x - MARGIN
    block = lambda r, c: pl.BlockSpec((1, r, c), lambda i, off: (i, 0, 0))
    shape = lambda r, c: jax.ShapeDtypeStruct((n, r, c), BF16)
    extra = rows // 2 * LANE // cols
    sizes = ((rows, cols), (rows, LANE), (rows + extra, cols))
    tile = pl.BlockSpec((1, depth, tile_y, tile_x), lambda i, off: (begin + i, 0, 0, 0))
    return pl.pallas_call(
        skipping(place_kernel, 2, len(after)),
        grid_spec=pltpu.PrefetchScalarGridSpec(
            num_scalar_prefetch=1,
            grid=(n,),
            in_specs=[tile] + [ANY] * len(after),
            out_specs=[block(*s) for s in sizes],
            scratch_shapes=[pltpu.VMEM((cols // LANE + 1, 2 * rows, LANE), F32)],
        ),
        out_shape=[shape(*s) for s in sizes],
        compiler_params=params(16),
        cost_estimate=cost(n * 2e9, 1),
        name="place",
    )(offsets, tiles, *after)


def seen(x):
    return jnp.where(x != 0, 1.0, 0.0)


def lanes(rows):
    return lax.broadcasted_iota(jnp.int32, (rows, LANE), 1)


def edges_kernel(own_ref, right_ref, low_ref, to_right_ref, to_left_ref):
    rows, cols = own_ref.shape[1:]
    half = rows // 2
    packed = low_ref[0, rows:, :].astype(F32)
    corner = jnp.concatenate([packed[:, k : k + LANE] for k in range(0, cols, LANE)], axis=0)
    corner = jnp.concatenate([pltpu.roll(corner, LANE // 2, 1), corner], axis=0)
    right = right_ref[0].astype(F32)
    to_right_ref[0, :rows] = jnp.where(lanes(rows) < LANE // 2, right, corner).astype(BF16)
    own = own_ref[0, :, cols - LANE :].astype(F32)
    low = low_ref[0, :rows, cols - LANE :].astype(F32)
    to_right_ref[0, rows:] = ((own + low) / (seen(own) + seen(low))).astype(BF16)
    to_left_ref[0, :rows] = own_ref[0, :, :LANE]
    to_left_ref[0, rows:] = low_ref[0, :rows, :LANE]


def edges(own, right, low, after):
    n, rows, _ = own.shape
    block = lambda r, c: pl.BlockSpec((1, r, c), lambda i: (i, 0, 0))
    out = (2 * rows, LANE)
    return pl.pallas_call(
        skipping(edges_kernel, 3, len(after)),
        grid=(n,),
        in_specs=[block(*a.shape[1:]) for a in (own, right, low)] + [ANY] * len(after),
        out_specs=[block(*out)] * 2,
        out_shape=[jax.ShapeDtypeStruct((n,) + out, BF16)] * 2,
        compiler_params=params(16),
        cost_estimate=cost(4e10 if own.shape[0] == 1 else 1, 1),
        name="edges",
    )(own, right, low, *after)


SIDE = 63


def join_kernel(
    sides_ref, own_ref, low_ref, mine_ref, left_ref, right_ref, exact_ref, strip_ref, out_ref, tail_ref
):
    rows, cols = own_ref.shape[1:]
    inside = lanes(rows) < LANE // 2

    def parts(ref):
        pair = ref[0, :rows].astype(F32)
        return jnp.where(inside, pair, 0.0), jnp.where(inside, pltpu.roll(pair, LANE // 2, 1), 0.0)

    own = own_ref[0].astype(F32)
    low = low_ref[0].astype(F32)
    total = own + low
    count = seen(own) + seen(low)
    a, b = parts(left_ref)
    edge = (total[:, :LANE] + a + b) / (count[:, :LANE] + seen(a) + seen(b))
    rest = total[:, LANE:] / count[:, LANE:]
    exact_ref[0, :, :LANE] = edge
    exact_ref[0, :, LANE:] = rest
    out_ref[0, :rows, :LANE] = edge.astype(BF16)
    out_ref[0, :rows, LANE:cols] = rest.astype(BF16)

    a, b = parts(mine_ref)
    own = right_ref[0, :rows].astype(F32)
    low = right_ref[0, rows:].astype(F32)
    count = seen(own) + seen(low) + seen(a) + seen(b)
    strip = (own + low + a + b) / jnp.maximum(count, 1.0)
    strip = jnp.where(sides_ref[3] > 0, strip, 0.0)
    strip_ref[0] = strip.astype(BF16)

    left = left_ref[0, rows:]
    out_ref[0, :rows, cols:] = jnp.where(lanes(rows) < SIDE, strip, left.astype(F32)).astype(BF16)
    extra = out_ref.shape[1] - rows
    pick = lanes(extra) == SIDE - 1
    pick &= lax.broadcasted_iota(jnp.int32, (extra, LANE), 0) == 0
    pick = jnp.where(pick, 1.0, 0.0).astype(BF16)
    column = lax.dot_general(pick, left, (((1,), (1,)), ((), ())), preferred_element_type=F32)
    out_ref[0, rows:, :cols] = column.astype(BF16)
    out_ref[0, rows:, cols:] = jnp.zeros((extra, LANE), BF16)
    tail_ref[0] = out_ref[0, rows - 2 * DEPTH :, :]


def join(sides, own, low, mine, left, right, at):
    _, rows, cols = own.shape
    block = lambda r, c, k: pl.BlockSpec((1, r, c), lambda i: (k, 0, 0))
    pair = block(2 * rows, LANE, at)
    extra = 2 * DEPTH
    sizes = (
        (rows, cols, F32),
        (rows, LANE, BF16),
        (rows + extra, cols + LANE, BF16),
        (2 * extra, cols + LANE, BF16),
    )
    return pl.pallas_call(
        join_kernel,
        grid=(1,),
        in_specs=[pl.BlockSpec(memory_space=pltpu.SMEM)]
        + [block(rows, cols, at), block(rows, cols, at), pair, pair, pair],
        out_specs=[block(r, c, 0) for r, c, _ in sizes],
        out_shape=[jax.ShapeDtypeStruct((1, r, c), t) for r, c, t in sizes],
        compiler_params=params(16),
        cost_estimate=cost(1, 1),
        name="join",
    )(sides, own, low, mine, left, right)


def gate(message, after):
    return pl.pallas_call(
        lambda *refs: None,
        in_specs=[ANY] * (1 + len(after)),
        out_specs=ANY,
        out_shape=jax.ShapeDtypeStruct(message.shape, message.dtype),
        input_output_aliases={0: 0},
        cost_estimate=cost(1, 1),
        name="gate",
    )(message, *after)


def bands_kernel(kern_ref, across_ref, within_ref):
    which = pl.program_id(0)
    wide = 3 * 2 * LANE
    shape = (16, wide)
    row = lax.broadcasted_iota(jnp.int32, shape, 0)
    lane = lax.broadcasted_iota(jnp.int32, shape, 1)
    tap = row - (lane - 4 * LANE) - (LANE - REACH)
    base = jnp.zeros(shape, F32)
    for k in range(TAPS):
        base = jnp.where(tap == k, kern_ref[which, 2 * TAPS + k], base)

    for q in range(across_ref.shape[1] // 16):
        turned = pltpu.roll(base, (wide - 4 * LANE + 16 * q) % wide, 1)
        across_ref[0, 16 * q : 16 * (q + 1), :] = turned[:, : 2 * LANE].astype(BF16)

    shape = (16, within_ref.shape[2])
    row = lax.broadcasted_iota(jnp.int32, shape, 0)
    lane = lax.broadcasted_iota(jnp.int32, shape, 1)
    tap_y = lane // DEPTH - row // DEPTH
    tap_z = lane % DEPTH - row % DEPTH + REACH
    in_y = jnp.zeros(shape, F32)
    in_z = jnp.zeros(shape, F32)
    for k in range(TAPS):
        in_y = jnp.where(tap_y == k, kern_ref[which, TAPS + k], in_y)
    for k in range(REACH + 1 - DEPTH, REACH + DEPTH):
        in_z = jnp.where(tap_z == k, kern_ref[which, k], in_z)
    both = in_y * in_z

    for q in range(within_ref.shape[1] // 16):
        turned = pltpu.roll(both, 16 * q, 1)
        within_ref[0, 16 * q : 16 * (q + 1), :] = turned.astype(BF16)


def bands(kern, after):
    count = kern.shape[0]
    shapes = ((4 * LANE, 2 * LANE), (BIG * DEPTH, (BIG + 2 * REACH) * DEPTH))
    return pl.pallas_call(
        skipping(bands_kernel, 1, len(after)),
        grid=(count,),
        in_specs=[pl.BlockSpec(memory_space=pltpu.SMEM)] + [ANY] * len(after),
        out_specs=[pl.BlockSpec((1,) + s, lambda i: (i, 0, 0)) for s in shapes],
        out_shape=[jax.ShapeDtypeStruct((count,) + s, BF16) for s in shapes],
        compiler_params=params(32),
        cost_estimate=cost(2e9, 1),
        name="bands",
    )(kern, *after)


@functools.lru_cache(None)
def pyramid_matrices(rows, cols, depth):
    half_x, half_y, half_z = cols // 2, rows // 2, depth // 2
    taps = np.array(GAUSS, np.float32) / 16
    extra_x = (-2, -1, half_x)
    one_x = np.zeros((cols + 2 * LANE, half_x + LANE), np.float32)
    for lane in range(half_x + len(extra_x)):
        x = lane if lane < half_x else extra_x[lane - half_x]
        for k in range(5):
            one_x[LANE + 2 * x + k - 2, lane] = taps[k]
    extra_y = (-2, -1, half_y)
    order = [(z, y) for z in range(half_z) for y in range(half_y)]
    order += [(z, y) for y in extra_y for z in range(half_z)]
    height = -(-len(order) // 16) * 16
    reach_in = (rows + 10) * depth
    one_zy = np.zeros((height, reach_in), np.float32)
    for i, (z, y) in enumerate(order):
        for a in range(5):
            for b in range(5):
                zi = 2 * z + b - 2
                if 0 <= zi < depth:
                    one_zy[i, (2 * y + a - 2 + 6) * depth + zi] = taps[a] * taps[b]
    two_x = np.zeros((half_x + LANE, half_x // 2), np.float32)
    for x in range(half_x // 2):
        for k in range(5):
            source = 2 * x + k - 2
            lane = source if 0 <= source < half_x else half_x + extra_x.index(source)
            two_x[lane, x] = taps[k]
    place_of = {zy: i for i, zy in enumerate(order)}
    two_zy = np.zeros((half_z * half_y // 4, height), np.float32)
    for z in range(half_z // 2):
        for y in range(half_y // 2):
            for a in range(5):
                for b in range(5):
                    at = (2 * z + b - 2, 2 * y + a - 2)
                    if 0 <= at[0] < half_z:
                        two_zy[z * (half_y // 2) + y, place_of[at]] = taps[a] * taps[b]
    return tuple(m.astype(ml_dtypes.bfloat16) for m in (one_x, one_zy, two_x, two_zy))


def deconvolve_kernel(
    sides_ref,
    exact_ref,
    above_ref,
    below_ref,
    far_ref,
    left_ref,
    right_ref,
    across_ref,
    within_ref,
    one_x_ref,
    one_zy_ref,
    two_x_ref,
    two_zy_ref,
    *others,
):
    if len(others) > 11:
        others = others[3:]
    deconvolve_body(
        sides_ref,
        exact_ref,
        above_ref,
        below_ref,
        far_ref,
        left_ref,
        right_ref,
        across_ref,
        within_ref,
        one_x_ref,
        one_zy_ref,
        two_x_ref,
        two_zy_ref,
        *others,
    )


def deconvolve_body(
    sides_ref,
    exact_ref,
    above_ref,
    below_ref,
    far_ref,
    left_ref,
    right_ref,
    across_ref,
    within_ref,
    one_x_ref,
    one_zy_ref,
    two_x_ref,
    two_zy_ref,
    restored_ref,
    level_one_ref,
    level_two_ref,
    joined,
    joined_short,
    ratio,
    estimate,
    estimate_short,
    result,
    high,
    low,
):
    rows8, cols = exact_ref.shape[1:]
    wide = cols + 2 * LANE
    far8 = far_ref.shape[1] // 2
    own = slice(far8 + rows8, far8 + 2 * rows8)
    frame8 = far8 + 3 * rows8
    middle = slice(LANE, LANE + cols)
    after = slice(LANE + cols, wide)

    extra = far8
    lane = lax.broadcasted_iota(jnp.int32, (extra, LANE), 1)
    pick = jnp.where(lane == SIDE - 1, 1.0, 0.0).astype(BF16)

    def unpack(source, count, begin):
        to = slice(begin, begin + count)
        joined_short[to, middle] = source[0, :count, :cols]
        sides = source[0, :count, cols:]
        joined_short[to, after] = sides
        column = lax.dot_general(
            source[0, count:, :cols], pick, (((0,), (0,)), ((), ())), preferred_element_type=F32
        )[rows8 - count :]
        lane = lax.broadcasted_iota(jnp.int32, (count, LANE), 1)
        joined_short[to, :LANE] = jnp.where(lane == SIDE - 1, column, sides.astype(F32)).astype(BF16)

    unpack(far_ref, far8, 0)
    unpack(above_ref, rows8, far8)
    unpack(below_ref, rows8, far8 + 2 * rows8)
    joined_short[own, middle] = exact_ref[0].astype(BF16)
    joined_short[own, :LANE] = left_ref[0, rows8:]
    joined_short[own, after] = right_ref[0]
    joined_short[frame8:, :] = jnp.zeros_like(joined_short[frame8:, :])
    joined[...] = joined_short[...].astype(F32)
    joined[own, middle] = exact_ref[0]

    blocks = range(wide // (2 * LANE))

    def correlate(source, which, size, start, exact, finish):
        deep = (size + 2 * REACH) * DEPTH
        size8 = size * DEPTH
        matrix = within_ref[0, which, :size8, :deep]
        here = slice(start, start + size8)
        for n in blocks:
            to = slice(2 * LANE * n, 2 * LANE * (n + 1))
            out = dot(matrix, source[start : start + deep, to])
            if exact:
                high[here, to], low[here, to] = split(out)
            else:
                high[here, to] = out.astype(BF16)
        for n in blocks:
            begin = 2 * LANE * n - LANE
            lo, hi = max(begin, 0), min(begin + 4 * LANE, wide)
            band = across_ref[0, which, lo - begin : hi - begin, :]
            out = dot(high[here, lo:hi], band)
            if exact:
                out = out + dot(low[here, lo:hi], band)
            finish(start, size8, slice(2 * LANE * n, 2 * LANE * (n + 1)), out)

    def ratio_from(shift):
        def finish(start, size8, to, out):
            top = joined[start + shift * DEPTH : start + shift * DEPTH + size8, to]
            bottom = jnp.maximum(out, TINY)
            inverse = pl.reciprocal(bottom, approx=True)
            inverse = inverse * (2.0 - bottom * inverse)
            ratio[start : start + size8, to] = (top * inverse).astype(BF16)

        return finish

    def first_estimate(start, size8, to, out):
        at = slice(start, start + size8)
        begin = start + 2 * REACH * DEPTH
        value = joined[begin : begin + size8, to] * out
        estimate[at, to] = value
        estimate_short[at, to] = value.astype(BF16)

    def last_estimate(start, size8, to, out):
        begin = start + 2 * REACH * DEPTH
        value = estimate[begin : begin + size8, to] * out
        for b in range(2):
            result[to.start // LANE + b, start : start + size8, :] = value[:, b * LANE : (b + 1) * LANE]

    for i in range(5):
        correlate(joined_short, 0, BIG, i * BIG * DEPTH, False, ratio_from(REACH))
    for i in range(4):
        correlate(ratio, 1, BIG, i * BIG * DEPTH, i in (1, 2), first_estimate)
    for i in range(4):
        correlate(estimate_short, 0, SMALL, i * SMALL * DEPTH, False, ratio_from(3 * REACH))
    ratio[4 * SMALL * DEPTH : (4 * SMALL + 4) * DEPTH, :] = jnp.zeros((4 * DEPTH, wide), BF16)
    for i in range(3):
        correlate(ratio, 1, SMALL, i * SMALL * DEPTH, True, last_estimate)

    planes = restored_ref.shape[1]
    height = restored_ref.shape[2]
    for z in range(planes):
        at = pl.ds(6 * planes + z, height, stride=planes)
        for b in range(cols // LANE):
            restored_ref[0, z, :, b * LANE : (b + 1) * LANE] = result[1 + b, at, :]

    def twice(left, right):
        big, small = split(right)
        return dot(left, big) + dot(left, small)

    def twice_left(left, right):
        big, small = split(left)
        return dot(big, right) + dot(small, right)

    reach_in = one_zy_ref.shape[1]
    fine = jnp.concatenate([result[b, :reach_in, :] for b in range(wide // LANE)], axis=1)
    one = twice(one_zy_ref[...], dot(fine.astype(BF16), one_x_ref[...]))
    half_z, half_y, half_x = level_one_ref.shape[1:]
    inner = half_z * half_y
    level_one_ref[0] = one[:inner, :half_x].reshape(half_z, half_y, half_x)
    row = lax.broadcasted_iota(jnp.int32, one.shape, 0) - inner
    lane = lax.broadcasted_iota(jnp.int32, one.shape, 1) - half_x
    up, down, left, right = (sides_ref[k] for k in range(4))
    keep_row = jnp.where(row < 0, 1, jnp.where(row < 2 * half_z, up, down))
    keep_lane = jnp.where(lane < 0, 1, jnp.where(lane < 2, left, right))
    one = jnp.where(keep_row * keep_lane > 0, one, 0.0)
    two = twice(two_zy_ref[...], twice_left(one, two_x_ref[...]))
    level_two_ref[0] = two.reshape(level_two_ref.shape[1:])


def deconvolve(at, chans, sides, group, places, across, within, matrices, earlier):
    rows8, cols = group[0].shape[1:]
    rows = rows8 // DEPTH
    wide = cols + 2 * LANE
    one = lambda a, k: pl.BlockSpec((1,) + a.shape[1:], lambda i: (k, 0, 0))
    mine = lambda s: pl.BlockSpec((1,) + s[1:], lambda i: (at,) + (0,) * (len(s) - 1))
    same = lambda a: pl.BlockSpec(a.shape, lambda i: (0,) * a.ndim)
    outs = (
        (chans, DEPTH, rows, cols),
        (chans, DEPTH // 2, rows // 2, cols // 2),
        (chans, DEPTH // 4, rows // 4, cols // 4),
    )
    shapes = [jax.ShapeDtypeStruct(s, F32) for s in outs]
    ratio_rows = 5 * BIG * DEPTH
    estimate_rows = 4 * BIG * DEPTH
    result_rows = 3 * SMALL * DEPTH
    operands = [sides, *group, across, within, *matrices]
    return pl.pallas_call(
        deconvolve_kernel,
        grid=(1,),
        in_specs=[pl.BlockSpec(memory_space=pltpu.SMEM)]
        + [one(a, k) for a, k in zip(group, places)]
        + [mine(across.shape), mine(within.shape)]
        + [same(m) for m in matrices]
        + [pl.BlockSpec(memory_space=pl.ANY) for _ in earlier],
        out_specs=[mine(s) for s in outs],
        out_shape=shapes,
        input_output_aliases={len(operands) + k: k for k in range(len(earlier))},
        scratch_shapes=[
            pltpu.VMEM((FRAME * DEPTH, wide), F32),
            pltpu.VMEM((FRAME * DEPTH, wide), BF16),
            pltpu.VMEM((ratio_rows, wide), BF16),
            pltpu.VMEM((estimate_rows, wide), F32),
            pltpu.VMEM((estimate_rows, wide), BF16),
            pltpu.VMEM((wide // LANE, result_rows, LANE), F32),
            pltpu.VMEM((ratio_rows, wide), BF16),
            pltpu.VMEM((ratio_rows, wide), BF16),
        ],
        compiler_params=params(40),
        cost_estimate=cost(1, 1),
        name="deconvolve",
    )(*operands, *earlier)


def per_device(tiles, offsets, psf):
    chans, depth, tile_y, tile_x = tiles.shape
    cols = tile_x - MARGIN
    rows = tile_y - MARGIN
    size_x, size_y = lax.axis_size("gx"), lax.axis_size("gy")
    at_x, at_y = lax.axis_index("gx"), lax.axis_index("gy")

    def shift(block, axis, distance):
        devices = range(lax.axis_size(axis))
        route = [(i, i + distance) for i in devices if i + distance in devices]
        return lax.ppermute(block, axis, route)

    sides = jnp.stack([at_y > 0, at_y < size_y - 1, at_x > 0, at_x < size_x - 1])
    sides = sides.astype(jnp.int32)
    matrices = [jnp.asarray(m) for m in pyramid_matrices(rows, cols, depth)]

    at_tile = offsets.reshape(2)
    own, right, low = place(tiles, at_tile, 0, 1, ())
    kern = psf / jnp.sum(psf, axis=-1, keepdims=True)
    both = jnp.stack([kern, kern[:, :, ::-1]], axis=1)
    across, within = bands(both.reshape(chans * 2, 3 * TAPS), (right,))
    pieces = [(own, right, shift(low, "gy", 1))]
    own, right, low = place(tiles, at_tile, 1, chans - 1, (within,))
    pieces.append((own, right, shift(low, "gy", 1)))
    across = across.reshape((chans, 2) + across.shape[1:])
    within = within.reshape((chans, 2) + within.shape[1:])

    groups = []
    before = (pieces[1][1],)
    for own, right, low in pieces:
        mine, to_left = edges(own, right, low, before)
        left = shift(mine, "gx", 1)
        right = shift(to_left, "gx", -1)
        joined = [
            join(sides, own, low, mine, left, right, k) for k in range(own.shape[0])
        ]
        before = (joined[0][2],)
        far = jnp.concatenate([tail for *_, tail in joined], axis=0)
        far = shift(far, "gy", 2)
        for k, (exact, strip, message, _) in enumerate(joined):
            if k:
                message = gate(message, (far,))
            above = shift(message, "gy", 1)
            below = shift(message, "gy", -1)
            groups.append(((exact, above, below, far, left, strip), (0, 0, 0, k, k, 0)))

    outs = ()
    for at, (group, places) in enumerate(groups):
        outs = deconvolve(at, chans, sides, group, places, across, within, matrices, outs)
    return tuple(outs)


def solution(mesh):
    in_specs = (P(None, None, "gy", "gx"), P("gy", "gx", None), P())
    out_specs = (P(None, None, "gy", "gx"), P(None, None, "gy", "gx"), P(None, None, "gy", "gx"))
    return jax.shard_map(
        per_device, mesh=mesh, in_specs=in_specs, out_specs=out_specs, check_vma=False
    )
```

```python
import functools

import jax
import jax.numpy as jnp
import ml_dtypes
import numpy as np
from jax import lax
from jax.experimental import pallas as pl
from jax.experimental.pallas import tpu as pltpu
from jax.sharding import PartitionSpec as P

MARGIN = 32
REACH = 15
TAPS = 31
DEPTH = 8
LANE = 128
GAUSS = (1, 4, 6, 4, 1)
TINY = 1e-30
BF16 = jnp.bfloat16
F32 = jnp.float32
MIB = 1 << 20

BEFORE = 66
FRAME = 200
BIG = 34
SMALL = 26


def params(mib):
    return pltpu.CompilerParams(vmem_limit_bytes=mib * MIB)


def cost(flops, nbytes):
    return pl.CostEstimate(flops=int(flops), bytes_accessed=int(nbytes), transcendentals=0)


ANY = pl.BlockSpec(memory_space=pl.ANY)
VMEM = pl.BlockSpec(memory_space=pltpu.VMEM)


def skipping(kernel, at, count):
    def run(*refs):
        kernel(*refs[:at], *refs[at + count :])

    return run


def dot(a, b):
    return jnp.dot(a, b, preferred_element_type=F32)


def split(value):
    high = value.astype(BF16)
    return high, (value - high.astype(F32)).astype(BF16)


def place_kernel(off_ref, tile_ref, own_ref, right_ref, low_ref, canvas):
    depth, tile_y, tile_x = tile_ref.shape[1:]
    parts = canvas.shape[0]
    wide = parts * LANE
    rows = own_ref.shape[1]
    cols = own_ref.shape[2]
    top = off_ref[0]
    left = off_ref[1]
    canvas[...] = jnp.zeros_like(canvas)
    shift = (
        lax.broadcasted_iota(jnp.int32, (tile_x, wide), 1)
        == lax.broadcasted_iota(jnp.int32, (tile_x, wide), 0) + left
    )
    shift = jnp.where(shift, 1.0, 0.0).astype(BF16)
    for z in range(depth):
        moved = dot(tile_ref[0, z], shift)
        for b in range(parts):
            to = pl.ds(top * depth + z, tile_y, stride=depth)
            canvas[b, to, :] = moved[:, b * LANE : (b + 1) * LANE]
    for b in range(parts - 1):
        to = slice(b * LANE, (b + 1) * LANE)
        own_ref[0, :, to] = canvas[b, :rows, :].astype(BF16)
        low_ref[0, :rows, to] = canvas[b, rows:, :].astype(BF16)
    right_ref[0] = canvas[parts - 1, :rows, :].astype(BF16)
    half = rows // 2
    upper = canvas[parts - 1, rows : rows + half, :]
    lower = canvas[parts - 1, rows + half :, :]
    corner = (upper + pltpu.roll(lower, LANE // 2, 1)).astype(BF16)
    part = half // (parts - 1)
    for b in range(parts - 1):
        low_ref[0, rows:, b * LANE : (b + 1) * LANE] = corner[b * part : (b + 1) * part]


def place(tiles, offsets, begin, n, after):
    _, depth, tile_y, tile_x = tiles.shape
    rows = (tile_y - MARGIN) * depth
    cols = tile_x - MARGIN
    block = lambda r, c: pl.BlockSpec((1, r, c), lambda i, off: (i, 0, 0))
    shape = lambda r, c: jax.ShapeDtypeStruct((n, r, c), BF16)
    extra = rows // 2 * LANE // cols
    sizes = ((rows, cols), (rows, LANE), (rows + extra, cols))
    tile = pl.BlockSpec((1, depth, tile_y, tile_x), lambda i, off: (begin + i, 0, 0, 0))
    return pl.pallas_call(
        skipping(place_kernel, 2, len(after)),
        grid_spec=pltpu.PrefetchScalarGridSpec(
            num_scalar_prefetch=1,
            grid=(n,),
            in_specs=[tile] + [ANY] * len(after),
            out_specs=[block(*s) for s in sizes],
            scratch_shapes=[pltpu.VMEM((cols // LANE + 1, 2 * rows, LANE), F32)],
        ),
        out_shape=[shape(*s) for s in sizes],
        compiler_params=params(16),
        cost_estimate=cost(n * 2e9, 1),
        name="place",
    )(offsets, tiles, *after)


def seen(x):
    return jnp.where(x != 0, 1.0, 0.0)


def lanes(rows):
    return lax.broadcasted_iota(jnp.int32, (rows, LANE), 1)


def edges_kernel(own_ref, right_ref, low_ref, to_right_ref, to_left_ref):
    rows, cols = own_ref.shape[1:]
    half = rows // 2
    packed = low_ref[0, rows:, :].astype(F32)
    corner = jnp.concatenate([packed[:, k : k + LANE] for k in range(0, cols, LANE)], axis=0)
    corner = jnp.concatenate([pltpu.roll(corner, LANE // 2, 1), corner], axis=0)
    right = right_ref[0].astype(F32)
    to_right_ref[0, :rows] = jnp.where(lanes(rows) < LANE // 2, right, corner).astype(BF16)
    own = own_ref[0, :, cols - LANE :].astype(F32)
    low = low_ref[0, :rows, cols - LANE :].astype(F32)
    to_right_ref[0, rows:] = ((own + low) / (seen(own) + seen(low))).astype(BF16)
    to_left_ref[0, :rows] = own_ref[0, :, :LANE]
    to_left_ref[0, rows:] = low_ref[0, :rows, :LANE]


def edges(own, right, low, after):
    n, rows, _ = own.shape
    block = lambda r, c: pl.BlockSpec((1, r, c), lambda i: (i, 0, 0))
    out = (2 * rows, LANE)
    return pl.pallas_call(
        skipping(edges_kernel, 3, len(after)),
        grid=(n,),
        in_specs=[block(*a.shape[1:]) for a in (own, right, low)] + [ANY] * len(after),
        out_specs=[block(*out)] * 2,
        out_shape=[jax.ShapeDtypeStruct((n,) + out, BF16)] * 2,
        compiler_params=params(16),
        cost_estimate=cost(4e10 if own.shape[0] == 1 else 1, 1),
        name="edges",
    )(own, right, low, *after)


SIDE = 63


def join_kernel(
    at, sides_ref, own_ref, low_ref, mine_ref, left_ref, right_ref, exact_ref, strip_ref, out_ref, tail_ref
):
    rows, cols = own_ref.shape[1:]
    own_ref, low_ref, mine_ref, left_ref, right_ref = (
        ref.at[at : at + 1] for ref in (own_ref, low_ref, mine_ref, left_ref, right_ref)
    )
    inside = lanes(rows) < LANE // 2

    def parts(ref):
        pair = ref[0, :rows].astype(F32)
        return jnp.where(inside, pair, 0.0), jnp.where(inside, pltpu.roll(pair, LANE // 2, 1), 0.0)

    own = own_ref[0].astype(F32)
    low = low_ref[0, :rows].astype(F32)
    total = own + low
    count = seen(own) + seen(low)
    a, b = parts(left_ref)
    edge = (total[:, :LANE] + a + b) / (count[:, :LANE] + seen(a) + seen(b))
    rest = total[:, LANE:] / count[:, LANE:]
    exact_ref[0, :, :LANE] = edge
    exact_ref[0, :, LANE:] = rest
    out_ref[0, :rows, :LANE] = edge.astype(BF16)
    out_ref[0, :rows, LANE:cols] = rest.astype(BF16)

    a, b = parts(mine_ref)
    own = right_ref[0, :rows].astype(F32)
    low = right_ref[0, rows:].astype(F32)
    count = seen(own) + seen(low) + seen(a) + seen(b)
    strip = (own + low + a + b) / jnp.maximum(count, 1.0)
    strip = jnp.where(sides_ref[3] > 0, strip, 0.0)
    strip_ref[0] = strip.astype(BF16)

    left = left_ref[0, rows:]
    out_ref[0, :rows, cols:] = jnp.where(lanes(rows) < SIDE, strip, left.astype(F32)).astype(BF16)
    extra = out_ref.shape[1] - rows
    pick = lanes(extra) == SIDE - 1
    pick &= lax.broadcasted_iota(jnp.int32, (extra, LANE), 0) == 0
    pick = jnp.where(pick, 1.0, 0.0).astype(BF16)
    column = lax.dot_general(pick, left, (((1,), (1,)), ((), ())), preferred_element_type=F32)
    out_ref[0, rows:, :cols] = column.astype(BF16)
    out_ref[0, rows:, cols:] = jnp.zeros((extra, LANE), BF16)
    tail_ref[0] = out_ref[0, rows - 2 * DEPTH :, :]


def join(sides, own, low, mine, left, right, at):
    _, rows, cols = own.shape
    extra = 2 * DEPTH
    sizes = (
        (rows, cols, F32),
        (rows, LANE, BF16),
        (rows + extra, cols + LANE, BF16),
        (2 * extra, cols + LANE, BF16),
    )
    return pl.pallas_call(
        functools.partial(join_kernel, at),
        in_specs=[pl.BlockSpec(memory_space=pltpu.SMEM)] + [VMEM] * 5,
        out_specs=[VMEM] * 4,
        out_shape=[jax.ShapeDtypeStruct((1, r, c), t) for r, c, t in sizes],
        compiler_params=params(12),
        cost_estimate=cost(1, 1),
        name="join",
    )(sides, own, low, mine, left, right)


def bands_kernel(kern_ref, across_ref, within_ref):
    which = pl.program_id(0)
    wide = 3 * 2 * LANE
    shape = (16, wide)
    row = lax.broadcasted_iota(jnp.int32, shape, 0)
    lane = lax.broadcasted_iota(jnp.int32, shape, 1)
    tap = row - (lane - 4 * LANE) - (LANE - REACH)
    base = jnp.zeros(shape, F32)
    for k in range(TAPS):
        base = jnp.where(tap == k, kern_ref[which, 2 * TAPS + k], base)

    for q in range(across_ref.shape[1] // 16):
        turned = pltpu.roll(base, (wide - 4 * LANE + 16 * q) % wide, 1)
        across_ref[0, 16 * q : 16 * (q + 1), :] = turned[:, : 2 * LANE].astype(BF16)

    shape = (16, within_ref.shape[2])
    row = lax.broadcasted_iota(jnp.int32, shape, 0)
    lane = lax.broadcasted_iota(jnp.int32, shape, 1)
    tap_y = lane // DEPTH - row // DEPTH
    tap_z = lane % DEPTH - row % DEPTH + REACH
    in_y = jnp.zeros(shape, F32)
    in_z = jnp.zeros(shape, F32)
    for k in range(TAPS):
        in_y = jnp.where(tap_y == k, kern_ref[which, TAPS + k], in_y)
    for k in range(REACH + 1 - DEPTH, REACH + DEPTH):
        in_z = jnp.where(tap_z == k, kern_ref[which, k], in_z)
    both = in_y * in_z

    for q in range(within_ref.shape[1] // 16):
        turned = pltpu.roll(both, 16 * q, 1)
        within_ref[0, 16 * q : 16 * (q + 1), :] = turned.astype(BF16)


def bands(kern, after):
    count = kern.shape[0]
    shapes = ((4 * LANE, 2 * LANE), (BIG * DEPTH, (BIG + 2 * REACH) * DEPTH))
    return pl.pallas_call(
        skipping(bands_kernel, 1, len(after)),
        grid=(count,),
        in_specs=[pl.BlockSpec(memory_space=pltpu.SMEM)] + [ANY] * len(after),
        out_specs=[pl.BlockSpec((1,) + s, lambda i: (i, 0, 0)) for s in shapes],
        out_shape=[jax.ShapeDtypeStruct((count,) + s, BF16) for s in shapes],
        compiler_params=params(32),
        cost_estimate=cost(2e9, 1),
        name="bands",
    )(kern, *after)


@functools.lru_cache(None)
def pyramid_matrices(rows, cols, depth):
    half_x, half_y, half_z = cols // 2, rows // 2, depth // 2
    taps = np.array(GAUSS, np.float32) / 16
    extra_x = (-2, -1, half_x)
    one_x = np.zeros((cols + 2 * LANE, half_x + LANE), np.float32)
    for lane in range(half_x + len(extra_x)):
        x = lane if lane < half_x else extra_x[lane - half_x]
        for k in range(5):
            one_x[LANE + 2 * x + k - 2, lane] = taps[k]
    extra_y = (-2, -1, half_y)
    order = [(z, y) for z in range(half_z) for y in range(half_y)]
    order += [(z, y) for y in extra_y for z in range(half_z)]
    height = -(-len(order) // 16) * 16
    reach_in = (rows + 10) * depth
    one_zy = np.zeros((height, reach_in), np.float32)
    for i, (z, y) in enumerate(order):
        for a in range(5):
            for b in range(5):
                zi = 2 * z + b - 2
                if 0 <= zi < depth:
                    one_zy[i, (2 * y + a - 2 + 6) * depth + zi] = taps[a] * taps[b]
    two_x = np.zeros((half_x + LANE, half_x // 2), np.float32)
    for x in range(half_x // 2):
        for k in range(5):
            source = 2 * x + k - 2
            lane = source if 0 <= source < half_x else half_x + extra_x.index(source)
            two_x[lane, x] = taps[k]
    place_of = {zy: i for i, zy in enumerate(order)}
    two_zy = np.zeros((half_z * half_y // 4, height), np.float32)
    for z in range(half_z // 2):
        for y in range(half_y // 2):
            for a in range(5):
                for b in range(5):
                    at = (2 * z + b - 2, 2 * y + a - 2)
                    if 0 <= at[0] < half_z:
                        two_zy[z * (half_y // 2) + y, place_of[at]] = taps[a] * taps[b]
    return tuple(m.astype(ml_dtypes.bfloat16) for m in (one_x, one_zy, two_x, two_zy))


def deconvolve_kernel(
    places,
    sides_ref,
    exact_ref,
    above_ref,
    below_ref,
    far_ref,
    left_ref,
    right_ref,
    across_ref,
    within_ref,
    one_x_ref,
    one_zy_ref,
    two_x_ref,
    two_zy_ref,
    *others,
):
    if len(others) > 11:
        others = others[3:]
    at, k = places
    far_ref = far_ref.at[at : at + 1]
    left_ref = left_ref.at[k : k + 1]
    across_ref = across_ref.at[at : at + 1]
    within_ref = within_ref.at[at : at + 1]
    deconvolve_body(
        sides_ref,
        exact_ref,
        above_ref,
        below_ref,
        far_ref,
        left_ref,
        right_ref,
        across_ref,
        within_ref,
        one_x_ref,
        one_zy_ref,
        two_x_ref,
        two_zy_ref,
        *others,
    )


def deconvolve_body(
    sides_ref,
    exact_ref,
    above_ref,
    below_ref,
    far_ref,
    left_ref,
    right_ref,
    across_ref,
    within_ref,
    one_x_ref,
    one_zy_ref,
    two_x_ref,
    two_zy_ref,
    restored_ref,
    level_one_ref,
    level_two_ref,
    joined,
    joined_short,
    ratio,
    estimate,
    estimate_short,
    result,
    high,
    low,
):
    rows8, cols = exact_ref.shape[1:]
    wide = cols + 2 * LANE
    far8 = far_ref.shape[1] // 2
    own = slice(far8 + rows8, far8 + 2 * rows8)
    frame8 = far8 + 3 * rows8
    middle = slice(LANE, LANE + cols)
    after = slice(LANE + cols, wide)

    extra = far8
    lane = lax.broadcasted_iota(jnp.int32, (extra, LANE), 1)
    pick = jnp.where(lane == SIDE - 1, 1.0, 0.0).astype(BF16)

    def unpack(source, count, begin):
        to = slice(begin, begin + count)
        joined_short[to, middle] = source[0, :count, :cols]
        sides = source[0, :count, cols:]
        joined_short[to, after] = sides
        column = lax.dot_general(
            source[0, count:, :cols], pick, (((0,), (0,)), ((), ())), preferred_element_type=F32
        )[rows8 - count :]
        lane = lax.broadcasted_iota(jnp.int32, (count, LANE), 1)
        joined_short[to, :LANE] = jnp.where(lane == SIDE - 1, column, sides.astype(F32)).astype(BF16)

    unpack(far_ref, far8, 0)
    unpack(above_ref, rows8, far8)
    unpack(below_ref, rows8, far8 + 2 * rows8)
    joined_short[own, middle] = exact_ref[0].astype(BF16)
    joined_short[own, :LANE] = left_ref[0, rows8:]
    joined_short[own, after] = right_ref[0]
    joined_short[frame8:, :] = jnp.zeros_like(joined_short[frame8:, :])
    joined[...] = joined_short[...].astype(F32)
    joined[own, middle] = exact_ref[0]

    blocks = range(wide // (2 * LANE))

    def correlate(source, which, size, start, exact, finish):
        deep = (size + 2 * REACH) * DEPTH
        size8 = size * DEPTH
        matrix = within_ref[0, which, :size8, :deep]
        here = slice(start, start + size8)
        for n in blocks:
            to = slice(2 * LANE * n, 2 * LANE * (n + 1))
            out = dot(matrix, source[start : start + deep, to])
            if exact:
                high[here, to], low[here, to] = split(out)
            else:
                high[here, to] = out.astype(BF16)
        for n in blocks:
            begin = 2 * LANE * n - LANE
            lo, hi = max(begin, 0), min(begin + 4 * LANE, wide)
            band = across_ref[0, which, lo - begin : hi - begin, :]
            out = dot(high[here, lo:hi], band)
            if exact:
                out = out + dot(low[here, lo:hi], band)
            finish(start, size8, slice(2 * LANE * n, 2 * LANE * (n + 1)), out)

    def ratio_from(shift):
        def finish(start, size8, to, out):
            top = joined[start + shift * DEPTH : start + shift * DEPTH + size8, to]
            bottom = jnp.maximum(out, TINY)
            inverse = pl.reciprocal(bottom, approx=True)
            inverse = inverse * (2.0 - bottom * inverse)
            ratio[start : start + size8, to] = (top * inverse).astype(BF16)

        return finish

    def first_estimate(start, size8, to, out):
        at = slice(start, start + size8)
        begin = start + 2 * REACH * DEPTH
        value = joined[begin : begin + size8, to] * out
        estimate[at, to] = value
        estimate_short[at, to] = value.astype(BF16)

    def last_estimate(start, size8, to, out):
        begin = start + 2 * REACH * DEPTH
        value = estimate[begin : begin + size8, to] * out
        for b in range(2):
            result[to.start // LANE + b, start : start + size8, :] = value[:, b * LANE : (b + 1) * LANE]

    for i in range(5):
        correlate(joined_short, 0, BIG, i * BIG * DEPTH, False, ratio_from(REACH))
    for i in range(4):
        correlate(ratio, 1, BIG, i * BIG * DEPTH, i in (1, 2), first_estimate)
    for i in range(4):
        correlate(estimate_short, 0, SMALL, i * SMALL * DEPTH, False, ratio_from(3 * REACH))
    ratio[4 * SMALL * DEPTH : (4 * SMALL + 4) * DEPTH, :] = jnp.zeros((4 * DEPTH, wide), BF16)
    for i in range(3):
        correlate(ratio, 1, SMALL, i * SMALL * DEPTH, True, last_estimate)

    planes = restored_ref.shape[1]
    height = restored_ref.shape[2]
    for z in range(planes):
        at = pl.ds(6 * planes + z, height, stride=planes)
        for b in range(cols // LANE):
            restored_ref[0, z, :, b * LANE : (b + 1) * LANE] = result[1 + b, at, :]

    def twice(left, right):
        big, small = split(right)
        return dot(left, big) + dot(left, small)

    def twice_left(left, right):
        big, small = split(left)
        return dot(big, right) + dot(small, right)

    reach_in = one_zy_ref.shape[1]
    fine = jnp.concatenate([result[b, :reach_in, :] for b in range(wide // LANE)], axis=1)
    one = twice(one_zy_ref[...], dot(fine.astype(BF16), one_x_ref[...]))
    half_z, half_y, half_x = level_one_ref.shape[1:]
    inner = half_z * half_y
    level_one_ref[0] = one[:inner, :half_x].reshape(half_z, half_y, half_x)
    row = lax.broadcasted_iota(jnp.int32, one.shape, 0) - inner
    lane = lax.broadcasted_iota(jnp.int32, one.shape, 1) - half_x
    up, down, left, right = (sides_ref[k] for k in range(4))
    keep_row = jnp.where(row < 0, 1, jnp.where(row < 2 * half_z, up, down))
    keep_lane = jnp.where(lane < 0, 1, jnp.where(lane < 2, left, right))
    one = jnp.where(keep_row * keep_lane > 0, one, 0.0)
    two = twice(two_zy_ref[...], twice_left(one, two_x_ref[...]))
    level_two_ref[0] = two.reshape(level_two_ref.shape[1:])


def deconvolve(at, places, sides, group, across, within, matrices, earlier):
    chans = across.shape[0]
    rows8, cols = group[0].shape[1:]
    rows = rows8 // DEPTH
    wide = cols + 2 * LANE
    mine = lambda s: pl.BlockSpec((1,) + s[1:], lambda i: (at,) + (0,) * (len(s) - 1))
    outs = (
        (chans, DEPTH, rows, cols),
        (chans, DEPTH // 2, rows // 2, cols // 2),
        (chans, DEPTH // 4, rows // 4, cols // 4),
    )
    shapes = [jax.ShapeDtypeStruct(s, F32) for s in outs]
    ratio_rows = 5 * BIG * DEPTH
    estimate_rows = 4 * BIG * DEPTH
    result_rows = 3 * SMALL * DEPTH
    operands = [sides, *group, across, within, *matrices]
    return pl.pallas_call(
        functools.partial(deconvolve_kernel, places),
        grid=(1,),
        in_specs=[pl.BlockSpec(memory_space=pltpu.SMEM)]
        + [VMEM] * (len(operands) - 1)
        + [ANY] * len(earlier),
        out_specs=[mine(s) for s in outs],
        out_shape=shapes,
        input_output_aliases={len(operands) + k: k for k in range(len(earlier))},
        scratch_shapes=[
            pltpu.VMEM((FRAME * DEPTH, wide), F32),
            pltpu.VMEM((FRAME * DEPTH, wide), BF16),
            pltpu.VMEM((ratio_rows, wide), BF16),
            pltpu.VMEM((estimate_rows, wide), F32),
            pltpu.VMEM((estimate_rows, wide), BF16),
            pltpu.VMEM((wide // LANE, result_rows, LANE), F32),
            pltpu.VMEM((ratio_rows, wide), BF16),
            pltpu.VMEM((ratio_rows, wide), BF16),
        ],
        compiler_params=params(32),
        cost_estimate=cost(1e10, 1),
        name="deconvolve",
    )(*operands, *earlier)


def per_device(tiles, offsets, psf):
    chans, depth, tile_y, tile_x = tiles.shape
    cols = tile_x - MARGIN
    rows = tile_y - MARGIN
    size_x, size_y = lax.axis_size("gx"), lax.axis_size("gy")
    at_x, at_y = lax.axis_index("gx"), lax.axis_index("gy")

    def shift(block, axis, distance):
        devices = range(lax.axis_size(axis))
        route = [(i, i + distance) for i in devices if i + distance in devices]
        return lax.ppermute(block, axis, route)

    sides = jnp.stack([at_y > 0, at_y < size_y - 1, at_x > 0, at_x < size_x - 1])
    sides = sides.astype(jnp.int32)
    matrices = [jnp.asarray(m) for m in pyramid_matrices(rows, cols, depth)]

    at_tile = offsets.reshape(2)
    own, right, low = place(tiles, at_tile, 0, 1, ())
    kern = psf / jnp.sum(psf, axis=-1, keepdims=True)
    both = jnp.stack([kern, kern[:, :, ::-1]], axis=1)
    across, within = bands(both.reshape(chans * 2, 3 * TAPS), (right,))
    pieces = [(own, right, shift(low, "gy", 1))]
    own, right, low = place(tiles, at_tile, 1, chans - 1, (within,))
    pieces.append((own, right, shift(low, "gy", 1)))
    across = across.reshape((chans, 2) + across.shape[1:])
    within = within.reshape((chans, 2) + within.shape[1:])

    groups = []
    tails = []
    before = (pieces[1][1],)
    for own, right, low in pieces:
        mine, to_left = edges(own, right, low, before)
        left = shift(mine, "gx", 1)
        right = shift(to_left, "gx", -1)
        for k in range(own.shape[0]):
            exact, strip, message, tail = join(sides, own, low, mine, left, right, k)
            above = shift(message, "gy", 1)
            below = shift(message, "gy", -1)
            groups.append([exact, above, below, left, strip, k])
            tails.append(tail)
        before = (message,)
    far = shift(jnp.concatenate(tails, axis=0), "gy", 2)

    outs = ()
    for at, (exact, above, below, left, strip, k) in enumerate(groups):
        group = (exact, above, below, far, left, strip)
        outs = deconvolve(at, (at, k), sides, group, across, within, matrices, outs)
    return tuple(outs)


def solution(mesh):
    in_specs = (P(None, None, "gy", "gx"), P("gy", "gx", None), P())
    out_specs = (P(None, None, "gy", "gx"), P(None, None, "gy", "gx"), P(None, None, "gy", "gx"))
    return jax.shard_map(
        per_device, mesh=mesh, in_specs=in_specs, out_specs=out_specs, check_vma=False
    )
```

```python
import functools

import jax
import jax.numpy as jnp
import ml_dtypes
import numpy as np
from jax import lax
from jax.experimental import pallas as pl
from jax.experimental.pallas import tpu as pltpu
from jax.sharding import PartitionSpec as P

MARGIN = 32
REACH = 15
TAPS = 31
DEPTH = 8
LANE = 128
GAUSS = (1, 4, 6, 4, 1)
TINY = 1e-30
BF16 = jnp.bfloat16
F32 = jnp.float32
MIB = 1 << 20

BEFORE = 66
FRAME = 200
BIG = 34
SMALL = 26


def params(mib):
    return pltpu.CompilerParams(vmem_limit_bytes=mib * MIB)


def cost(flops, nbytes):
    return pl.CostEstimate(flops=int(flops), bytes_accessed=int(nbytes), transcendentals=0)


ANY = pl.BlockSpec(memory_space=pl.ANY)
VMEM = pl.BlockSpec(memory_space=pltpu.VMEM)


def skipping(kernel, at, count):
    def run(*refs):
        kernel(*refs[:at], *refs[at + count :])

    return run


def dot(a, b):
    return jnp.dot(a, b, preferred_element_type=F32)


def split(value):
    high = value.astype(BF16)
    return high, (value - high.astype(F32)).astype(BF16)


def place_kernel(off_ref, tile_ref, own_ref, right_ref, low_ref, canvas):
    depth, tile_y, tile_x = tile_ref.shape[1:]
    parts = canvas.shape[0]
    wide = parts * LANE
    rows = own_ref.shape[1]
    cols = own_ref.shape[2]
    top = off_ref[0]
    left = off_ref[1]
    canvas[...] = jnp.zeros_like(canvas)
    shift = (
        lax.broadcasted_iota(jnp.int32, (tile_x, wide), 1)
        == lax.broadcasted_iota(jnp.int32, (tile_x, wide), 0) + left
    )
    shift = jnp.where(shift, 1.0, 0.0).astype(BF16)
    for z in range(depth):
        moved = dot(tile_ref[0, z], shift)
        for b in range(parts):
            to = pl.ds(top * depth + z, tile_y, stride=depth)
            canvas[b, to, :] = moved[:, b * LANE : (b + 1) * LANE]
    for b in range(parts - 1):
        to = slice(b * LANE, (b + 1) * LANE)
        own_ref[0, :, to] = canvas[b, :rows, :].astype(BF16)
        low_ref[0, :rows, to] = canvas[b, rows:, :].astype(BF16)
    right_ref[0] = canvas[parts - 1, :rows, :].astype(BF16)
    half = rows // 2
    upper = canvas[parts - 1, rows : rows + half, :]
    lower = canvas[parts - 1, rows + half :, :]
    corner = (upper + pltpu.roll(lower, LANE // 2, 1)).astype(BF16)
    part = half // (parts - 1)
    for b in range(parts - 1):
        low_ref[0, rows:, b * LANE : (b + 1) * LANE] = corner[b * part : (b + 1) * part]


def place(tiles, offsets, begin, n, after):
    _, depth, tile_y, tile_x = tiles.shape
    rows = (tile_y - MARGIN) * depth
    cols = tile_x - MARGIN
    block = lambda r, c: pl.BlockSpec((1, r, c), lambda i, off: (i, 0, 0))
    shape = lambda r, c: jax.ShapeDtypeStruct((n, r, c), BF16)
    extra = rows // 2 * LANE // cols
    sizes = ((rows, cols), (rows, LANE), (rows + extra, cols))
    tile = pl.BlockSpec((1, depth, tile_y, tile_x), lambda i, off: (begin + i, 0, 0, 0))
    return pl.pallas_call(
        skipping(place_kernel, 2, len(after)),
        grid_spec=pltpu.PrefetchScalarGridSpec(
            num_scalar_prefetch=1,
            grid=(n,),
            in_specs=[tile] + [ANY] * len(after),
            out_specs=[block(*s) for s in sizes],
            scratch_shapes=[pltpu.VMEM((cols // LANE + 1, 2 * rows, LANE), F32)],
        ),
        out_shape=[shape(*s) for s in sizes],
        compiler_params=params(16),
        cost_estimate=cost(n * 2e9, 1),
        name="place",
    )(offsets, tiles, *after)


def seen(x):
    return jnp.where(x != 0, 1.0, 0.0)


def lanes(rows):
    return lax.broadcasted_iota(jnp.int32, (rows, LANE), 1)


def edges_kernel(own_ref, right_ref, low_ref, to_right_ref, to_left_ref):
    rows, cols = own_ref.shape[1:]
    half = rows // 2
    packed = low_ref[0, rows:, :].astype(F32)
    corner = jnp.concatenate([packed[:, k : k + LANE] for k in range(0, cols, LANE)], axis=0)
    corner = jnp.concatenate([pltpu.roll(corner, LANE // 2, 1), corner], axis=0)
    right = right_ref[0].astype(F32)
    to_right_ref[0, :rows] = jnp.where(lanes(rows) < LANE // 2, right, corner).astype(BF16)
    own = own_ref[0, :, cols - LANE :].astype(F32)
    low = low_ref[0, :rows, cols - LANE :].astype(F32)
    to_right_ref[0, rows:] = ((own + low) / (seen(own) + seen(low))).astype(BF16)
    own = own_ref[0, :, :LANE].astype(F32)
    low = pltpu.roll(low_ref[0, :rows, :LANE].astype(F32), LANE // 2, 1)
    to_left_ref[0] = jnp.where(lanes(rows) < LANE // 2, own, low).astype(BF16)


def edges(own, right, low, after):
    n, rows, _ = own.shape
    block = lambda r, c: pl.BlockSpec((1, r, c), lambda i: (i, 0, 0))
    outs = ((2 * rows, LANE), (rows, LANE))
    return pl.pallas_call(
        skipping(edges_kernel, 3, len(after)),
        grid=(n,),
        in_specs=[block(*a.shape[1:]) for a in (own, right, low)] + [ANY] * len(after),
        out_specs=[block(*out) for out in outs],
        out_shape=[jax.ShapeDtypeStruct((n,) + out, BF16) for out in outs],
        compiler_params=params(16),
        cost_estimate=cost(4e10 if own.shape[0] == 1 else 1, 1),
        name="edges",
    )(own, right, low, *after)


SIDE = 63


def join_kernel(
    at, sides_ref, own_ref, low_ref, mine_ref, left_ref, right_ref, exact_ref, out_ref, tail_ref
):
    rows, cols = own_ref.shape[1:]
    own_ref, low_ref, mine_ref, left_ref, right_ref = (
        ref.at[at : at + 1] for ref in (own_ref, low_ref, mine_ref, left_ref, right_ref)
    )
    inside = lanes(rows) < LANE // 2

    def parts(ref):
        pair = ref[0, :rows].astype(F32)
        return jnp.where(inside, pair, 0.0), jnp.where(inside, pltpu.roll(pair, LANE // 2, 1), 0.0)

    own = own_ref[0].astype(F32)
    low = low_ref[0, :rows].astype(F32)
    total = own + low
    count = seen(own) + seen(low)
    a, b = parts(left_ref)
    edge = (total[:, :LANE] + a + b) / (count[:, :LANE] + seen(a) + seen(b))
    rest = total[:, LANE:] / count[:, LANE:]
    exact_ref[0, :, :LANE] = edge
    exact_ref[0, :, LANE:] = rest
    out_ref[0, :rows, :LANE] = edge.astype(BF16)
    out_ref[0, :rows, LANE:cols] = rest.astype(BF16)

    a, b = parts(mine_ref)
    own, low = parts(right_ref)
    count = seen(own) + seen(low) + seen(a) + seen(b)
    strip = (own + low + a + b) / jnp.maximum(count, 1.0)
    strip = jnp.where(sides_ref[3] > 0, strip, 0.0)

    left = left_ref[0, rows:]
    out_ref[0, :rows, cols:] = jnp.where(lanes(rows) < SIDE, strip, left.astype(F32)).astype(BF16)
    extra = out_ref.shape[1] - rows
    pick = lanes(extra) == SIDE - 1
    pick &= lax.broadcasted_iota(jnp.int32, (extra, LANE), 0) == 0
    pick = jnp.where(pick, 1.0, 0.0).astype(BF16)
    column = lax.dot_general(pick, left, (((1,), (1,)), ((), ())), preferred_element_type=F32)
    out_ref[0, rows:, :cols] = column.astype(BF16)
    out_ref[0, rows:, cols:] = jnp.zeros((extra, LANE), BF16)
    tail_ref[0] = out_ref[0, rows - 2 * DEPTH :, :]


def join(sides, own, low, mine, left, right, at):
    _, rows, cols = own.shape
    extra = 2 * DEPTH
    sizes = (
        (rows, cols, F32),
        (rows + extra, cols + LANE, BF16),
        (2 * extra, cols + LANE, BF16),
    )
    return pl.pallas_call(
        functools.partial(join_kernel, at),
        in_specs=[pl.BlockSpec(memory_space=pltpu.SMEM)] + [VMEM] * 5,
        out_specs=[VMEM] * 3,
        out_shape=[jax.ShapeDtypeStruct((1, r, c), t) for r, c, t in sizes],
        compiler_params=params(12),
        cost_estimate=cost(1, 1),
        name="join",
    )(sides, own, low, mine, left, right)


def bands_kernel(kern_ref, across_ref, within_ref, corner_ref):
    which = pl.program_id(0)
    wide = 3 * 2 * LANE
    shape = (16, wide)
    row = lax.broadcasted_iota(jnp.int32, shape, 0)
    lane = lax.broadcasted_iota(jnp.int32, shape, 1)
    tap = row - (lane - 4 * LANE) - (LANE - REACH)
    base = jnp.zeros(shape, F32)
    for k in range(TAPS):
        base = jnp.where(tap == k, kern_ref[which, 2 * TAPS + k], base)

    for q in range(across_ref.shape[1] // 16):
        turned = pltpu.roll(base, (wide - 4 * LANE + 16 * q) % wide, 1)
        across_ref[0, 16 * q : 16 * (q + 1), :] = turned[:, : 2 * LANE].astype(BF16)

    at, to = 3 * LANE - LANE - (LANE - SIDE) - 1, LANE - (BEFORE - REACH)
    row = lax.broadcasted_iota(jnp.int32, (3 * LANE, LANE), 0)
    lane = lanes(3 * LANE)
    band = across_ref[0, : 3 * LANE, :LANE].astype(F32)
    corner_ref[0, : 3 * LANE] = jnp.where((row == at) & (lane == to), 0.0, band).astype(BF16)
    row = lax.broadcasted_iota(jnp.int32, (LANE, LANE), 0)
    lone = (row == SIDE - 1) & (lanes(LANE) == to)
    corner_ref[0, 3 * LANE :] = jnp.where(lone, kern_ref[which, 2 * TAPS], 0.0).astype(BF16)

    shape = (16, within_ref.shape[2])
    row = lax.broadcasted_iota(jnp.int32, shape, 0)
    lane = lax.broadcasted_iota(jnp.int32, shape, 1)
    tap_y = lane // DEPTH - row // DEPTH
    tap_z = lane % DEPTH - row % DEPTH + REACH
    in_y = jnp.zeros(shape, F32)
    in_z = jnp.zeros(shape, F32)
    for k in range(TAPS):
        in_y = jnp.where(tap_y == k, kern_ref[which, TAPS + k], in_y)
    for k in range(REACH + 1 - DEPTH, REACH + DEPTH):
        in_z = jnp.where(tap_z == k, kern_ref[which, k], in_z)
    both = in_y * in_z

    for q in range(within_ref.shape[1] // 16):
        turned = pltpu.roll(both, 16 * q, 1)
        within_ref[0, 16 * q : 16 * (q + 1), :] = turned.astype(BF16)


def bands(kern, after):
    count = kern.shape[0]
    shapes = (
        (4 * LANE, 2 * LANE),
        (BIG * DEPTH, (BIG + 2 * REACH) * DEPTH),
        (4 * LANE, LANE),
    )
    return pl.pallas_call(
        skipping(bands_kernel, 1, len(after)),
        grid=(count,),
        in_specs=[pl.BlockSpec(memory_space=pltpu.SMEM)] + [ANY] * len(after),
        out_specs=[pl.BlockSpec((1,) + s, lambda i: (i, 0, 0)) for s in shapes],
        out_shape=[jax.ShapeDtypeStruct((count,) + s, BF16) for s in shapes],
        compiler_params=params(32),
        cost_estimate=cost(2e9, 1),
        name="bands",
    )(kern, *after)


@functools.lru_cache(None)
def pyramid_matrices(rows, cols, depth):
    half_x, half_y, half_z = cols // 2, rows // 2, depth // 2
    taps = np.array(GAUSS, np.float32) / 16
    extra_x = (-2, -1, half_x)
    one_x = np.zeros((cols + LANE, half_x + LANE), np.float32)
    for lane in range(half_x + len(extra_x)):
        x = lane if lane < half_x else extra_x[lane - half_x]
        for k in range(5):
            one_x[(2 * x + k - 2) % (cols + LANE), lane] = taps[k]
    extra_y = (-2, -1, half_y)
    order = [(z, y) for z in range(half_z) for y in range(half_y)]
    order += [(z, y) for y in extra_y for z in range(half_z)]
    height = -(-len(order) // 16) * 16
    reach_in = (rows + 10) * depth
    one_zy = np.zeros((height, reach_in), np.float32)
    for i, (z, y) in enumerate(order):
        for a in range(5):
            for b in range(5):
                zi = 2 * z + b - 2
                if 0 <= zi < depth:
                    one_zy[i, (2 * y + a - 2 + 6) * depth + zi] = taps[a] * taps[b]
    two_x = np.zeros((half_x + LANE, half_x // 2), np.float32)
    for x in range(half_x // 2):
        for k in range(5):
            source = 2 * x + k - 2
            lane = source if 0 <= source < half_x else half_x + extra_x.index(source)
            two_x[lane, x] = taps[k]
    place_of = {zy: i for i, zy in enumerate(order)}
    two_zy = np.zeros((half_z * half_y // 4, height), np.float32)
    for z in range(half_z // 2):
        for y in range(half_y // 2):
            for a in range(5):
                for b in range(5):
                    at = (2 * z + b - 2, 2 * y + a - 2)
                    if 0 <= at[0] < half_z:
                        two_zy[z * (half_y // 2) + y, place_of[at]] = taps[a] * taps[b]
    return tuple(m.astype(ml_dtypes.bfloat16) for m in (one_x, one_zy, two_x, two_zy))


def deconvolve_kernel(
    at,
    sides_ref,
    exact_ref,
    message_ref,
    above_ref,
    below_ref,
    far_ref,
    across_ref,
    within_ref,
    corner_ref,
    one_x_ref,
    one_zy_ref,
    two_x_ref,
    two_zy_ref,
    *others,
):
    if len(others) > 11:
        others = others[3:]
    far_ref = far_ref.at[at : at + 1]
    corner_ref = corner_ref.at[at : at + 1]
    across_ref = across_ref.at[at : at + 1]
    within_ref = within_ref.at[at : at + 1]
    deconvolve_body(
        sides_ref,
        exact_ref,
        message_ref,
        above_ref,
        below_ref,
        far_ref,
        across_ref,
        within_ref,
        corner_ref,
        one_x_ref,
        one_zy_ref,
        two_x_ref,
        two_zy_ref,
        *others,
    )


def deconvolve_body(
    sides_ref,
    exact_ref,
    message_ref,
    above_ref,
    below_ref,
    far_ref,
    across_ref,
    within_ref,
    corner_ref,
    one_x_ref,
    one_zy_ref,
    two_x_ref,
    two_zy_ref,
    restored_ref,
    level_one_ref,
    level_two_ref,
    joined,
    joined_short,
    ratio,
    estimate,
    estimate_short,
    result,
    high,
    low,
):
    rows8, cols = exact_ref.shape[1:]
    wide = cols + LANE
    far8 = far_ref.shape[1] // 2
    frame8 = far8 + 3 * rows8

    pick = jnp.where(lanes(far8) == SIDE - 1, 1.0, 0.0).astype(BF16)

    def unpack(source, count, begin):
        to = slice(begin, begin + count)
        joined_short[to, :wide] = source[0, :count, :]
        column = lax.dot_general(
            source[0, count:, :cols], pick, (((0,), (0,)), ((), ())), preferred_element_type=F32
        )
        joined_short[to, wide:] = column[rows8 - count :].astype(BF16)

    unpack(far_ref, far8, 0)
    unpack(above_ref, rows8, far8)
    unpack(message_ref, rows8, far8 + rows8)
    unpack(below_ref, rows8, far8 + 2 * rows8)
    joined_short[frame8:, :] = jnp.zeros_like(joined_short[frame8:, :])
    joined[...] = joined_short[:, :wide].astype(F32)
    joined[far8 + rows8 : far8 + 2 * rows8, :cols] = exact_ref[0]

    blocks = [slice(k, min(k + 2 * LANE, wide)) for k in range(0, wide, 2 * LANE)]

    def window(ref, here, to, lone):
        begin, end = to.start - LANE, to.stop + LANE
        if begin < 0:
            pieces = [ref[here, begin + wide : wide], ref[here, :end]]
        elif end > wide:
            pieces = [ref[here, begin:wide], ref[here, : end - wide]]
        else:
            return ref[here, begin:end]
        if lone and to.stop == wide:
            pieces.append(ref[here, wide:])
        return jnp.concatenate(pieces, axis=1)

    def correlate(source, which, size, start, exact, finish, lone=False):
        deep = (size + 2 * REACH) * DEPTH
        size8 = size * DEPTH
        matrix = within_ref[0, which, :size8, :deep]
        here = slice(start, start + size8)
        for to in blocks:
            if lone and to.stop == wide:
                to = slice(to.start, wide + LANE)
            out = dot(matrix, source[start : start + deep, to])
            if exact:
                high[here, to], low[here, to] = split(out)
            else:
                high[here, to] = out.astype(BF16)
        for to in blocks:
            width = to.stop - to.start
            if lone and to.stop == wide:
                band = corner_ref[0, which]
            else:
                band = across_ref[0, which, : width + 2 * LANE, :width]
            out = dot(window(high, here, to, lone), band)
            if exact:
                out = out + dot(window(low, here, to, False), band)
            finish(start, size8, to, out)

    def ratio_from(shift):
        def finish(start, size8, to, out):
            top = joined[start + shift * DEPTH : start + shift * DEPTH + size8, to]
            bottom = jnp.maximum(out, TINY)
            inverse = pl.reciprocal(bottom, approx=True)
            inverse = inverse * (2.0 - bottom * inverse)
            ratio[start : start + size8, to] = (top * inverse).astype(BF16)

        return finish

    def first_estimate(start, size8, to, out):
        at = slice(start, start + size8)
        begin = start + 2 * REACH * DEPTH
        value = joined[begin : begin + size8, to] * out
        estimate[at, to] = value
        estimate_short[at, to] = value.astype(BF16)

    def last_estimate(start, size8, to, out):
        begin = start + 2 * REACH * DEPTH
        value = estimate[begin : begin + size8, to] * out
        for b in range((to.stop - to.start) // LANE):
            result[to.start // LANE + b, start : start + size8, :] = value[:, b * LANE : (b + 1) * LANE]

    for i in range(5):
        correlate(joined_short, 0, BIG, i * BIG * DEPTH, False, ratio_from(REACH), True)
    for i in range(4):
        correlate(ratio, 1, BIG, i * BIG * DEPTH, i in (1, 2), first_estimate)
    for i in range(4):
        correlate(estimate_short, 0, SMALL, i * SMALL * DEPTH, False, ratio_from(3 * REACH))
    ratio[4 * SMALL * DEPTH : (4 * SMALL + 4) * DEPTH, :] = jnp.zeros((4 * DEPTH, wide), BF16)
    for i in range(3):
        correlate(ratio, 1, SMALL, i * SMALL * DEPTH, True, last_estimate)

    planes = restored_ref.shape[1]
    height = restored_ref.shape[2]
    for z in range(planes):
        at = pl.ds(6 * planes + z, height, stride=planes)
        for b in range(cols // LANE):
            restored_ref[0, z, :, b * LANE : (b + 1) * LANE] = result[b, at, :]

    def twice(left, right):
        big, small = split(right)
        return dot(left, big) + dot(left, small)

    def twice_left(left, right):
        big, small = split(left)
        return dot(big, right) + dot(small, right)

    reach_in = one_zy_ref.shape[1]
    fine = jnp.concatenate([result[b, :reach_in, :] for b in range(wide // LANE)], axis=1)
    one = twice(one_zy_ref[...], dot(fine.astype(BF16), one_x_ref[...]))
    half_z, half_y, half_x = level_one_ref.shape[1:]
    inner = half_z * half_y
    level_one_ref[0] = one[:inner, :half_x].reshape(half_z, half_y, half_x)
    row = lax.broadcasted_iota(jnp.int32, one.shape, 0) - inner
    lane = lax.broadcasted_iota(jnp.int32, one.shape, 1) - half_x
    up, down, left, right = (sides_ref[k] for k in range(4))
    keep_row = jnp.where(row < 0, 1, jnp.where(row < 2 * half_z, up, down))
    keep_lane = jnp.where(lane < 0, 1, jnp.where(lane < 2, left, right))
    one = jnp.where(keep_row * keep_lane > 0, one, 0.0)
    two = twice(two_zy_ref[...], twice_left(one, two_x_ref[...]))
    level_two_ref[0] = two.reshape(level_two_ref.shape[1:])


def deconvolve(at, sides, group, tables, matrices, earlier):
    chans = tables[0].shape[0]
    rows8, cols = group[0].shape[1:]
    rows = rows8 // DEPTH
    wide = cols + LANE
    mine = lambda s: pl.BlockSpec((1,) + s[1:], lambda i: (at,) + (0,) * (len(s) - 1))
    outs = (
        (chans, DEPTH, rows, cols),
        (chans, DEPTH // 2, rows // 2, cols // 2),
        (chans, DEPTH // 4, rows // 4, cols // 4),
    )
    shapes = [jax.ShapeDtypeStruct(s, F32) for s in outs]
    ratio_rows = 5 * BIG * DEPTH
    estimate_rows = 4 * BIG * DEPTH
    result_rows = 3 * SMALL * DEPTH
    operands = [sides, *group, *tables, *matrices]
    return pl.pallas_call(
        functools.partial(deconvolve_kernel, at),
        grid=(1,),
        in_specs=[pl.BlockSpec(memory_space=pltpu.SMEM)]
        + [VMEM] * (len(operands) - 1)
        + [ANY] * len(earlier),
        out_specs=[mine(s) for s in outs],
        out_shape=shapes,
        input_output_aliases={len(operands) + k: k for k in range(len(earlier))},
        scratch_shapes=[
            pltpu.VMEM((FRAME * DEPTH, wide), F32),
            pltpu.VMEM((FRAME * DEPTH, wide + LANE), BF16),
            pltpu.VMEM((ratio_rows, wide), BF16),
            pltpu.VMEM((estimate_rows, wide), F32),
            pltpu.VMEM((estimate_rows, wide), BF16),
            pltpu.VMEM((wide // LANE, result_rows, LANE), F32),
            pltpu.VMEM((ratio_rows, wide + LANE), BF16),
            pltpu.VMEM((ratio_rows, wide), BF16),
        ],
        compiler_params=params(32),
        cost_estimate=cost(1e10, 1),
        name="deconvolve",
    )(*operands, *earlier)


def per_device(tiles, offsets, psf):
    chans, depth, tile_y, tile_x = tiles.shape
    cols = tile_x - MARGIN
    rows = tile_y - MARGIN
    size_x, size_y = lax.axis_size("gx"), lax.axis_size("gy")
    at_x, at_y = lax.axis_index("gx"), lax.axis_index("gy")

    def shift(block, axis, distance):
        devices = range(lax.axis_size(axis))
        route = [(i, i + distance) for i in devices if i + distance in devices]
        return lax.ppermute(block, axis, route)

    sides = jnp.stack([at_y > 0, at_y < size_y - 1, at_x > 0, at_x < size_x - 1])
    sides = sides.astype(jnp.int32)
    matrices = [jnp.asarray(m) for m in pyramid_matrices(rows, cols, depth)]

    at_tile = offsets.reshape(2)
    own, right, low = place(tiles, at_tile, 0, 1, ())
    kern = psf / jnp.sum(psf, axis=-1, keepdims=True)
    both = jnp.stack([kern, kern[:, :, ::-1]], axis=1)
    tables = bands(both.reshape(chans * 2, 3 * TAPS), (right,))
    pieces = [(own, right, shift(low, "gy", 1))]
    own, right, low = place(tiles, at_tile, 1, chans - 1, (tables[1],))
    pieces.append((own, right, shift(low, "gy", 1)))
    tables = [t.reshape((chans, 2) + t.shape[1:]) for t in tables]

    groups = []
    tails = []
    before = (pieces[1][1],)
    for own, right, low in pieces:
        mine, to_left = edges(own, right, low, before)
        left = shift(mine, "gx", 1)
        right = shift(to_left, "gx", -1)
        for k in range(own.shape[0]):
            exact, message, tail = join(sides, own, low, mine, left, right, k)
            above = shift(message, "gy", 1)
            below = shift(message, "gy", -1)
            groups.append([exact, message, above, below])
            tails.append(tail)
        before = (message,)
    far = shift(jnp.concatenate(tails, axis=0), "gy", 2)

    outs = ()
    for at, group in enumerate(groups):
        outs = deconvolve(at, sides, [*group, far], tables, matrices, outs)
    return tuple(outs)


def solution(mesh):
    in_specs = (P(None, None, "gy", "gx"), P("gy", "gx", None), P())
    out_specs = (P(None, None, "gy", "gx"), P(None, None, "gy", "gx"), P(None, None, "gy", "gx"))
    return jax.shard_map(
        per_device, mesh=mesh, in_specs=in_specs, out_specs=out_specs, check_vma=False
    )
```

```python
import functools

import jax
import jax.numpy as jnp
import ml_dtypes
import numpy as np
from jax import lax
from jax.experimental import pallas as pl
from jax.experimental.pallas import tpu as pltpu
from jax.sharding import PartitionSpec as P

MARGIN = 32
REACH = 15
TAPS = 31
DEPTH = 8
LANE = 128
GAUSS = (1, 4, 6, 4, 1)
TINY = 1e-30
BF16 = jnp.bfloat16
F32 = jnp.float32
MIB = 1 << 20

BEFORE = 66
FRAME = 200
BIG = 34
SMALL = 26


def params(mib):
    return pltpu.CompilerParams(vmem_limit_bytes=mib * MIB)


def cost(flops, nbytes):
    return pl.CostEstimate(flops=int(flops), bytes_accessed=int(nbytes), transcendentals=0)


ANY = pl.BlockSpec(memory_space=pl.ANY)
VMEM = pl.BlockSpec(memory_space=pltpu.VMEM)


def skipping(kernel, at, count):
    def run(*refs):
        kernel(*refs[:at], *refs[at + count :])

    return run


def dot(a, b):
    return jnp.dot(a, b, preferred_element_type=F32)


def split(value):
    high = value.astype(BF16)
    return high, (value - high.astype(F32)).astype(BF16)


def place_kernel(off_ref, tile_ref, own_ref, right_ref, low_ref, canvas):
    depth, tile_y, tile_x = tile_ref.shape[1:]
    parts = canvas.shape[0]
    wide = parts * LANE
    rows = own_ref.shape[1]
    cols = own_ref.shape[2]
    top = off_ref[0]
    left = off_ref[1]
    canvas[...] = jnp.zeros_like(canvas)
    shift = (
        lax.broadcasted_iota(jnp.int32, (tile_x, wide), 1)
        == lax.broadcasted_iota(jnp.int32, (tile_x, wide), 0) + left
    )
    shift = jnp.where(shift, 1.0, 0.0).astype(BF16)
    for z in range(depth):
        moved = dot(tile_ref[0, z], shift)
        for b in range(parts):
            to = pl.ds(top * depth + z, tile_y, stride=depth)
            canvas[b, to, :] = moved[:, b * LANE : (b + 1) * LANE]
    for b in range(parts - 1):
        to = slice(b * LANE, (b + 1) * LANE)
        own_ref[0, :, to] = canvas[b, :rows, :].astype(BF16)
        low_ref[0, :rows, to] = canvas[b, rows:, :].astype(BF16)
    right_ref[0] = canvas[parts - 1, :rows, :].astype(BF16)
    half = rows // 2
    upper = canvas[parts - 1, rows : rows + half, :]
    lower = canvas[parts - 1, rows + half :, :]
    corner = (upper + pltpu.roll(lower, LANE // 2, 1)).astype(BF16)
    part = half // (parts - 1)
    for b in range(parts - 1):
        low_ref[0, rows:, b * LANE : (b + 1) * LANE] = corner[b * part : (b + 1) * part]


def place(tiles, offsets, begin, n, after):
    _, depth, tile_y, tile_x = tiles.shape
    rows = (tile_y - MARGIN) * depth
    cols = tile_x - MARGIN
    block = lambda r, c: pl.BlockSpec((1, r, c), lambda i, off: (i, 0, 0))
    shape = lambda r, c: jax.ShapeDtypeStruct((n, r, c), BF16)
    extra = rows // 2 * LANE // cols
    sizes = ((rows, cols), (rows, LANE), (rows + extra, cols))
    tile = pl.BlockSpec((1, depth, tile_y, tile_x), lambda i, off: (begin + i, 0, 0, 0))
    return pl.pallas_call(
        skipping(place_kernel, 2, len(after)),
        grid_spec=pltpu.PrefetchScalarGridSpec(
            num_scalar_prefetch=1,
            grid=(n,),
            in_specs=[tile] + [ANY] * len(after),
            out_specs=[block(*s) for s in sizes],
            scratch_shapes=[pltpu.VMEM((cols // LANE + 1, 2 * rows, LANE), F32)],
        ),
        out_shape=[shape(*s) for s in sizes],
        compiler_params=params(16),
        cost_estimate=cost(n * 2e9, 1),
        name="place",
    )(offsets, tiles, *after)


def seen(x):
    return jnp.where(x != 0, 1.0, 0.0)


def lanes(rows):
    return lax.broadcasted_iota(jnp.int32, (rows, LANE), 1)


def edges_kernel(own_ref, right_ref, low_ref, to_right_ref, to_left_ref):
    rows, cols = own_ref.shape[1:]
    half = rows // 2
    packed = low_ref[0, rows:, :].astype(F32)
    corner = jnp.concatenate([packed[:, k : k + LANE] for k in range(0, cols, LANE)], axis=0)
    corner = jnp.concatenate([pltpu.roll(corner, LANE // 2, 1), corner], axis=0)
    right = right_ref[0].astype(F32)
    to_right_ref[0, :rows] = jnp.where(lanes(rows) < LANE // 2, right, corner).astype(BF16)
    own = own_ref[0, :, cols - LANE :].astype(F32)
    low = low_ref[0, :rows, cols - LANE :].astype(F32)
    to_right_ref[0, rows:] = ((own + low) / (seen(own) + seen(low))).astype(BF16)
    own = own_ref[0, :, :LANE].astype(F32)
    low = pltpu.roll(low_ref[0, :rows, :LANE].astype(F32), LANE // 2, 1)
    to_left_ref[0] = jnp.where(lanes(rows) < LANE // 2, own, low).astype(BF16)


def edges(own, right, low, after):
    n, rows, _ = own.shape
    block = lambda r, c: pl.BlockSpec((1, r, c), lambda i: (i, 0, 0))
    outs = ((2 * rows, LANE), (rows, LANE))
    return pl.pallas_call(
        skipping(edges_kernel, 3, len(after)),
        grid=(n,),
        in_specs=[block(*a.shape[1:]) for a in (own, right, low)] + [ANY] * len(after),
        out_specs=[block(*out) for out in outs],
        out_shape=[jax.ShapeDtypeStruct((n,) + out, BF16) for out in outs],
        compiler_params=params(16),
        cost_estimate=cost(4e10 if own.shape[0] == 1 else 1, 1),
        name="edges",
    )(own, right, low, *after)


SIDE = 63


def join_kernel(
    at, sides_ref, own_ref, low_ref, mine_ref, left_ref, right_ref, exact_ref, out_ref, tail_ref
):
    rows, cols = own_ref.shape[1:]
    own_ref, low_ref, mine_ref, left_ref, right_ref = (
        ref.at[at : at + 1] for ref in (own_ref, low_ref, mine_ref, left_ref, right_ref)
    )
    inside = lanes(rows) < LANE // 2

    def parts(ref):
        pair = ref[0, :rows].astype(F32)
        return jnp.where(inside, pair, 0.0), jnp.where(inside, pltpu.roll(pair, LANE // 2, 1), 0.0)

    own = own_ref[0].astype(F32)
    low = low_ref[0, :rows].astype(F32)
    total = own + low
    count = seen(own) + seen(low)
    a, b = parts(left_ref)
    edge = (total[:, :LANE] + a + b) / (count[:, :LANE] + seen(a) + seen(b))
    rest = total[:, LANE:] / count[:, LANE:]
    exact_ref[0, :, :LANE] = edge
    exact_ref[0, :, LANE:] = rest
    out_ref[0, :rows, :LANE] = edge.astype(BF16)
    out_ref[0, :rows, LANE:cols] = rest.astype(BF16)

    a, b = parts(mine_ref)
    own, low = parts(right_ref)
    count = seen(own) + seen(low) + seen(a) + seen(b)
    strip = (own + low + a + b) / jnp.maximum(count, 1.0)
    strip = jnp.where(sides_ref[3] > 0, strip, 0.0)

    left = left_ref[0, rows:]
    out_ref[0, :rows, cols:] = jnp.where(lanes(rows) < SIDE, strip, left.astype(F32)).astype(BF16)
    extra = out_ref.shape[1] - rows
    pick = lanes(extra) == SIDE - 1
    pick &= lax.broadcasted_iota(jnp.int32, (extra, LANE), 0) == 0
    pick = jnp.where(pick, 1.0, 0.0).astype(BF16)
    column = lax.dot_general(pick, left, (((1,), (1,)), ((), ())), preferred_element_type=F32)
    out_ref[0, rows:, :cols] = column.astype(BF16)
    out_ref[0, rows:, cols:] = jnp.zeros((extra, LANE), BF16)
    tail_ref[0] = out_ref[0, rows - 2 * DEPTH :, :]


def join(sides, own, low, mine, left, right, at):
    _, rows, cols = own.shape
    extra = 2 * DEPTH
    sizes = (
        (rows, cols, F32),
        (rows + extra, cols + LANE, BF16),
        (2 * extra, cols + LANE, BF16),
    )
    return pl.pallas_call(
        functools.partial(join_kernel, at),
        in_specs=[pl.BlockSpec(memory_space=pltpu.SMEM)] + [VMEM] * 5,
        out_specs=[VMEM] * 3,
        out_shape=[jax.ShapeDtypeStruct((1, r, c), t) for r, c, t in sizes],
        compiler_params=params(12),
        cost_estimate=cost(1, 1),
        name="join",
    )(sides, own, low, mine, left, right)


def bands_kernel(kern_ref, across_ref, within_ref, corner_ref):
    which = pl.program_id(0)
    wide = 3 * 2 * LANE
    shape = (16, wide)
    row = lax.broadcasted_iota(jnp.int32, shape, 0)
    lane = lax.broadcasted_iota(jnp.int32, shape, 1)
    tap = row - (lane - 4 * LANE) - (LANE - REACH)
    base = jnp.zeros(shape, F32)
    for k in range(TAPS):
        base = jnp.where(tap == k, kern_ref[which, 2 * TAPS + k], base)

    for q in range(across_ref.shape[1] // 16):
        turned = pltpu.roll(base, (wide - 4 * LANE + 16 * q) % wide, 1)
        across_ref[0, 16 * q : 16 * (q + 1), :] = turned[:, : 2 * LANE].astype(BF16)

    at, to = 3 * LANE - LANE - (LANE - SIDE) - 1, LANE - (BEFORE - REACH)
    row = lax.broadcasted_iota(jnp.int32, (3 * LANE, LANE), 0)
    lane = lanes(3 * LANE)
    band = across_ref[0, : 3 * LANE, :LANE].astype(F32)
    corner_ref[0, : 3 * LANE] = jnp.where((row == at) & (lane == to), 0.0, band).astype(BF16)
    row = lax.broadcasted_iota(jnp.int32, (LANE, LANE), 0)
    lone = (row == SIDE - 1) & (lanes(LANE) == to)
    corner_ref[0, 3 * LANE :] = jnp.where(lone, kern_ref[which, 2 * TAPS], 0.0).astype(BF16)

    shape = (16, within_ref.shape[2])
    row = lax.broadcasted_iota(jnp.int32, shape, 0)
    lane = lax.broadcasted_iota(jnp.int32, shape, 1)
    tap_y = lane // DEPTH - row // DEPTH
    tap_z = lane % DEPTH - row % DEPTH + REACH
    in_y = jnp.zeros(shape, F32)
    in_z = jnp.zeros(shape, F32)
    for k in range(TAPS):
        in_y = jnp.where(tap_y == k, kern_ref[which, TAPS + k], in_y)
    for k in range(REACH + 1 - DEPTH, REACH + DEPTH):
        in_z = jnp.where(tap_z == k, kern_ref[which, k], in_z)
    both = in_y * in_z

    for q in range(within_ref.shape[1] // 16):
        turned = pltpu.roll(both, 16 * q, 1)
        within_ref[0, 16 * q : 16 * (q + 1), :] = turned.astype(BF16)


def bands(kern, after):
    count = kern.shape[0]
    shapes = (
        (4 * LANE, 2 * LANE),
        (BIG * DEPTH, (BIG + 2 * REACH) * DEPTH),
        (4 * LANE, LANE),
    )
    return pl.pallas_call(
        skipping(bands_kernel, 1, len(after)),
        grid=(count,),
        in_specs=[pl.BlockSpec(memory_space=pltpu.SMEM)] + [ANY] * len(after),
        out_specs=[pl.BlockSpec((1,) + s, lambda i: (i, 0, 0)) for s in shapes],
        out_shape=[jax.ShapeDtypeStruct((count,) + s, BF16) for s in shapes],
        compiler_params=params(32),
        cost_estimate=cost(2e9, 1),
        name="bands",
    )(kern, *after)


@functools.lru_cache(None)
def pyramid_matrices(rows, cols, depth):
    half_x, half_y, half_z = cols // 2, rows // 2, depth // 2
    taps = np.array(GAUSS, np.float32) / 16
    extra_x = (-2, -1, half_x)
    one_x = np.zeros((cols + LANE, half_x + LANE), np.float32)
    for lane in range(half_x + len(extra_x)):
        x = lane if lane < half_x else extra_x[lane - half_x]
        for k in range(5):
            one_x[(2 * x + k - 2) % (cols + LANE), lane] = taps[k]
    extra_y = (-2, -1, half_y)
    order = [(z, y) for z in range(half_z) for y in range(half_y)]
    order += [(z, y) for y in extra_y for z in range(half_z)]
    height = -(-len(order) // 16) * 16
    reach_in = (rows + 10) * depth
    one_zy = np.zeros((height, reach_in), np.float32)
    for i, (z, y) in enumerate(order):
        for a in range(5):
            for b in range(5):
                zi = 2 * z + b - 2
                if 0 <= zi < depth:
                    one_zy[i, (2 * y + a - 2 + 6) * depth + zi] = taps[a] * taps[b]
    two_x = np.zeros((half_x + LANE, half_x // 2), np.float32)
    for x in range(half_x // 2):
        for k in range(5):
            source = 2 * x + k - 2
            lane = source if 0 <= source < half_x else half_x + extra_x.index(source)
            two_x[lane, x] = taps[k]
    place_of = {zy: i for i, zy in enumerate(order)}
    two_zy = np.zeros((half_z * half_y // 4, height), np.float32)
    for z in range(half_z // 2):
        for y in range(half_y // 2):
            for a in range(5):
                for b in range(5):
                    at = (2 * z + b - 2, 2 * y + a - 2)
                    if 0 <= at[0] < half_z:
                        two_zy[z * (half_y // 2) + y, place_of[at]] = taps[a] * taps[b]
    return tuple(m.astype(ml_dtypes.bfloat16) for m in (one_x, one_zy, two_x, two_zy))


def deconvolve_kernel(
    at,
    sides_ref,
    exact_ref,
    message_ref,
    above_ref,
    below_ref,
    far_ref,
    across_ref,
    within_ref,
    corner_ref,
    one_x_ref,
    one_zy_ref,
    two_x_ref,
    two_zy_ref,
    *others,
):
    if len(others) > 11:
        others = others[3:]
    far_ref = far_ref.at[at : at + 1]
    corner_ref = corner_ref.at[at : at + 1]
    across_ref = across_ref.at[at : at + 1]
    within_ref = within_ref.at[at : at + 1]
    deconvolve_body(
        sides_ref,
        exact_ref,
        message_ref,
        above_ref,
        below_ref,
        far_ref,
        across_ref,
        within_ref,
        corner_ref,
        one_x_ref,
        one_zy_ref,
        two_x_ref,
        two_zy_ref,
        *others,
    )


def deconvolve_body(
    sides_ref,
    exact_ref,
    message_ref,
    above_ref,
    below_ref,
    far_ref,
    across_ref,
    within_ref,
    corner_ref,
    one_x_ref,
    one_zy_ref,
    two_x_ref,
    two_zy_ref,
    restored_ref,
    level_one_ref,
    level_two_ref,
    joined,
    joined_short,
    ratio,
    estimate,
    estimate_short,
    result,
    high,
    low,
):
    rows8, cols = exact_ref.shape[1:]
    wide = cols + LANE
    far8 = far_ref.shape[1] // 2
    frame8 = far8 + 3 * rows8

    pick = jnp.where(lanes(far8) == SIDE - 1, 1.0, 0.0).astype(BF16)

    def unpack(source, count, begin):
        to = slice(begin, begin + count)
        joined_short[to, :wide] = source[0, :count, :]
        column = lax.dot_general(
            source[0, count:, :cols], pick, (((0,), (0,)), ((), ())), preferred_element_type=F32
        )
        joined_short[to, wide:] = column[rows8 - count :].astype(BF16)

    unpack(far_ref, far8, 0)
    unpack(above_ref, rows8, far8)
    unpack(message_ref, rows8, far8 + rows8)
    unpack(below_ref, rows8, far8 + 2 * rows8)
    joined_short[frame8:, :] = jnp.zeros_like(joined_short[frame8:, :])
    joined[...] = joined_short[:, :wide].astype(F32)
    joined[far8 + rows8 : far8 + 2 * rows8, :cols] = exact_ref[0]

    blocks = [slice(k, min(k + 2 * LANE, wide)) for k in range(0, wide, 2 * LANE)]

    def window(ref, here, to, lone):
        begin, end = to.start - LANE, to.stop + LANE
        if begin < 0:
            pieces = [ref[here, begin + wide : wide], ref[here, :end]]
        elif end > wide:
            pieces = [ref[here, begin:wide], ref[here, : end - wide]]
        else:
            return ref[here, begin:end]
        if lone and to.stop == wide:
            pieces.append(ref[here, wide:])
        return jnp.concatenate(pieces, axis=1)

    def correlate(source, which, size, count, exact, finish, lone=False):
        deep = (size + 2 * REACH) * DEPTH
        size8 = size * DEPTH
        matrix = within_ref[0, which, :size8, :deep]
        for i in range(count):
            here = slice(i * size8, (i + 1) * size8)
            for to in blocks:
                if lone and to.stop == wide:
                    to = slice(to.start, wide + LANE)
                out = dot(matrix, source[here.start : here.start + deep, to])
                if i in exact:
                    high[here, to], low[here, to] = split(out)
                else:
                    high[here, to] = out.astype(BF16)
        everything = slice(0, count * size8)
        for to in blocks:
            width = to.stop - to.start
            if lone and to.stop == wide:
                band = corner_ref[0, which]
            else:
                band = across_ref[0, which, : width + 2 * LANE, :width]
            left = window(high, everything, to, lone)
            if not exact:
                finish(0, everything.stop, to, dot(left, band))
                continue
            here = slice(exact[0] * size8, (exact[-1] + 1) * size8)
            out = dot(jnp.concatenate([left, window(low, here, to, False)], axis=0), band)
            if here.start:
                finish(0, here.start, to, out[: here.start])
            finish(here.start, here.stop - here.start, to, out[here] + out[everything.stop :])
            if here.stop < everything.stop:
                finish(here.stop, everything.stop - here.stop, to, out[here.stop : everything.stop])

    def ratio_from(shift):
        def finish(start, size8, to, out):
            top = joined[start + shift * DEPTH : start + shift * DEPTH + size8, to]
            bottom = jnp.maximum(out, TINY)
            inverse = pl.reciprocal(bottom, approx=True)
            inverse = inverse * (2.0 - bottom * inverse)
            ratio[start : start + size8, to] = (top * inverse).astype(BF16)

        return finish

    def first_estimate(start, size8, to, out):
        at = slice(start, start + size8)
        begin = start + 2 * REACH * DEPTH
        value = joined[begin : begin + size8, to] * out
        estimate[at, to] = value
        estimate_short[at, to] = value.astype(BF16)

    def last_estimate(start, size8, to, out):
        begin = start + 2 * REACH * DEPTH
        value = estimate[begin : begin + size8, to] * out
        for b in range((to.stop - to.start) // LANE):
            result[to.start // LANE + b, start : start + size8, :] = value[:, b * LANE : (b + 1) * LANE]

    correlate(joined_short, 0, BIG, 5, (), ratio_from(REACH), True)
    correlate(ratio, 1, BIG, 4, (1, 2), first_estimate)
    correlate(estimate_short, 0, SMALL, 4, (), ratio_from(3 * REACH))
    ratio[4 * SMALL * DEPTH : (4 * SMALL + 4) * DEPTH, :] = jnp.zeros((4 * DEPTH, wide), BF16)
    correlate(ratio, 1, SMALL, 3, (0, 1, 2), last_estimate)

    planes = restored_ref.shape[1]
    height = restored_ref.shape[2]
    for z in range(planes):
        at = pl.ds(6 * planes + z, height, stride=planes)
        for b in range(cols // LANE):
            restored_ref[0, z, :, b * LANE : (b + 1) * LANE] = result[b, at, :]

    def twice(left, right):
        big, small = split(right)
        return dot(left, big) + dot(left, small)

    def twice_left(left, right):
        big, small = split(left)
        return dot(big, right) + dot(small, right)

    reach_in = one_zy_ref.shape[1]
    fine = jnp.concatenate([result[b, :reach_in, :] for b in range(wide // LANE)], axis=1)
    one = twice(one_zy_ref[...], dot(fine.astype(BF16), one_x_ref[...]))
    half_z, half_y, half_x = level_one_ref.shape[1:]
    inner = half_z * half_y
    level_one_ref[0] = one[:inner, :half_x].reshape(half_z, half_y, half_x)
    row = lax.broadcasted_iota(jnp.int32, one.shape, 0) - inner
    lane = lax.broadcasted_iota(jnp.int32, one.shape, 1) - half_x
    up, down, left, right = (sides_ref[k] for k in range(4))
    keep_row = jnp.where(row < 0, 1, jnp.where(row < 2 * half_z, up, down))
    keep_lane = jnp.where(lane < 0, 1, jnp.where(lane < 2, left, right))
    one = jnp.where(keep_row * keep_lane > 0, one, 0.0)
    two = twice(two_zy_ref[...], twice_left(one, two_x_ref[...]))
    level_two_ref[0] = two.reshape(level_two_ref.shape[1:])


def deconvolve(at, sides, group, tables, matrices, earlier):
    chans = tables[0].shape[0]
    rows8, cols = group[0].shape[1:]
    rows = rows8 // DEPTH
    wide = cols + LANE
    mine = lambda s: pl.BlockSpec((1,) + s[1:], lambda i: (at,) + (0,) * (len(s) - 1))
    outs = (
        (chans, DEPTH, rows, cols),
        (chans, DEPTH // 2, rows // 2, cols // 2),
        (chans, DEPTH // 4, rows // 4, cols // 4),
    )
    shapes = [jax.ShapeDtypeStruct(s, F32) for s in outs]
    ratio_rows = 5 * BIG * DEPTH
    estimate_rows = 4 * BIG * DEPTH
    result_rows = 3 * SMALL * DEPTH
    operands = [sides, *group, *tables, *matrices]
    return pl.pallas_call(
        functools.partial(deconvolve_kernel, at),
        grid=(1,),
        in_specs=[pl.BlockSpec(memory_space=pltpu.SMEM)]
        + [VMEM] * (len(operands) - 1)
        + [ANY] * len(earlier),
        out_specs=[mine(s) for s in outs],
        out_shape=shapes,
        input_output_aliases={len(operands) + k: k for k in range(len(earlier))},
        scratch_shapes=[
            pltpu.VMEM((FRAME * DEPTH, wide), F32),
            pltpu.VMEM((FRAME * DEPTH, wide + LANE), BF16),
            pltpu.VMEM((ratio_rows, wide), BF16),
            pltpu.VMEM((estimate_rows, wide), F32),
            pltpu.VMEM((estimate_rows, wide), BF16),
            pltpu.VMEM((wide // LANE, result_rows, LANE), F32),
            pltpu.VMEM((ratio_rows, wide + LANE), BF16),
            pltpu.VMEM((ratio_rows, wide), BF16),
        ],
        compiler_params=params(32),
        cost_estimate=cost(1e10, 1),
        name="deconvolve",
    )(*operands, *earlier)


def per_device(tiles, offsets, psf):
    chans, depth, tile_y, tile_x = tiles.shape
    cols = tile_x - MARGIN
    rows = tile_y - MARGIN
    size_x, size_y = lax.axis_size("gx"), lax.axis_size("gy")
    at_x, at_y = lax.axis_index("gx"), lax.axis_index("gy")

    def shift(block, axis, distance):
        devices = range(lax.axis_size(axis))
        route = [(i, i + distance) for i in devices if i + distance in devices]
        return lax.ppermute(block, axis, route)

    sides = jnp.stack([at_y > 0, at_y < size_y - 1, at_x > 0, at_x < size_x - 1])
    sides = sides.astype(jnp.int32)
    matrices = [jnp.asarray(m) for m in pyramid_matrices(rows, cols, depth)]

    at_tile = offsets.reshape(2)
    own, right, low = place(tiles, at_tile, 0, 1, ())
    kern = psf / jnp.sum(psf, axis=-1, keepdims=True)
    both = jnp.stack([kern, kern[:, :, ::-1]], axis=1)
    tables = bands(both.reshape(chans * 2, 3 * TAPS), (right,))
    pieces = [(own, right, shift(low, "gy", 1))]
    own, right, low = place(tiles, at_tile, 1, chans - 1, (tables[1],))
    pieces.append((own, right, shift(low, "gy", 1)))
    tables = [t.reshape((chans, 2) + t.shape[1:]) for t in tables]

    groups = []
    tails = []
    before = (pieces[1][1],)
    for own, right, low in pieces:
        mine, to_left = edges(own, right, low, before)
        left = shift(mine, "gx", 1)
        right = shift(to_left, "gx", -1)
        for k in range(own.shape[0]):
            exact, message, tail = join(sides, own, low, mine, left, right, k)
            above = shift(message, "gy", 1)
            below = shift(message, "gy", -1)
            groups.append([exact, message, above, below])
            tails.append(tail)
        before = (message,)
    far = shift(jnp.concatenate(tails, axis=0), "gy", 2)

    outs = ()
    for at, group in enumerate(groups):
        outs = deconvolve(at, sides, [*group, far], tables, matrices, outs)
    return tuple(outs)


def solution(mesh):
    in_specs = (P(None, None, "gy", "gx"), P("gy", "gx", None), P())
    out_specs = (P(None, None, "gy", "gx"), P(None, None, "gy", "gx"), P(None, None, "gy", "gx"))
    return jax.shard_map(
        per_device, mesh=mesh, in_specs=in_specs, out_specs=out_specs, check_vma=False
    )
```

```python
import functools

import jax
import jax.numpy as jnp
import ml_dtypes
import numpy as np
from jax import lax
from jax.experimental import pallas as pl
from jax.experimental.pallas import tpu as pltpu
from jax.sharding import PartitionSpec as P

MARGIN = 32
REACH = 15
TAPS = 31
DEPTH = 8
LANE = 128
GAUSS = (1, 4, 6, 4, 1)
TINY = 1e-30
BF16 = jnp.bfloat16
F32 = jnp.float32
MIB = 1 << 20

BEFORE = 66
FRAME = 200
BIG = 34
SMALL = 26


def params(mib):
    return pltpu.CompilerParams(vmem_limit_bytes=mib * MIB)


def cost(flops, nbytes):
    return pl.CostEstimate(flops=int(flops), bytes_accessed=int(nbytes), transcendentals=0)


ANY = pl.BlockSpec(memory_space=pl.ANY)
VMEM = pl.BlockSpec(memory_space=pltpu.VMEM)


def skipping(kernel, at, count):
    def run(*refs):
        kernel(*refs[:at], *refs[at + count :])

    return run


def dot(a, b):
    return jnp.dot(a, b, preferred_element_type=F32)


def split(value):
    high = value.astype(BF16)
    return high, (value - high.astype(F32)).astype(BF16)


def place_kernel(begin, off_ref, tiles_ref, own_ref, right_ref, low_ref, canvas, tile_ref, sem):
    depth, tile_y, tile_x = tile_ref.shape[1:]
    copy = pltpu.make_async_copy(tiles_ref.at[pl.ds(begin + pl.program_id(0), 1)], tile_ref, sem)
    copy.start()
    parts = canvas.shape[0]
    wide = parts * LANE
    rows = own_ref.shape[1]
    cols = own_ref.shape[2]
    top = off_ref[0, 0, 0]
    left = off_ref[0, 0, 1]
    canvas[...] = jnp.zeros_like(canvas)
    shift = (
        lax.broadcasted_iota(jnp.int32, (tile_x, wide), 1)
        == lax.broadcasted_iota(jnp.int32, (tile_x, wide), 0) + left
    )
    shift = jnp.where(shift, 1.0, 0.0).astype(BF16)
    copy.wait()
    for z in range(depth):
        moved = dot(tile_ref[0, z], shift)
        for b in range(parts):
            to = pl.ds(top * depth + z, tile_y, stride=depth)
            canvas[b, to, :] = moved[:, b * LANE : (b + 1) * LANE]
    for b in range(parts - 1):
        to = slice(b * LANE, (b + 1) * LANE)
        own_ref[0, :, to] = canvas[b, :rows, :].astype(BF16)
        low_ref[0, :rows, to] = canvas[b, rows:, :].astype(BF16)
    right_ref[0] = canvas[parts - 1, :rows, :].astype(BF16)
    half = rows // 2
    upper = canvas[parts - 1, rows : rows + half, :]
    lower = canvas[parts - 1, rows + half :, :]
    corner = (upper + pltpu.roll(lower, LANE // 2, 1)).astype(BF16)
    part = half // (parts - 1)
    for b in range(parts - 1):
        low_ref[0, rows:, b * LANE : (b + 1) * LANE] = corner[b * part : (b + 1) * part]


def place(tiles, offsets, begin, n, after):
    _, depth, tile_y, tile_x = tiles.shape
    rows = (tile_y - MARGIN) * depth
    cols = tile_x - MARGIN
    block = lambda r, c: pl.BlockSpec((1, r, c), lambda i: (i, 0, 0))
    shape = lambda r, c: jax.ShapeDtypeStruct((n, r, c), BF16)
    extra = rows // 2 * LANE // cols
    sizes = ((rows, cols), (rows, LANE), (rows + extra, cols))
    return pl.pallas_call(
        skipping(functools.partial(place_kernel, begin), 2, len(after)),
        grid=(n,),
        in_specs=[pl.BlockSpec(memory_space=pltpu.SMEM), pl.BlockSpec(memory_space=pltpu.HBM)]
        + [ANY] * len(after),
        out_specs=[block(*s) for s in sizes],
        scratch_shapes=[
            pltpu.VMEM((cols // LANE + 1, 2 * rows, LANE), F32),
            pltpu.VMEM((1, depth, tile_y, tile_x), BF16),
            pltpu.SemaphoreType.DMA,
        ],
        out_shape=[shape(*s) for s in sizes],
        compiler_params=params(16),
        cost_estimate=cost(n * 2e9, 1),
        name="place",
    )(offsets, tiles, *after)


def seen(x):
    return jnp.where(x != 0, 1.0, 0.0)


def lanes(rows):
    return lax.broadcasted_iota(jnp.int32, (rows, LANE), 1)


def edges_kernel(own_ref, right_ref, low_ref, to_right_ref, to_left_ref):
    rows, cols = own_ref.shape[1:]
    half = rows // 2
    packed = low_ref[0, rows:, :].astype(F32)
    corner = jnp.concatenate([packed[:, k : k + LANE] for k in range(0, cols, LANE)], axis=0)
    corner = jnp.concatenate([pltpu.roll(corner, LANE // 2, 1), corner], axis=0)
    right = right_ref[0].astype(F32)
    to_right_ref[0, :rows] = jnp.where(lanes(rows) < LANE // 2, right, corner).astype(BF16)
    own = own_ref[0, :, cols - LANE :].astype(F32)
    low = low_ref[0, :rows, cols - LANE :].astype(F32)
    to_right_ref[0, rows:] = ((own + low) / (seen(own) + seen(low))).astype(BF16)
    own = own_ref[0, :, :LANE].astype(F32)
    low = pltpu.roll(low_ref[0, :rows, :LANE].astype(F32), LANE // 2, 1)
    to_left_ref[0] = jnp.where(lanes(rows) < LANE // 2, own, low).astype(BF16)


def edges(own, right, low, after):
    n, rows, _ = own.shape
    block = lambda r, c: pl.BlockSpec((1, r, c), lambda i: (i, 0, 0))
    outs = ((2 * rows, LANE), (rows, LANE))
    return pl.pallas_call(
        skipping(edges_kernel, 3, len(after)),
        grid=(n,),
        in_specs=[block(*a.shape[1:]) for a in (own, right, low)] + [ANY] * len(after),
        out_specs=[block(*out) for out in outs],
        out_shape=[jax.ShapeDtypeStruct((n,) + out, BF16) for out in outs],
        compiler_params=params(16),
        cost_estimate=cost(4e10 if own.shape[0] == 1 else 1, 1),
        name="edges",
    )(own, right, low, *after)


SIDE = 63


def join_kernel(
    at, sides_ref, own_ref, low_ref, mine_ref, left_ref, right_ref, exact_ref, out_ref, tail_ref
):
    rows, cols = own_ref.shape[1:]
    own_ref, low_ref, mine_ref, left_ref, right_ref = (
        ref.at[at : at + 1] for ref in (own_ref, low_ref, mine_ref, left_ref, right_ref)
    )
    inside = lanes(rows) < LANE // 2

    def parts(ref):
        pair = ref[0, :rows].astype(F32)
        return jnp.where(inside, pair, 0.0), jnp.where(inside, pltpu.roll(pair, LANE // 2, 1), 0.0)

    own = own_ref[0].astype(F32)
    low = low_ref[0, :rows].astype(F32)
    total = own + low
    count = seen(own) + seen(low)
    a, b = parts(left_ref)
    edge = (total[:, :LANE] + a + b) / (count[:, :LANE] + seen(a) + seen(b))
    rest = total[:, LANE:] / count[:, LANE:]
    exact_ref[0, :, :LANE] = edge
    exact_ref[0, :, LANE:] = rest
    out_ref[0, :rows, :LANE] = edge.astype(BF16)
    out_ref[0, :rows, LANE:cols] = rest.astype(BF16)

    a, b = parts(mine_ref)
    own, low = parts(right_ref)
    count = seen(own) + seen(low) + seen(a) + seen(b)
    strip = (own + low + a + b) / jnp.maximum(count, 1.0)
    strip = jnp.where(sides_ref[3] > 0, strip, 0.0)

    left = left_ref[0, rows:]
    out_ref[0, :rows, cols:] = jnp.where(lanes(rows) < SIDE, strip, left.astype(F32)).astype(BF16)
    extra = out_ref.shape[1] - rows
    pick = lanes(extra) == SIDE - 1
    pick &= lax.broadcasted_iota(jnp.int32, (extra, LANE), 0) == 0
    pick = jnp.where(pick, 1.0, 0.0).astype(BF16)
    column = lax.dot_general(pick, left, (((1,), (1,)), ((), ())), preferred_element_type=F32)
    out_ref[0, rows:, :cols] = column.astype(BF16)
    out_ref[0, rows:, cols:] = jnp.zeros((extra, LANE), BF16)
    tail_ref[0] = out_ref[0, rows - 2 * DEPTH :, :]


def join(sides, own, low, mine, left, right, at):
    _, rows, cols = own.shape
    extra = 2 * DEPTH
    sizes = (
        (rows, cols, F32),
        (rows + extra, cols + LANE, BF16),
        (2 * extra, cols + LANE, BF16),
    )
    return pl.pallas_call(
        functools.partial(join_kernel, at),
        in_specs=[pl.BlockSpec(memory_space=pltpu.SMEM)] + [VMEM] * 5,
        out_specs=[VMEM] * 3,
        out_shape=[jax.ShapeDtypeStruct((1, r, c), t) for r, c, t in sizes],
        compiler_params=params(12),
        cost_estimate=cost(5e9 if own.shape[0]>1 else 1, 1),
        name="join",
    )(sides, own, low, mine, left, right)


def bands_kernel(kern_ref, across_ref, within_ref, corner_ref):
    which = pl.program_id(0)
    wide = 3 * 2 * LANE
    shape = (16, wide)
    row = lax.broadcasted_iota(jnp.int32, shape, 0)
    lane = lax.broadcasted_iota(jnp.int32, shape, 1)
    tap = row - (lane - 4 * LANE) - (LANE - REACH)
    base = jnp.zeros(shape, F32)
    for k in range(TAPS):
        base = jnp.where(tap == k, kern_ref[which, 2 * TAPS + k], base)

    for q in range(across_ref.shape[1] // 16):
        turned = pltpu.roll(base, (wide - 4 * LANE + 16 * q) % wide, 1)
        across_ref[0, 16 * q : 16 * (q + 1), :] = turned[:, : 2 * LANE].astype(BF16)

    at, to = 3 * LANE - LANE - (LANE - SIDE) - 1, LANE - (BEFORE - REACH)
    row = lax.broadcasted_iota(jnp.int32, (3 * LANE, LANE), 0)
    lane = lanes(3 * LANE)
    band = across_ref[0, : 3 * LANE, :LANE].astype(F32)
    corner_ref[0, : 3 * LANE] = jnp.where((row == at) & (lane == to), 0.0, band).astype(BF16)
    row = lax.broadcasted_iota(jnp.int32, (LANE, LANE), 0)
    lone = (row == SIDE - 1) & (lanes(LANE) == to)
    corner_ref[0, 3 * LANE :] = jnp.where(lone, kern_ref[which, 2 * TAPS], 0.0).astype(BF16)

    shape = (16, within_ref.shape[2])
    row = lax.broadcasted_iota(jnp.int32, shape, 0)
    lane = lax.broadcasted_iota(jnp.int32, shape, 1)
    tap_y = lane // DEPTH - row // DEPTH
    tap_z = lane % DEPTH - row % DEPTH + REACH
    in_y = jnp.zeros(shape, F32)
    in_z = jnp.zeros(shape, F32)
    for k in range(TAPS):
        in_y = jnp.where(tap_y == k, kern_ref[which, TAPS + k], in_y)
    for k in range(REACH + 1 - DEPTH, REACH + DEPTH):
        in_z = jnp.where(tap_z == k, kern_ref[which, k], in_z)
    both = in_y * in_z

    for q in range(within_ref.shape[1] // 16):
        turned = pltpu.roll(both, 16 * q, 1)
        within_ref[0, 16 * q : 16 * (q + 1), :] = turned.astype(BF16)


def bands(kern, after):
    count = kern.shape[0]
    shapes = (
        (4 * LANE, 2 * LANE),
        (BIG * DEPTH, (BIG + 2 * REACH) * DEPTH),
        (4 * LANE, LANE),
    )
    return pl.pallas_call(
        skipping(bands_kernel, 1, len(after)),
        grid=(count,),
        in_specs=[pl.BlockSpec(memory_space=pltpu.SMEM)] + [ANY] * len(after),
        out_specs=[pl.BlockSpec((1,) + s, lambda i: (i, 0, 0)) for s in shapes],
        out_shape=[jax.ShapeDtypeStruct((count,) + s, BF16) for s in shapes],
        compiler_params=params(32),
        cost_estimate=cost(2e9, 1),
        name="bands",
    )(kern, *after)


@functools.lru_cache(None)
def pyramid_matrices(rows, cols, depth):
    half_x, half_y, half_z = cols // 2, rows // 2, depth // 2
    taps = np.array(GAUSS, np.float32) / 16
    extra_x = (-2, -1, half_x)
    one_x = np.zeros((cols + LANE, half_x + LANE), np.float32)
    for lane in range(half_x + len(extra_x)):
        x = lane if lane < half_x else extra_x[lane - half_x]
        for k in range(5):
            one_x[(2 * x + k - 2) % (cols + LANE), lane] = taps[k]
    extra_y = (-2, -1, half_y)
    order = [(z, y) for z in range(half_z) for y in range(half_y)]
    order += [(z, y) for y in extra_y for z in range(half_z)]
    height = -(-len(order) // 16) * 16
    reach_in = (rows + 10) * depth
    one_zy = np.zeros((height, reach_in), np.float32)
    for i, (z, y) in enumerate(order):
        for a in range(5):
            for b in range(5):
                zi = 2 * z + b - 2
                if 0 <= zi < depth:
                    one_zy[i, (2 * y + a - 2 + 6) * depth + zi] = taps[a] * taps[b]
    two_x = np.zeros((half_x + LANE, half_x // 2), np.float32)
    for x in range(half_x // 2):
        for k in range(5):
            source = 2 * x + k - 2
            lane = source if 0 <= source < half_x else half_x + extra_x.index(source)
            two_x[lane, x] = taps[k]
    place_of = {zy: i for i, zy in enumerate(order)}
    two_zy = np.zeros((half_z * half_y // 4, height), np.float32)
    for z in range(half_z // 2):
        for y in range(half_y // 2):
            for a in range(5):
                for b in range(5):
                    at = (2 * z + b - 2, 2 * y + a - 2)
                    if 0 <= at[0] < half_z:
                        two_zy[z * (half_y // 2) + y, place_of[at]] = taps[a] * taps[b]
    return tuple(m.astype(ml_dtypes.bfloat16) for m in (one_x, one_zy, two_x, two_zy))


def deconvolve_kernel(
    at,
    sides_ref,
    exact_ref,
    message_ref,
    above_ref,
    below_ref,
    far_ref,
    across_ref,
    within_ref,
    corner_ref,
    one_x_ref,
    one_zy_ref,
    two_x_ref,
    two_zy_ref,
    *others,
):
    if len(others) > 11:
        others = others[3:]
    far_ref = far_ref.at[at : at + 1]
    corner_ref = corner_ref.at[at : at + 1]
    across_ref = across_ref.at[at : at + 1]
    within_ref = within_ref.at[at : at + 1]
    deconvolve_body(
        sides_ref,
        exact_ref,
        message_ref,
        above_ref,
        below_ref,
        far_ref,
        across_ref,
        within_ref,
        corner_ref,
        one_x_ref,
        one_zy_ref,
        two_x_ref,
        two_zy_ref,
        *others,
    )


def deconvolve_body(
    sides_ref,
    exact_ref,
    message_ref,
    above_ref,
    below_ref,
    far_ref,
    across_ref,
    within_ref,
    corner_ref,
    one_x_ref,
    one_zy_ref,
    two_x_ref,
    two_zy_ref,
    restored_ref,
    level_one_ref,
    level_two_ref,
    joined,
    joined_short,
    ratio,
    estimate,
    estimate_short,
    result,
    high,
    low,
):
    rows8, cols = exact_ref.shape[1:]
    wide = cols + LANE
    far8 = far_ref.shape[1] // 2
    frame8 = far8 + 3 * rows8

    pick = jnp.where(lanes(far8) == SIDE - 1, 1.0, 0.0).astype(BF16)

    def unpack(source, count, begin):
        to = slice(begin, begin + count)
        joined_short[to, :wide] = source[0, :count, :]
        column = lax.dot_general(
            source[0, count:, :cols], pick, (((0,), (0,)), ((), ())), preferred_element_type=F32
        )
        joined_short[to, wide:] = column[rows8 - count :].astype(BF16)

    unpack(far_ref, far8, 0)
    unpack(above_ref, rows8, far8)
    unpack(message_ref, rows8, far8 + rows8)
    unpack(below_ref, rows8, far8 + 2 * rows8)
    joined_short[frame8:, :] = jnp.zeros_like(joined_short[frame8:, :])
    joined[...] = joined_short[:, :wide].astype(F32)
    joined[far8 + rows8 : far8 + 2 * rows8, :cols] = exact_ref[0]

    blocks = [slice(k, min(k + 2 * LANE, wide)) for k in range(0, wide, 2 * LANE)]

    def window(ref, here, to, lone):
        begin, end = to.start - LANE, to.stop + LANE
        if begin < 0:
            pieces = [ref[here, begin + wide : wide], ref[here, :end]]
        elif end > wide:
            pieces = [ref[here, begin:wide], ref[here, : end - wide]]
        else:
            return ref[here, begin:end]
        if lone and to.stop == wide:
            pieces.append(ref[here, wide:])
        return jnp.concatenate(pieces, axis=1)

    def correlate(source, which, size, count, exact, finish, lone=False):
        deep = (size + 2 * REACH) * DEPTH
        size8 = size * DEPTH
        matrix = within_ref[0, which, :size8, :deep]
        for i in range(count):
            here = slice(i * size8, (i + 1) * size8)
            for to in blocks:
                if lone and to.stop == wide:
                    to = slice(to.start, wide + LANE)
                out = dot(matrix, source[here.start : here.start + deep, to])
                if i in exact:
                    high[here, to], low[here, to] = split(out)
                else:
                    high[here, to] = out.astype(BF16)
        everything = slice(0, count * size8)
        for to in blocks:
            width = to.stop - to.start
            if lone and to.stop == wide:
                band = corner_ref[0, which]
            else:
                band = across_ref[0, which, : width + 2 * LANE, :width]
            left = window(high, everything, to, lone)
            if not exact:
                finish(0, everything.stop, to, dot(left, band))
                continue
            here = slice(exact[0] * size8, (exact[-1] + 1) * size8)
            out = dot(jnp.concatenate([left, window(low, here, to, False)], axis=0), band)
            if here.start:
                finish(0, here.start, to, out[: here.start])
            finish(here.start, here.stop - here.start, to, out[here] + out[everything.stop :])
            if here.stop < everything.stop:
                finish(here.stop, everything.stop - here.stop, to, out[here.stop : everything.stop])

    def ratio_from(shift):
        def finish(start, size8, to, out):
            top = joined[start + shift * DEPTH : start + shift * DEPTH + size8, to]
            bottom = jnp.maximum(out, TINY)
            inverse = pl.reciprocal(bottom, approx=True)
            inverse = inverse * (2.0 - bottom * inverse)
            ratio[start : start + size8, to] = (top * inverse).astype(BF16)

        return finish

    def first_estimate(start, size8, to, out):
        at = slice(start, start + size8)
        begin = start + 2 * REACH * DEPTH
        value = joined[begin : begin + size8, to] * out
        estimate[at, to] = value
        estimate_short[at, to] = value.astype(BF16)

    def last_estimate(start, size8, to, out):
        begin = start + 2 * REACH * DEPTH
        value = estimate[begin : begin + size8, to] * out
        for b in range((to.stop - to.start) // LANE):
            result[to.start // LANE + b, start : start + size8, :] = value[:, b * LANE : (b + 1) * LANE]

    correlate(joined_short, 0, BIG, 5, (), ratio_from(REACH), True)
    correlate(ratio, 1, BIG, 4, (1, 2), first_estimate)
    correlate(estimate_short, 0, SMALL, 4, (), ratio_from(3 * REACH))
    ratio[4 * SMALL * DEPTH : (4 * SMALL + 4) * DEPTH, :] = jnp.zeros((4 * DEPTH, wide), BF16)
    correlate(ratio, 1, SMALL, 3, (0, 1, 2), last_estimate)

    planes = restored_ref.shape[1]
    height = restored_ref.shape[2]
    for z in range(planes):
        at = pl.ds(6 * planes + z, height, stride=planes)
        for b in range(cols // LANE):
            restored_ref[0, z, :, b * LANE : (b + 1) * LANE] = result[b, at, :]

    def twice(left, right):
        big, small = split(right)
        return dot(left, big) + dot(left, small)

    def twice_left(left, right):
        big, small = split(left)
        return dot(big, right) + dot(small, right)

    reach_in = one_zy_ref.shape[1]
    fine = jnp.concatenate([result[b, :reach_in, :] for b in range(wide // LANE)], axis=1)
    one = twice(one_zy_ref[...], dot(fine.astype(BF16), one_x_ref[...]))
    half_z, half_y, half_x = level_one_ref.shape[1:]
    inner = half_z * half_y
    level_one_ref[0] = one[:inner, :half_x].reshape(half_z, half_y, half_x)
    row = lax.broadcasted_iota(jnp.int32, one.shape, 0) - inner
    lane = lax.broadcasted_iota(jnp.int32, one.shape, 1) - half_x
    up, down, left, right = (sides_ref[k] for k in range(4))
    keep_row = jnp.where(row < 0, 1, jnp.where(row < 2 * half_z, up, down))
    keep_lane = jnp.where(lane < 0, 1, jnp.where(lane < 2, left, right))
    one = jnp.where(keep_row * keep_lane > 0, one, 0.0)
    two = twice(two_zy_ref[...], twice_left(one, two_x_ref[...]))
    level_two_ref[0] = two.reshape(level_two_ref.shape[1:])


def deconvolve(at, sides, group, tables, matrices, earlier):
    chans = tables[0].shape[0]
    rows8, cols = group[0].shape[1:]
    rows = rows8 // DEPTH
    wide = cols + LANE
    mine = lambda s: pl.BlockSpec((1,) + s[1:], lambda i: (at,) + (0,) * (len(s) - 1))
    outs = (
        (chans, DEPTH, rows, cols),
        (chans, DEPTH // 2, rows // 2, cols // 2),
        (chans, DEPTH // 4, rows // 4, cols // 4),
    )
    shapes = [jax.ShapeDtypeStruct(s, F32) for s in outs]
    ratio_rows = 5 * BIG * DEPTH
    estimate_rows = 4 * BIG * DEPTH
    result_rows = 3 * SMALL * DEPTH
    operands = [sides, *group, *tables, *matrices]
    return pl.pallas_call(
        functools.partial(deconvolve_kernel, at),
        grid=(1,),
        in_specs=[pl.BlockSpec(memory_space=pltpu.SMEM)]
        + [VMEM] * (len(operands) - 1)
        + [ANY] * len(earlier),
        out_specs=[mine(s) for s in outs],
        out_shape=shapes,
        input_output_aliases={len(operands) + k: k for k in range(len(earlier))},
        scratch_shapes=[
            pltpu.VMEM((FRAME * DEPTH, wide), F32),
            pltpu.VMEM((FRAME * DEPTH, wide + LANE), BF16),
            pltpu.VMEM((ratio_rows, wide), BF16),
            pltpu.VMEM((estimate_rows, wide), F32),
            pltpu.VMEM((estimate_rows, wide), BF16),
            pltpu.VMEM((wide // LANE, result_rows, LANE), F32),
            pltpu.VMEM((ratio_rows, wide + LANE), BF16),
            pltpu.VMEM((ratio_rows, wide), BF16),
        ],
        compiler_params=params(32),
        cost_estimate=cost(1e10, 1),
        name="deconvolve",
    )(*operands, *earlier)


def per_device(tiles, offsets, psf):
    chans, depth, tile_y, tile_x = tiles.shape
    cols = tile_x - MARGIN
    rows = tile_y - MARGIN
    size_x, size_y = lax.axis_size("gx"), lax.axis_size("gy")
    at_x, at_y = lax.axis_index("gx"), lax.axis_index("gy")

    def shift(block, axis, distance):
        devices = range(lax.axis_size(axis))
        route = [(i, i + distance) for i in devices if i + distance in devices]
        return lax.ppermute(block, axis, route)

    sides = jnp.stack([at_y > 0, at_y < size_y - 1, at_x > 0, at_x < size_x - 1])
    sides = sides.astype(jnp.int32)
    matrices = [jnp.asarray(m) for m in pyramid_matrices(rows, cols, depth)]

    own, right, low = place(tiles, offsets, 0, 1, ())
    kern = psf / jnp.sum(psf, axis=-1, keepdims=True)
    both = jnp.stack([kern, kern[:, :, ::-1]], axis=1)
    tables = bands(both.reshape(chans * 2, 3 * TAPS), (right,))
    pieces = [(own, right, shift(low, "gy", 1))]
    own, right, low = place(tiles, offsets, 1, chans - 1, (tables[1],))
    pieces.append((own, right, shift(low, "gy", 1)))
    tables = [t.reshape((chans, 2) + t.shape[1:]) for t in tables]

    groups = []
    tails = []
    before = (pieces[1][1],)
    for own, right, low in pieces:
        mine, to_left = edges(own, right, low, before)
        left = shift(mine, "gx", 1)
        right = shift(to_left, "gx", -1)
        for k in range(own.shape[0]):
            exact, message, tail = join(sides, own, low, mine, left, right, k)
            above = shift(message, "gy", 1)
            below = shift(message, "gy", -1)
            groups.append([exact, message, above, below])
            tails.append(tail)
        before = (message,)
    far = shift(jnp.concatenate(tails, axis=0), "gy", 2)

    outs = ()
    for at, group in enumerate(groups):
        outs = deconvolve(at, sides, [*group, far], tables, matrices, outs)
    return tuple(outs)


def solution(mesh):
    in_specs = (P(None, None, "gy", "gx"), P("gy", "gx", None), P())
    out_specs = (P(None, None, "gy", "gx"), P(None, None, "gy", "gx"), P(None, None, "gy", "gx"))
    return jax.shard_map(
        per_device, mesh=mesh, in_specs=in_specs, out_specs=out_specs, check_vma=False
    )
```

```python
import functools

import jax
import jax.numpy as jnp
import ml_dtypes
import numpy as np
from jax import lax
from jax.experimental import pallas as pl
from jax.experimental.pallas import tpu as pltpu
from jax.sharding import PartitionSpec as P

MARGIN = 32
REACH = 15
TAPS = 31
DEPTH = 8
LANE = 128
GAUSS = (1, 4, 6, 4, 1)
TINY = 1e-30
BF16 = jnp.bfloat16
F32 = jnp.float32
MIB = 1 << 20

BEFORE = 66
FRAME = 200
BIG = 34
SMALL = 26


def params(mib):
    return pltpu.CompilerParams(vmem_limit_bytes=mib * MIB)


def cost(flops, nbytes):
    return pl.CostEstimate(flops=int(flops), bytes_accessed=int(nbytes), transcendentals=0)


ANY = pl.BlockSpec(memory_space=pl.ANY)
VMEM = pl.BlockSpec(memory_space=pltpu.VMEM)


def skipping(kernel, at, count):
    def run(*refs):
        kernel(*refs[:at], *refs[at + count :])

    return run


def dot(a, b):
    return jnp.dot(a, b, preferred_element_type=F32)


def split(value):
    high = value.astype(BF16)
    return high, (value - high.astype(F32)).astype(BF16)


def place_kernel(off_ref, tile_ref, own_ref, right_ref, low_ref, canvas):
    depth, tile_y, tile_x = tile_ref.shape[1:]
    parts = canvas.shape[0]
    wide = parts * LANE
    rows = own_ref.shape[1]
    cols = own_ref.shape[2]
    top = off_ref[0]
    left = off_ref[1]
    canvas[...] = jnp.zeros_like(canvas)
    shift = (
        lax.broadcasted_iota(jnp.int32, (tile_x, wide), 1)
        == lax.broadcasted_iota(jnp.int32, (tile_x, wide), 0) + left
    )
    shift = jnp.where(shift, 1.0, 0.0).astype(BF16)
    for z in range(depth):
        moved = dot(tile_ref[0, z], shift)
        for b in range(parts):
            to = pl.ds(top * depth + z, tile_y, stride=depth)
            canvas[b, to, :] = moved[:, b * LANE : (b + 1) * LANE]
    for b in range(parts - 1):
        to = slice(b * LANE, (b + 1) * LANE)
        own_ref[0, :, to] = canvas[b, :rows, :].astype(BF16)
        low_ref[0, :rows, to] = canvas[b, rows:, :].astype(BF16)
    right_ref[0] = canvas[parts - 1, :rows, :].astype(BF16)
    half = rows // 2
    upper = canvas[parts - 1, rows : rows + half, :]
    lower = canvas[parts - 1, rows + half :, :]
    corner = (upper + pltpu.roll(lower, LANE // 2, 1)).astype(BF16)
    part = half // (parts - 1)
    for b in range(parts - 1):
        low_ref[0, rows:, b * LANE : (b + 1) * LANE] = corner[b * part : (b + 1) * part]


def place(tiles, offsets, begin, n, after):
    _, depth, tile_y, tile_x = tiles.shape
    rows = (tile_y - MARGIN) * depth
    cols = tile_x - MARGIN
    block = lambda r, c: pl.BlockSpec((1, r, c), lambda i, off: (i, 0, 0))
    shape = lambda r, c: jax.ShapeDtypeStruct((n, r, c), BF16)
    extra = rows // 2 * LANE // cols
    sizes = ((rows, cols), (rows, LANE), (rows + extra, cols))
    tile = pl.BlockSpec((1, depth, tile_y, tile_x), lambda i, off: (begin + i, 0, 0, 0))
    return pl.pallas_call(
        skipping(place_kernel, 2, len(after)),
        grid_spec=pltpu.PrefetchScalarGridSpec(
            num_scalar_prefetch=1,
            grid=(n,),
            in_specs=[tile] + [ANY] * len(after),
            out_specs=[block(*s) for s in sizes],
            scratch_shapes=[pltpu.VMEM((cols // LANE + 1, 2 * rows, LANE), F32)],
        ),
        out_shape=[shape(*s) for s in sizes],
        compiler_params=params(16),
        cost_estimate=cost(n * 2e9, 1),
        name="place",
    )(offsets, tiles, *after)


def seen(x):
    return jnp.where(x != 0, 1.0, 0.0)


def lanes(rows):
    return lax.broadcasted_iota(jnp.int32, (rows, LANE), 1)


def edges_kernel(own_ref, right_ref, low_ref, to_right_ref, to_left_ref):
    rows, cols = own_ref.shape[1:]
    half = rows // 2
    packed = low_ref[0, rows:, :].astype(F32)
    corner = jnp.concatenate([packed[:, k : k + LANE] for k in range(0, cols, LANE)], axis=0)
    corner = jnp.concatenate([pltpu.roll(corner, LANE // 2, 1), corner], axis=0)
    right = right_ref[0].astype(F32)
    to_right_ref[0, :rows] = jnp.where(lanes(rows) < LANE // 2, right, corner).astype(BF16)
    own = own_ref[0, :, cols - LANE :].astype(F32)
    low = low_ref[0, :rows, cols - LANE :].astype(F32)
    to_right_ref[0, rows:] = ((own + low) / (seen(own) + seen(low))).astype(BF16)
    own = own_ref[0, :, :LANE].astype(F32)
    low = pltpu.roll(low_ref[0, :rows, :LANE].astype(F32), LANE // 2, 1)
    to_left_ref[0] = jnp.where(lanes(rows) < LANE // 2, own, low).astype(BF16)


def edges(own, right, low, after):
    n, rows, _ = own.shape
    block = lambda r, c: pl.BlockSpec((1, r, c), lambda i: (i, 0, 0))
    outs = ((2 * rows, LANE), (rows, LANE))
    return pl.pallas_call(
        skipping(edges_kernel, 3, len(after)),
        grid=(n,),
        in_specs=[block(*a.shape[1:]) for a in (own, right, low)] + [ANY] * len(after),
        out_specs=[block(*out) for out in outs],
        out_shape=[jax.ShapeDtypeStruct((n,) + out, BF16) for out in outs],
        compiler_params=params(16),
        cost_estimate=cost(4e10 if own.shape[0] == 1 else 1, 1),
        name="edges",
    )(own, right, low, *after)


SIDE = 63


def join_kernel(
    at, sides_ref, own_ref, low_ref, mine_ref, left_ref, right_ref, exact_ref, out_ref, tail_ref
):
    rows, cols = own_ref.shape[1:]
    own_ref, low_ref, mine_ref, left_ref, right_ref = (
        ref.at[at : at + 1] for ref in (own_ref, low_ref, mine_ref, left_ref, right_ref)
    )
    inside = lanes(rows) < LANE // 2

    def parts(ref):
        pair = ref[0, :rows].astype(F32)
        return jnp.where(inside, pair, 0.0), jnp.where(inside, pltpu.roll(pair, LANE // 2, 1), 0.0)

    own = own_ref[0].astype(F32)
    low = low_ref[0, :rows].astype(F32)
    total = own + low
    count = seen(own) + seen(low)
    a, b = parts(left_ref)
    edge = (total[:, :LANE] + a + b) / (count[:, :LANE] + seen(a) + seen(b))
    rest = total[:, LANE:] / count[:, LANE:]
    exact_ref[0, :, :LANE] = edge
    exact_ref[0, :, LANE:] = rest
    out_ref[0, :rows, :LANE] = edge.astype(BF16)
    out_ref[0, :rows, LANE:cols] = rest.astype(BF16)

    a, b = parts(mine_ref)
    own, low = parts(right_ref)
    count = seen(own) + seen(low) + seen(a) + seen(b)
    strip = (own + low + a + b) / jnp.maximum(count, 1.0)
    strip = jnp.where(sides_ref[3] > 0, strip, 0.0)

    left = left_ref[0, rows:]
    out_ref[0, :rows, cols:] = jnp.where(lanes(rows) < SIDE, strip, left.astype(F32)).astype(BF16)
    extra = out_ref.shape[1] - rows
    pick = lanes(extra) == SIDE - 1
    pick &= lax.broadcasted_iota(jnp.int32, (extra, LANE), 0) == 0
    pick = jnp.where(pick, 1.0, 0.0).astype(BF16)
    column = lax.dot_general(pick, left, (((1,), (1,)), ((), ())), preferred_element_type=F32)
    out_ref[0, rows:, :cols] = column.astype(BF16)
    out_ref[0, rows:, cols:] = jnp.zeros((extra, LANE), BF16)
    tail_ref[0] = out_ref[0, rows - 2 * DEPTH :, :]


def join(sides, own, low, mine, left, right, at, after):
    _, rows, cols = own.shape
    extra = 2 * DEPTH
    sizes = (
        (rows, cols, F32),
        (rows + extra, cols + LANE, BF16),
        (2 * extra, cols + LANE, BF16),
    )
    return pl.pallas_call(
        skipping(functools.partial(join_kernel, at), 6, len(after)),
        in_specs=[pl.BlockSpec(memory_space=pltpu.SMEM)] + [VMEM] * 5 + [ANY] * len(after),
        out_specs=[VMEM] * 3,
        out_shape=[jax.ShapeDtypeStruct((1, r, c), t) for r, c, t in sizes],
        compiler_params=params(12),
        cost_estimate=cost(1, 1),
        name="join",
    )(sides, own, low, mine, left, right, *after)


def bands_kernel(kern_ref, across_ref, within_ref, corner_ref):
    which = pl.program_id(0)
    wide = 3 * 2 * LANE
    shape = (16, wide)
    row = lax.broadcasted_iota(jnp.int32, shape, 0)
    lane = lax.broadcasted_iota(jnp.int32, shape, 1)
    tap = row - (lane - 4 * LANE) - (LANE - REACH)
    base = jnp.zeros(shape, F32)
    for k in range(TAPS):
        base = jnp.where(tap == k, kern_ref[which, 2 * TAPS + k], base)

    for q in range(across_ref.shape[1] // 16):
        turned = pltpu.roll(base, (wide - 4 * LANE + 16 * q) % wide, 1)
        across_ref[0, 16 * q : 16 * (q + 1), :] = turned[:, : 2 * LANE].astype(BF16)

    at, to = 3 * LANE - LANE - (LANE - SIDE) - 1, LANE - (BEFORE - REACH)
    row = lax.broadcasted_iota(jnp.int32, (3 * LANE, LANE), 0)
    lane = lanes(3 * LANE)
    band = across_ref[0, : 3 * LANE, :LANE].astype(F32)
    corner_ref[0, : 3 * LANE] = jnp.where((row == at) & (lane == to), 0.0, band).astype(BF16)
    row = lax.broadcasted_iota(jnp.int32, (LANE, LANE), 0)
    lone = (row == SIDE - 1) & (lanes(LANE) == to)
    corner_ref[0, 3 * LANE :] = jnp.where(lone, kern_ref[which, 2 * TAPS], 0.0).astype(BF16)

    shape = (16, within_ref.shape[2])
    row = lax.broadcasted_iota(jnp.int32, shape, 0)
    lane = lax.broadcasted_iota(jnp.int32, shape, 1)
    tap_y = lane // DEPTH - row // DEPTH
    tap_z = lane % DEPTH - row % DEPTH + REACH
    in_y = jnp.zeros(shape, F32)
    in_z = jnp.zeros(shape, F32)
    for k in range(TAPS):
        in_y = jnp.where(tap_y == k, kern_ref[which, TAPS + k], in_y)
    for k in range(REACH + 1 - DEPTH, REACH + DEPTH):
        in_z = jnp.where(tap_z == k, kern_ref[which, k], in_z)
    both = in_y * in_z

    for q in range(within_ref.shape[1] // 16):
        turned = pltpu.roll(both, 16 * q, 1)
        within_ref[0, 16 * q : 16 * (q + 1), :] = turned.astype(BF16)


def bands(kern, after):
    count = kern.shape[0]
    shapes = (
        (4 * LANE, 2 * LANE),
        (BIG * DEPTH, (BIG + 2 * REACH) * DEPTH),
        (4 * LANE, LANE),
    )
    return pl.pallas_call(
        skipping(bands_kernel, 1, len(after)),
        grid=(count,),
        in_specs=[pl.BlockSpec(memory_space=pltpu.SMEM)] + [ANY] * len(after),
        out_specs=[pl.BlockSpec((1,) + s, lambda i: (i, 0, 0)) for s in shapes],
        out_shape=[jax.ShapeDtypeStruct((count,) + s, BF16) for s in shapes],
        compiler_params=params(32),
        cost_estimate=cost(2e9, 1),
        name="bands",
    )(kern, *after)


@functools.lru_cache(None)
def pyramid_matrices(rows, cols, depth):
    half_x, half_y, half_z = cols // 2, rows // 2, depth // 2
    taps = np.array(GAUSS, np.float32) / 16
    extra_x = (-2, -1, half_x)
    one_x = np.zeros((cols + LANE, half_x + LANE), np.float32)
    for lane in range(half_x + len(extra_x)):
        x = lane if lane < half_x else extra_x[lane - half_x]
        for k in range(5):
            one_x[(2 * x + k - 2) % (cols + LANE), lane] = taps[k]
    extra_y = (-2, -1, half_y)
    order = [(z, y) for z in range(half_z) for y in range(half_y)]
    order += [(z, y) for y in extra_y for z in range(half_z)]
    height = -(-len(order) // 16) * 16
    reach_in = (rows + 10) * depth
    one_zy = np.zeros((height, reach_in), np.float32)
    for i, (z, y) in enumerate(order):
        for a in range(5):
            for b in range(5):
                zi = 2 * z + b - 2
                if 0 <= zi < depth:
                    one_zy[i, (2 * y + a - 2 + 6) * depth + zi] = taps[a] * taps[b]
    two_x = np.zeros((half_x + LANE, half_x // 2), np.float32)
    for x in range(half_x // 2):
        for k in range(5):
            source = 2 * x + k - 2
            lane = source if 0 <= source < half_x else half_x + extra_x.index(source)
            two_x[lane, x] = taps[k]
    place_of = {zy: i for i, zy in enumerate(order)}
    two_zy = np.zeros((half_z * half_y // 4, height), np.float32)
    for z in range(half_z // 2):
        for y in range(half_y // 2):
            for a in range(5):
                for b in range(5):
                    at = (2 * z + b - 2, 2 * y + a - 2)
                    if 0 <= at[0] < half_z:
                        two_zy[z * (half_y // 2) + y, place_of[at]] = taps[a] * taps[b]
    return tuple(m.astype(ml_dtypes.bfloat16) for m in (one_x, one_zy, two_x, two_zy))


def deconvolve_kernel(
    at,
    place_far,
    sides_ref,
    exact_ref,
    message_ref,
    above_ref,
    below_ref,
    far_ref,
    across_ref,
    within_ref,
    corner_ref,
    one_x_ref,
    one_zy_ref,
    two_x_ref,
    two_zy_ref,
    *others,
):
    if len(others) > 11:
        others = others[3:]
    far_ref = far_ref.at[place_far : place_far + 1]
    corner_ref = corner_ref.at[at : at + 1]
    across_ref = across_ref.at[at : at + 1]
    within_ref = within_ref.at[at : at + 1]
    deconvolve_body(
        sides_ref,
        exact_ref,
        message_ref,
        above_ref,
        below_ref,
        far_ref,
        across_ref,
        within_ref,
        corner_ref,
        one_x_ref,
        one_zy_ref,
        two_x_ref,
        two_zy_ref,
        *others,
    )


def deconvolve_body(
    sides_ref,
    exact_ref,
    message_ref,
    above_ref,
    below_ref,
    far_ref,
    across_ref,
    within_ref,
    corner_ref,
    one_x_ref,
    one_zy_ref,
    two_x_ref,
    two_zy_ref,
    restored_ref,
    level_one_ref,
    level_two_ref,
    joined,
    joined_short,
    ratio,
    estimate,
    estimate_short,
    result,
    high,
    low,
):
    rows8, cols = exact_ref.shape[1:]
    wide = cols + LANE
    far8 = far_ref.shape[1] // 2
    frame8 = far8 + 3 * rows8

    pick = jnp.where(lanes(far8) == SIDE - 1, 1.0, 0.0).astype(BF16)

    def unpack(source, count, begin):
        to = slice(begin, begin + count)
        joined_short[to, :wide] = source[0, :count, :]
        column = lax.dot_general(
            source[0, count:, :cols], pick, (((0,), (0,)), ((), ())), preferred_element_type=F32
        )
        joined_short[to, wide:] = column[rows8 - count :].astype(BF16)

    unpack(far_ref, far8, 0)
    unpack(above_ref, rows8, far8)
    unpack(message_ref, rows8, far8 + rows8)
    unpack(below_ref, rows8, far8 + 2 * rows8)
    joined_short[frame8:, :] = jnp.zeros_like(joined_short[frame8:, :])
    joined[...] = joined_short[:, :wide].astype(F32)
    joined[far8 + rows8 : far8 + 2 * rows8, :cols] = exact_ref[0]

    blocks = [slice(k, min(k + 2 * LANE, wide)) for k in range(0, wide, 2 * LANE)]

    def window(ref, here, to, lone):
        begin, end = to.start - LANE, to.stop + LANE
        if begin < 0:
            pieces = [ref[here, begin + wide : wide], ref[here, :end]]
        elif end > wide:
            pieces = [ref[here, begin:wide], ref[here, : end - wide]]
        else:
            return ref[here, begin:end]
        if lone and to.stop == wide:
            pieces.append(ref[here, wide:])
        return jnp.concatenate(pieces, axis=1)

    def correlate(source, which, size, count, exact, finish, lone=False):
        deep = (size + 2 * REACH) * DEPTH
        size8 = size * DEPTH
        matrix = within_ref[0, which, :size8, :deep]
        for i in range(count):
            here = slice(i * size8, (i + 1) * size8)
            for to in blocks:
                if lone and to.stop == wide:
                    to = slice(to.start, wide + LANE)
                out = dot(matrix, source[here.start : here.start + deep, to])
                if i in exact:
                    high[here, to], low[here, to] = split(out)
                else:
                    high[here, to] = out.astype(BF16)
        everything = slice(0, count * size8)
        for to in blocks:
            width = to.stop - to.start
            if lone and to.stop == wide:
                band = corner_ref[0, which]
            else:
                band = across_ref[0, which, : width + 2 * LANE, :width]
            left = window(high, everything, to, lone)
            if not exact:
                finish(0, everything.stop, to, dot(left, band))
                continue
            here = slice(exact[0] * size8, (exact[-1] + 1) * size8)
            out = dot(jnp.concatenate([left, window(low, here, to, False)], axis=0), band)
            if here.start:
                finish(0, here.start, to, out[: here.start])
            finish(here.start, here.stop - here.start, to, out[here] + out[everything.stop :])
            if here.stop < everything.stop:
                finish(here.stop, everything.stop - here.stop, to, out[here.stop : everything.stop])

    def ratio_from(shift):
        def finish(start, size8, to, out):
            top = joined[start + shift * DEPTH : start + shift * DEPTH + size8, to]
            bottom = jnp.maximum(out, TINY)
            inverse = pl.reciprocal(bottom, approx=True)
            inverse = inverse * (2.0 - bottom * inverse)
            ratio[start : start + size8, to] = (top * inverse).astype(BF16)

        return finish

    def first_estimate(start, size8, to, out):
        at = slice(start, start + size8)
        begin = start + 2 * REACH * DEPTH
        value = joined[begin : begin + size8, to] * out
        estimate[at, to] = value
        estimate_short[at, to] = value.astype(BF16)

    def last_estimate(start, size8, to, out):
        begin = start + 2 * REACH * DEPTH
        value = estimate[begin : begin + size8, to] * out
        for b in range((to.stop - to.start) // LANE):
            result[to.start // LANE + b, start : start + size8, :] = value[:, b * LANE : (b + 1) * LANE]

    correlate(joined_short, 0, BIG, 5, (), ratio_from(REACH), True)
    correlate(ratio, 1, BIG, 4, (1, 2), first_estimate)
    correlate(estimate_short, 0, SMALL, 4, (), ratio_from(3 * REACH))
    ratio[4 * SMALL * DEPTH : (4 * SMALL + 4) * DEPTH, :] = jnp.zeros((4 * DEPTH, wide), BF16)
    correlate(ratio, 1, SMALL, 3, (0, 1, 2), last_estimate)

    planes = restored_ref.shape[1]
    height = restored_ref.shape[2]
    for z in range(planes):
        at = pl.ds(6 * planes + z, height, stride=planes)
        for b in range(cols // LANE):
            restored_ref[0, z, :, b * LANE : (b + 1) * LANE] = result[b, at, :]

    def twice(left, right):
        big, small = split(right)
        return dot(left, big) + dot(left, small)

    def twice_left(left, right):
        big, small = split(left)
        return dot(big, right) + dot(small, right)

    reach_in = one_zy_ref.shape[1]
    fine = jnp.concatenate([result[b, :reach_in, :] for b in range(wide // LANE)], axis=1)
    one = twice(one_zy_ref[...], dot(fine.astype(BF16), one_x_ref[...]))
    half_z, half_y, half_x = level_one_ref.shape[1:]
    inner = half_z * half_y
    level_one_ref[0] = one[:inner, :half_x].reshape(half_z, half_y, half_x)
    row = lax.broadcasted_iota(jnp.int32, one.shape, 0) - inner
    lane = lax.broadcasted_iota(jnp.int32, one.shape, 1) - half_x
    up, down, left, right = (sides_ref[k] for k in range(4))
    keep_row = jnp.where(row < 0, 1, jnp.where(row < 2 * half_z, up, down))
    keep_lane = jnp.where(lane < 0, 1, jnp.where(lane < 2, left, right))
    one = jnp.where(keep_row * keep_lane > 0, one, 0.0)
    two = twice(two_zy_ref[...], twice_left(one, two_x_ref[...]))
    level_two_ref[0] = two.reshape(level_two_ref.shape[1:])


def deconvolve(at, place_far, sides, group, tables, matrices, earlier):
    chans = tables[0].shape[0]
    rows8, cols = group[0].shape[1:]
    rows = rows8 // DEPTH
    wide = cols + LANE
    mine = lambda s: pl.BlockSpec((1,) + s[1:], lambda i: (at,) + (0,) * (len(s) - 1))
    outs = (
        (chans, DEPTH, rows, cols),
        (chans, DEPTH // 2, rows // 2, cols // 2),
        (chans, DEPTH // 4, rows // 4, cols // 4),
    )
    shapes = [jax.ShapeDtypeStruct(s, F32) for s in outs]
    ratio_rows = 5 * BIG * DEPTH
    estimate_rows = 4 * BIG * DEPTH
    result_rows = 3 * SMALL * DEPTH
    operands = [sides, *group, *tables, *matrices]
    return pl.pallas_call(
        functools.partial(deconvolve_kernel, at, place_far),
        grid=(1,),
        in_specs=[pl.BlockSpec(memory_space=pltpu.SMEM)]
        + [VMEM] * (len(operands) - 1)
        + [ANY] * len(earlier),
        out_specs=[mine(s) for s in outs],
        out_shape=shapes,
        input_output_aliases={len(operands) + k: k for k in range(len(earlier))},
        scratch_shapes=[
            pltpu.VMEM((FRAME * DEPTH, wide), F32),
            pltpu.VMEM((FRAME * DEPTH, wide + LANE), BF16),
            pltpu.VMEM((ratio_rows, wide), BF16),
            pltpu.VMEM((estimate_rows, wide), F32),
            pltpu.VMEM((estimate_rows, wide), BF16),
            pltpu.VMEM((wide // LANE, result_rows, LANE), F32),
            pltpu.VMEM((ratio_rows, wide + LANE), BF16),
            pltpu.VMEM((ratio_rows, wide), BF16),
        ],
        compiler_params=params(32),
        cost_estimate=cost(1e10, 1),
        name="deconvolve",
    )(*operands, *earlier)


def per_device(tiles, offsets, psf):
    chans, depth, tile_y, tile_x = tiles.shape
    cols = tile_x - MARGIN
    rows = tile_y - MARGIN
    size_x, size_y = lax.axis_size("gx"), lax.axis_size("gy")
    at_x, at_y = lax.axis_index("gx"), lax.axis_index("gy")

    def shift(block, axis, distance):
        devices = range(lax.axis_size(axis))
        route = [(i, i + distance) for i in devices if i + distance in devices]
        return lax.ppermute(block, axis, route)

    sides = jnp.stack([at_y > 0, at_y < size_y - 1, at_x > 0, at_x < size_x - 1])
    sides = sides.astype(jnp.int32)
    matrices = [jnp.asarray(m) for m in pyramid_matrices(rows, cols, depth)]

    at_tile = offsets.reshape(2)
    own, right, low = place(tiles, at_tile, 0, 1, ())
    kern = psf / jnp.sum(psf, axis=-1, keepdims=True)
    both = jnp.stack([kern, kern[:, :, ::-1]], axis=1)
    tables = bands(both.reshape(chans * 2, 3 * TAPS), (right,))
    pieces = [(own, right, shift(low, "gy", 1))]
    own, right, low = place(tiles, at_tile, 1, chans - 1, (tables[1],))
    pieces.append((own, right, shift(low, "gy", 1)))
    tables = [t.reshape((chans, 2) + t.shape[1:]) for t in tables]

    groups = []
    before = (pieces[1][1],)
    earlier = ()
    for own, right, low in pieces:
        mine, to_left = edges(own, right, low, before)
        left = shift(mine, "gx", 1)
        right = shift(to_left, "gx", -1)
        joined = [
            join(sides, own, low, mine, left, right, k, earlier) for k in range(own.shape[0])
        ]
        far = shift(jnp.concatenate([tail for *_, tail in joined], axis=0), "gy", 2)
        for k, (exact, message, _) in enumerate(joined):
            above = shift(message, "gy", 1)
            below = shift(message, "gy", -1)
            groups.append((k, [exact, message, above, below, far]))
        before = (message,)
        earlier = (above, below)

    outs = ()
    for at, (k, group) in enumerate(groups):
        outs = deconvolve(at, k, sides, group, tables, matrices, outs)
    return tuple(outs)


def solution(mesh):
    in_specs = (P(None, None, "gy", "gx"), P("gy", "gx", None), P())
    out_specs = (P(None, None, "gy", "gx"), P(None, None, "gy", "gx"), P(None, None, "gy", "gx"))
    return jax.shard_map(
        per_device, mesh=mesh, in_specs=in_specs, out_specs=out_specs, check_vma=False
    )
```
